32 devices in a mesh: blk: 4 (over x, core), inner: 8 (over z, y).
Axes of the slice: x: 2, y: 2, z: 4, core: 2. Of those that a mesh axis runs over, the one named last changes fastest.
Arguments:
- queries: bfloat16 [8192, 4096], P(('blk', 'inner')), may hold values from -5 to 5
- keys: bfloat16 [8192, 512], P(('blk', 'inner')), may hold values from -5 to 5
- values: bfloat16 [8192, 512], P(('blk', 'inner')), may hold values from -6 to 6
- out_grad: bfloat16 [8192, 4096], P(('blk', 'inner')), may hold values from -6 to 6
- doc_lengths: int32 [16], replicated, may hold values from 1 to 768, 8192 in all
Outputs:
- attended: bfloat16 [8192, 4096], P(('blk', 'inner'))
- query_grad: bfloat16 [8192, 4096], P(('blk', 'inner'))
- key_grad: bfloat16 [8192, 512], P(('blk', 'inner'))
- value_grad: bfloat16 [8192, 512], P(('blk', 'inner'))
The draws below stay inside these ranges and needn't reach their ends.
All inputs are finite; a program needn't handle non-finite values.
Results may differ from the reference program's by a relative error of at most 0.025.
Values may be sent and summed in bfloat16 or wider, within the bound.
No kernel may reach another device: no remote copies, remote signals or barrier semaphores. Data moves between devices by JAX's collectives and lax.ppermute only.
A program may use at most 128 MiB of HBM per device.

```python
import math
import jax
import jax.numpy as jnp
import numpy as np
from jax import lax

HEAD_SIZE = 128
QUERY_HEADS = 32
KEY_VALUE_HEADS = 4
TOK_DEV = 256
SPAN = 4
PACKED_TOKENS = 8192
MAXDOC = 768
DOCS = 16


def draw_queries(key, part):
    query_group_width = QUERY_HEADS // KEY_VALUE_HEADS
    quad_shape = (PACKED_TOKENS, KEY_VALUE_HEADS, query_group_width, HEAD_SIZE)
    random_base_sample = jnp.clip(jax.random.normal(jax.random.fold_in(key, 1), quad_shape, jnp.float32), -4.0, 4.0)
    return random_base_sample.reshape(PACKED_TOKENS, QUERY_HEADS * HEAD_SIZE).astype(jnp.bfloat16)


def draw_keys(key, part):
    triple_shape = (PACKED_TOKENS, KEY_VALUE_HEADS, HEAD_SIZE)
    random_base_sample = jnp.clip(jax.random.normal(jax.random.fold_in(key, 2), triple_shape, jnp.float32), -4.0, 4.0)
    return random_base_sample.reshape(PACKED_TOKENS, KEY_VALUE_HEADS * HEAD_SIZE).astype(jnp.bfloat16)


def shard_levels(stream_key, extent, split, least, high):
    loudness, own = 1.0, jax.random.fold_in(stream_key, 6)
    for axis_at, parts in split:
        draws = jnp.exp(jax.random.uniform(jax.random.fold_in(own, axis_at), (parts,), jnp.float32, least / len(split), high / len(split)))
        loudness = loudness * jnp.repeat(draws, extent[axis_at] // parts).reshape([-1 if axis == axis_at else 1 for axis in range(len(extent))])
    return loudness


def length_profile(count, total, reach, slope):
    weights = [(1 << 20) // math.isqrt(grade ** slope) + 1 for grade in range(2, count + 1)]
    spare, holding = total - reach - (count - 1), [1] * (count - 1)
    while spare > 0:
        candidates = [i for i in range(count - 1) if holding[i] < reach]
        pool, budget = sum([weights[i] for i in candidates]), spare
        for i in candidates:
            extra = min(reach - holding[i], max(1, budget * weights[i] // pool), spare)
            holding[i] = holding[i] + extra
            spare = spare - extra
    return np.array([reach] + holding)


def uneven(own_key, amount, total, most, slope):
    if amount == 2:
        one = jax.random.randint(own_key, (), max(1, total - most), min(most, total - 1) + 1)
        return jnp.stack([one, total - one])
    lengths = jnp.asarray(length_profile(amount, total, most, slope), jnp.int32)
    pairs = (amount - 1) // 2
    giver, sink = lengths[1:1 + 2 * pairs:2], lengths[2:2 + 2 * pairs:2]
    margin = jnp.minimum(giver - 1, most - sink)
    passed = jax.random.randint(jax.random.fold_in(own_key, 1), (pairs,), 0, 1 << 20) % (margin + 1)
    lengths = lengths.at[1:1 + 2 * pairs:2].set(giver - passed).at[2:2 + 2 * pairs:2].set(sink + passed)
    return lengths[jax.random.permutation(jax.random.fold_in(own_key, 2), amount)]


def bell_draw(rng, shape, width, bound, pieces=(), kind=jnp.bfloat16):
    values = jax.random.normal(rng, shape, jnp.float32) * width
    if len(pieces) > 0:
        values = shard_levels(rng, shape, pieces, -0.22, 0.18) * values
    return jnp.clip(values, min=-bound, max=bound).astype(kind)


def setup_inputs(seed: int = 0) -> dict:
    seeds = jax.random.split(jax.random.key(seed), 6)
    return {
        "queries": draw_queries(jax.random.fold_in(seeds[5], 71), 0),
        "keys": draw_keys(jax.random.fold_in(seeds[5], 71), 0),
        "values": bell_draw(seeds[2], (PACKED_TOKENS, KEY_VALUE_HEADS * HEAD_SIZE), 1.0, 6.0, ((0, 32),)),
        "out_grad": bell_draw(seeds[3], (PACKED_TOKENS, QUERY_HEADS * HEAD_SIZE), 1.0, 6.0, ((0, 32),)),
        "doc_lengths": uneven(seeds[4], DOCS, PACKED_TOKENS, MAXDOC, 2).astype(jnp.int32),
    }


def doc_index(positions, doc_lengths):
    doc_ends = jnp.cumsum(doc_lengths).astype(jnp.int32)
    return lax.optimization_barrier(jnp.sum((doc_ends[None, :] <= positions[:, None]).astype(jnp.int32), axis=1)).astype(jnp.int32)

def block_terms(query_block, key_window_slice, value_window_slice, gradient_block, allowed):
    query_row_list = query_block.shape[0]
    sliding_frame = key_window_slice.shape[0]
    query_group_width = QUERY_HEADS // KEY_VALUE_HEADS
    score_scale = 1.0 / math.sqrt(HEAD_SIZE)
    query_quad = query_block.astype(jnp.float32).reshape(query_row_list, KEY_VALUE_HEADS, query_group_width, HEAD_SIZE)
    gradient_quad = gradient_block.astype(jnp.float32).reshape(query_row_list, KEY_VALUE_HEADS, query_group_width, HEAD_SIZE)
    key_triple = key_window_slice.astype(jnp.float32).reshape(sliding_frame, KEY_VALUE_HEADS, HEAD_SIZE)
    value_triple = value_window_slice.astype(jnp.float32).reshape(sliding_frame, KEY_VALUE_HEADS, HEAD_SIZE)
    scores = jnp.einsum('thgd,whd->hgtw', query_quad, key_triple) * score_scale
    scores = jnp.where(allowed[None, None], scores, -jnp.inf)
    row_max = lax.optimization_barrier(jnp.max(scores, axis=-1, keepdims=True))
    exp_scores = jnp.exp(scores - row_max)
    weights = (exp_scores / lax.optimization_barrier(jnp.sum(exp_scores, axis=-1, keepdims=True))).astype(jnp.bfloat16)
    weights_wide = lax.optimization_barrier(weights).astype(jnp.float32)
    attended = jnp.einsum('hgtw,whd->thgd', weights_wide, value_triple).astype(jnp.bfloat16)
    attended_wide = lax.optimization_barrier(attended).astype(jnp.float32)
    row_delta = jnp.einsum('thgd,thgd->hgt', gradient_quad, attended_wide)
    prob_grad = jnp.einsum('thgd,whd->hgtw', gradient_quad, value_triple)
    score_grad = (weights_wide * (prob_grad - row_delta[..., None]) * score_scale).astype(jnp.bfloat16)
    score_wide = lax.optimization_barrier(score_grad).astype(jnp.float32)
    query_factor = jnp.einsum('hgtw,whd->thgd', score_wide, key_triple).astype(jnp.bfloat16)
    key_portion = jnp.einsum('hgtw,thgd->whd', score_wide, query_quad)
    value_portion = jnp.einsum('hgtw,thgd->whd', weights_wide, gradient_quad)
    return (attended, query_factor, key_portion.reshape(sliding_frame, KEY_VALUE_HEADS * HEAD_SIZE), value_portion.reshape(sliding_frame, KEY_VALUE_HEADS * HEAD_SIZE))

def reference(queries, keys, values, out_grad, doc_lengths):
    blocks = PACKED_TOKENS // TOK_DEV
    backward_row_list = (SPAN - 1) * TOK_DEV
    sliding_frame = SPAN * TOK_DEV
    pad_keys = jnp.concatenate([jnp.zeros((backward_row_list, keys.shape[1]), keys.dtype), keys], axis=0)
    pad_values = jnp.concatenate([jnp.zeros((backward_row_list, values.shape[1]), values.dtype), values], axis=0)

    def scan_step(totals, block_index):
        key_total, value_total = totals
        row_start = (block_index * TOK_DEV).astype(jnp.int32)
        query_block = lax.dynamic_slice_in_dim(queries, row_start, TOK_DEV, 0)
        gradient_block = lax.dynamic_slice_in_dim(out_grad, row_start, TOK_DEV, 0)
        key_window_slice = lax.dynamic_slice_in_dim(pad_keys, row_start, sliding_frame, 0)
        value_window_slice = lax.dynamic_slice_in_dim(pad_values, row_start, sliding_frame, 0)
        query_pos = row_start + jnp.arange(TOK_DEV, dtype=jnp.int32)
        key_pos = row_start - backward_row_list + jnp.arange(sliding_frame, dtype=jnp.int32)
        same_doc = doc_index(key_pos, doc_lengths)[None, :] == doc_index(query_pos, doc_lengths)[:, None]
        allowed = (key_pos[None, :] <= query_pos[:, None]) & (key_pos[None, :] >= 0) & same_doc
        attended, query_factor, key_portion, value_portion = block_terms(query_block, key_window_slice, value_window_slice, gradient_block, allowed)
        previous = lax.dynamic_slice_in_dim(key_total, row_start, sliding_frame, 0)
        key_total = lax.dynamic_update_slice_in_dim(key_total, previous + key_portion, row_start, 0)
        previous = lax.dynamic_slice_in_dim(value_total, row_start, sliding_frame, 0)
        value_total = lax.dynamic_update_slice_in_dim(value_total, previous + value_portion, row_start, 0)
        return ((key_total, value_total), (attended.reshape(TOK_DEV, QUERY_HEADS * HEAD_SIZE), query_factor.reshape(TOK_DEV, QUERY_HEADS * HEAD_SIZE)))
    initial_totals = (jnp.zeros((PACKED_TOKENS + backward_row_list, KEY_VALUE_HEADS * HEAD_SIZE), jnp.float32), jnp.zeros((PACKED_TOKENS + backward_row_list, KEY_VALUE_HEADS * HEAD_SIZE), jnp.float32))
    (key_total, value_total), (attended_all, query_all) = lax.scan(scan_step, initial_totals, jnp.arange(blocks, dtype=jnp.int32))
    return (attended_all.reshape(PACKED_TOKENS, QUERY_HEADS * HEAD_SIZE), query_all.reshape(PACKED_TOKENS, QUERY_HEADS * HEAD_SIZE), key_total[backward_row_list:].astype(jnp.bfloat16), value_total[backward_row_list:].astype(jnp.bfloat16))
```

```python
import functools
import math

import jax
import jax.numpy as jnp
from jax import lax
from jax.experimental import pallas as pl
from jax.experimental.pallas import tpu as pltpu
from jax.sharding import PartitionSpec as P

HEAD_SIZE = 128
QUERY_HEADS = 32
KEY_VALUE_HEADS = 4
GROUP = QUERY_HEADS // KEY_VALUE_HEADS
SPAN = 4
AXES = ("blk", "inner")
CHUNK = 2
PAIR = 2
MASKED = -1e30
SCALE = 1.0 / math.sqrt(HEAD_SIZE)
EXP2_SCALE = SCALE * math.log2(math.e)

NN = (((1,), (0,)), ((), ()))
NT = (((1,), (1,)), ((), ()))
TN = (((0,), (0,)), ((), ()))


def dot(a, b, dims):
    return lax.dot_general(a, b, dims, preferred_element_type=jnp.float32)


def passed_along(value, steps):
    count = lax.axis_size("blk") * lax.axis_size("inner")
    first, last = (max(0, -steps), min(count, count - steps))
    return lax.ppermute(value, AXES, [(source, source + steps) for source in range(first, last)])


def write_bias(bias_ref, lengths_ref, first_ref, rows):
    docs = lengths_ref.shape[0]
    first = first_ref[0]
    query_pos = first + lax.broadcasted_iota(jnp.int32, (rows, 128), 0)

    def step(doc, carry):
        end, start = carry
        end = end + lengths_ref[doc]
        return end, jnp.where(query_pos >= end, end, start)

    _, start = lax.fori_loop(
        0, docs, step, (jnp.int32(0), jnp.zeros((rows, 128), jnp.int32))
    )
    lane = lax.broadcasted_iota(jnp.int32, (rows, 128), 1)
    for part in range(SPAN * rows // 128):
        key_pos = first - (SPAN - 1) * rows + part * 128 + lane
        allowed = (key_pos >= start) & (key_pos <= query_pos)
        bias_ref[:, part * 128 : (part + 1) * 128] = jnp.where(allowed, 0.0, MASKED)


def attention_kernel(
    first_ref,
    lengths_ref,
    q_ref,
    g_ref,
    far_ref,
    near_ref,
    own_ref,
    *refs,
):
    out_ref, dq_ref, dfar_ref, dnear_ref, down_ref, bias_ref, dk_ref, dv_ref = refs[-8:]
    rows = q_ref.shape[0]

    @pl.when(pl.program_id(0) == 0)
    def _():
        write_bias(bias_ref, lengths_ref, first_ref, rows)

    blocks = [far_ref.at[1], far_ref.at[0], near_ref, own_ref]

    def keys(j):
        return blocks[j][:, :HEAD_SIZE]

    def values(j):
        return blocks[j][:, HEAD_SIZE:]

    dk_ref[...] = jnp.zeros_like(dk_ref)
    dv_ref[...] = jnp.zeros_like(dv_ref)

    def pair_step(pair, carry):
        qs, gs, ps, ds, gls = [], [], [], [], []
        for sub in range(PAIR):
            cols = pl.ds(pl.multiple_of((pair * PAIR + sub) * HEAD_SIZE, HEAD_SIZE), HEAD_SIZE)
            q = q_ref[:, cols]
            g = g_ref[:, cols]
            s = [
                dot(q, keys(j), NT) * EXP2_SCALE + bias_ref[:, j * rows : (j + 1) * rows]
                for j in range(SPAN)
            ]
            m = jnp.max(functools.reduce(jnp.maximum, s), axis=1, keepdims=True)
            e = [jnp.exp2(x - m) for x in s]
            inv = 1.0 / jnp.sum(functools.reduce(jnp.add, e), axis=1, keepdims=True)
            p = [x.astype(jnp.bfloat16) for x in e]
            mixed = functools.reduce(jnp.add, [dot(p[j], values(j), NN) for j in range(SPAN)])
            out = (mixed * inv).astype(jnp.bfloat16)
            out_ref[:, cols] = out
            wide = g.astype(jnp.float32)
            delta = jnp.sum(wide * out.astype(jnp.float32), axis=1, keepdims=True) * inv
            gl = (wide * inv).astype(jnp.bfloat16)
            d = [
                (p[j].astype(jnp.float32) * (dot(gl, values(j), NT) - delta)).astype(jnp.bfloat16)
                for j in range(SPAN)
            ]
            dq = functools.reduce(jnp.add, [dot(d[j], keys(j), NN) for j in range(SPAN)])
            dq_ref[:, cols] = (dq * SCALE).astype(jnp.bfloat16)
            qs.append(q)
            gls.append(gl)
            ps.append(p)
            ds.append(d)
        for j in range(SPAN):
            span = slice(j * rows, (j + 1) * rows)
            dk_ref[:, span] += functools.reduce(
                jnp.add, [dot(qs[i], ds[i][j], TN) for i in range(PAIR)]
            )
            dv_ref[:, span] += functools.reduce(
                jnp.add, [dot(gls[i], ps[i][j], TN) for i in range(PAIR)]
            )
        return carry

    lax.fori_loop(0, GROUP // PAIR, pair_step, 0)
    targets = [dfar_ref.at[1], dfar_ref.at[0], dnear_ref, down_ref]
    for j in range(SPAN):
        span = slice(j * rows, (j + 1) * rows)
        target = targets[j]
        target[:, :HEAD_SIZE] = (dk_ref[:, span].T * SCALE).astype(target.dtype)
        target[:, HEAD_SIZE:] = dv_ref[:, span].T.astype(target.dtype)


def attention(chunk, first, lengths, queries, out_grad, far, near, own, done):
    rows = queries.shape[0]
    wide = GROUP * HEAD_SIZE
    pair = 2 * HEAD_SIZE
    heads = own.shape[1] // pair
    base = chunk * heads

    def query_block(h, *_):
        return (0, base + h)

    def block(h, *_):
        return (0, h)

    def far_block(h, *_):
        return (0, 0, h)

    in_specs = [
        pl.BlockSpec((rows, wide), query_block),
        pl.BlockSpec((rows, wide), query_block),
        pl.BlockSpec((2, rows, pair), far_block),
        pl.BlockSpec((rows, pair), block),
        pl.BlockSpec((rows, pair), block),
    ]
    operands = [first, lengths, queries, out_grad, far, near, own]
    aliases = {}
    if done is not None:
        in_specs += [pl.BlockSpec(memory_space=pl.ANY)] * 2
        aliases = {len(operands): 0, len(operands) + 1: 1}
        operands += list(done)
    return pl.pallas_call(
        attention_kernel,
        out_shape=(
            jax.ShapeDtypeStruct(queries.shape, jnp.bfloat16),
            jax.ShapeDtypeStruct(queries.shape, jnp.bfloat16),
            jax.ShapeDtypeStruct((2, rows, heads * pair), jnp.bfloat16),
            jax.ShapeDtypeStruct((rows, heads * pair), jnp.float32),
            jax.ShapeDtypeStruct((rows, heads * pair), jnp.float32),
        ),
        grid_spec=pltpu.PrefetchScalarGridSpec(
            num_scalar_prefetch=2,
            grid=(heads,),
            in_specs=in_specs,
            out_specs=(
                pl.BlockSpec((rows, wide), query_block),
                pl.BlockSpec((rows, wide), query_block),
                pl.BlockSpec((2, rows, pair), far_block),
                pl.BlockSpec((rows, pair), block),
                pl.BlockSpec((rows, pair), block),
            ),
            scratch_shapes=[
                pltpu.VMEM((rows, SPAN * rows), jnp.float32),
                pltpu.VMEM((HEAD_SIZE, SPAN * rows), jnp.float32),
                pltpu.VMEM((HEAD_SIZE, SPAN * rows), jnp.float32),
            ],
        ),
        input_output_aliases=aliases,
        compiler_params=pltpu.CompilerParams(vmem_limit_bytes=48 * 1024 * 1024),
        cost_estimate=pl.CostEstimate(
            flops=12 * rows * GROUP * heads * SPAN * rows * HEAD_SIZE * 2,
            bytes_accessed=heads * (4 * rows * wide * 2 + 14 * rows * pair),
            transcendentals=0,
        ),
        name="attention",
    )(*operands)


def local(queries, keys, values, out_grad, doc_lengths):
    rows = queries.shape[0]
    first = (lax.axis_index(AXES) * rows).astype(jnp.int32).reshape(1)
    chunks = KEY_VALUE_HEADS // CHUNK
    owns, nears, fars = [], [], []
    for chunk in range(chunks):
        parts = []
        for head in range(chunk * CHUNK, (chunk + 1) * CHUNK):
            span = slice(head * HEAD_SIZE, (head + 1) * HEAD_SIZE)
            parts += [keys[:, span], values[:, span]]
        owns.append(jnp.concatenate(parts, axis=1))
    for chunk in range(chunks):
        nears.append(passed_along(owns[chunk], 1))
    for chunk in range(chunks):
        fars.append(passed_along(jnp.stack([owns[chunk], nears[chunk]]), 2))
    done, totals = None, []
    for chunk in range(chunks):
        out, dq, dfar, dnear, down = attention(
            chunk, first, doc_lengths, queries, out_grad, fars[chunk], nears[chunk], owns[chunk], done
        )
        done = (out, dq)
        back = passed_along(dfar, -2).astype(jnp.float32)
        last = passed_along((dnear + back[1]).astype(jnp.bfloat16), -1)
        totals.append((down + back[0] + last.astype(jnp.float32)).astype(jnp.bfloat16))
    key_parts, value_parts = [], []
    for total in totals:
        for head in range(CHUNK):
            start = head * 2 * HEAD_SIZE
            key_parts.append(total[:, start : start + HEAD_SIZE])
            value_parts.append(total[:, start + HEAD_SIZE : start + 2 * HEAD_SIZE])
    return (
        done[0],
        done[1],
        jnp.concatenate(key_parts, axis=1),
        jnp.concatenate(value_parts, axis=1),
    )


def solution(mesh):
    spec = P(AXES, None)
    return jax.shard_map(
        local,
        mesh=mesh,
        in_specs=(spec, spec, spec, spec, P()),
        out_specs=(spec, spec, spec, spec),
        check_vma=False,
    )
```

```python
import math

import jax
import jax.numpy as jnp
from jax import lax
from jax.experimental import pallas as pl
from jax.experimental.pallas import tpu as pltpu
from jax.sharding import PartitionSpec as P

HEAD_SIZE = 128
QUERY_HEADS = 32
KEY_VALUE_HEADS = 4
GROUP = QUERY_HEADS // KEY_VALUE_HEADS
SPAN = 4
AXES = ("blk", "inner")
CHUNK = 2
HALF = 128
UNITS = 2
MASKED = -1e30
SCALE = 1.0 / math.sqrt(HEAD_SIZE)
EXP2_SCALE = SCALE * math.log2(math.e)

NN = (((1,), (0,)), ((), ()))
NT = (((1,), (1,)), ((), ()))


def dot(a, b, dims=NN):
    return lax.dot_general(a, b, dims, preferred_element_type=jnp.float32)


def device_count():
    return lax.axis_size("blk") * lax.axis_size("inner")


def passed_along(value, steps):
    count = device_count()
    first, last = (max(0, -steps), min(count, count - steps))
    return lax.ppermute(value, AXES, [(source, source + steps) for source in range(first, last)])


def swapped(value):
    return lax.ppermute(value, AXES, [(source, source ^ 1) for source in range(device_count())])


def write_bias(bias_ref, lengths_ref, first_ref, rows, width):
    docs = lengths_ref.shape[0]
    for half in range(rows // HALF):
        first = first_ref[0] + half * HALF
        query_pos = first + lax.broadcasted_iota(jnp.int32, (8, HALF), 1)

        def step(doc, carry, query_pos=query_pos):
            end, start = carry
            end = end + lengths_ref[doc]
            return end, jnp.where(query_pos >= end, end, start)

        _, start = lax.fori_loop(0, docs, step, (jnp.int32(0), jnp.zeros((8, HALF), jnp.int32)))
        start = jnp.broadcast_to(start[:1], (width, HALF))
        query_pos = jnp.broadcast_to(query_pos[:1], (width, HALF))
        key_pos = first + HALF - width + lax.broadcasted_iota(jnp.int32, (width, HALF), 0)
        allowed = (key_pos >= start) & (key_pos <= query_pos)
        bias_ref[half] = jnp.where(allowed, 0.0, MASKED)


def attention_kernel(first_ref, lengths_ref, q_ref, g_ref, far_ref, mid_ref, near_ref, own_ref, *refs):
    (
        out_ref, dq_ref, dfar_ref, dmid_ref, dnear_ref, down_ref,
        bias_ref, key_ref, value_ref, key_t_ref, value_t_ref, p_ref, d_ref, dk_ref, dv_ref,
    ) = refs[-15:]
    rows = q_ref.shape[0]
    window = SPAN * rows
    width = window - HALF
    write_bias(bias_ref, lengths_ref, first_ref, rows, width)
    for j, block in enumerate((far_ref, mid_ref, near_ref, own_ref)):
        span = slice(j * rows, (j + 1) * rows)
        key_ref[span] = block[:, :HEAD_SIZE]
        value_ref[span] = block[:, HEAD_SIZE:]
        key_t_ref[:, span] = block[:, :HEAD_SIZE].T
        value_t_ref[:, span] = block[:, HEAD_SIZE:].T
    dk_ref[...] = jnp.zeros_like(dk_ref)
    dv_ref[...] = jnp.zeros_like(dv_ref)
    steps = GROUP // (2 * UNITS)

    def step(index, carry):
        half = index // steps
        start = pl.multiple_of(half * HALF, HALF)
        base = (index % steps) * 2 * UNITS
        queries = pl.ds(start, HALF)
        span = pl.ds(start, width)
        key, value = key_ref[span], value_ref[span]
        key_t, value_t = key_t_ref[:, span], value_t_ref[:, span]
        bias = bias_ref[half]
        bias = jnp.concatenate([bias, bias], axis=1)
        qs, gs = [], []
        for unit in range(UNITS):
            cols = [
                pl.ds(pl.multiple_of((base + 2 * unit + i) * HEAD_SIZE, HEAD_SIZE), HEAD_SIZE)
                for i in range(2)
            ]
            here = slice(unit * 2 * HALF, (unit + 1) * 2 * HALF)
            q = jnp.concatenate([q_ref[queries, c] for c in cols], axis=0)
            g_t = jnp.concatenate([g_ref[queries, c] for c in cols], axis=0).T.astype(jnp.float32)
            s = dot(key, q, NT) * EXP2_SCALE + bias
            e = jnp.exp2(s - jnp.max(s, axis=0, keepdims=True))
            inv = 1.0 / jnp.sum(e, axis=0, keepdims=True)
            p = e.astype(jnp.bfloat16)
            p_ref[:, here] = p
            out_t = (dot(value_t, p) * inv).astype(jnp.bfloat16)
            out = out_t.T
            for i in range(2):
                out_ref[queries, cols[i]] = out[i * HALF : (i + 1) * HALF]
            delta = jnp.sum(g_t * out_t.astype(jnp.float32), axis=0, keepdims=True) * inv
            g_t = (g_t * inv).astype(jnp.bfloat16)
            d = (p.astype(jnp.float32) * (dot(value, g_t) - delta)).astype(jnp.bfloat16)
            d_ref[:, here] = d
            dq = (dot(key_t, d) * SCALE).astype(jnp.bfloat16).T
            for i in range(2):
                dq_ref[queries, cols[i]] = dq[i * HALF : (i + 1) * HALF]
            qs.append(q)
            gs.append(g_t.T)
        dk_ref[span] += dot(d_ref[...], jnp.concatenate(qs, axis=0))
        dv_ref[span] += dot(p_ref[...], jnp.concatenate(gs, axis=0))
        return carry

    lax.fori_loop(0, (rows // HALF) * steps, step, 0)
    for j, target in enumerate((dfar_ref, dmid_ref, dnear_ref, down_ref)):
        span = slice(j * rows, (j + 1) * rows)
        target[:, :HEAD_SIZE] = (dk_ref[span] * SCALE).astype(target.dtype)
        target[:, HEAD_SIZE:] = dv_ref[span].astype(target.dtype)


def attention(head, first, lengths, queries, out_grad, blocks, grads, parts):
    rows = queries.shape[0]
    wide = GROUP * HEAD_SIZE
    pair = 2 * HEAD_SIZE
    window = SPAN * rows
    width = window - HALF
    place = head % CHUNK
    query_spec = pl.BlockSpec((rows, wide), lambda i, *_: (0, head))
    block_spec = pl.BlockSpec((rows, pair), lambda i, *_: (0, place))
    operands = [first, lengths, queries, out_grad, *blocks]
    in_specs = [query_spec] * 2 + [block_spec] * 4
    aliases = {}
    for at, array in enumerate((*grads, *parts)):
        if array is not None:
            aliases[len(operands)] = at
            operands.append(array)
            in_specs.append(pl.BlockSpec(memory_space=pl.ANY))
    bf16, f32 = jnp.bfloat16, jnp.float32
    results = pl.pallas_call(
        attention_kernel,
        out_shape=[jax.ShapeDtypeStruct(queries.shape, bf16)] * 2
        + [jax.ShapeDtypeStruct((rows, CHUNK * pair), kind) for kind in (bf16, f32, f32, f32)],
        grid_spec=pltpu.PrefetchScalarGridSpec(
            num_scalar_prefetch=2,
            grid=(1,),
            in_specs=in_specs,
            out_specs=[query_spec] * 2 + [block_spec] * 4,
            scratch_shapes=[
                pltpu.VMEM((rows // HALF, width, HALF), f32),
                pltpu.VMEM((window, HEAD_SIZE), bf16),
                pltpu.VMEM((window, HEAD_SIZE), bf16),
                pltpu.VMEM((HEAD_SIZE, window), bf16),
                pltpu.VMEM((HEAD_SIZE, window), bf16),
                pltpu.VMEM((width, UNITS * 2 * HALF), bf16),
                pltpu.VMEM((width, UNITS * 2 * HALF), bf16),
                pltpu.VMEM((window, HEAD_SIZE), f32),
                pltpu.VMEM((window, HEAD_SIZE), f32),
            ],
        ),
        input_output_aliases=aliases,
        compiler_params=pltpu.CompilerParams(vmem_limit_bytes=48 * 1024 * 1024),
        cost_estimate=pl.CostEstimate(
            flops=12 * rows * GROUP * window * HEAD_SIZE * 2,
            bytes_accessed=4 * rows * wide * 2 + 22 * rows * pair,
            transcendentals=0,
        ),
        name="attention",
    )(*operands)
    return results[:2], results[2:]


def local(queries, keys, values, out_grad, doc_lengths):
    rows = queries.shape[0]
    index = lax.axis_index(AXES)
    odd = index % 2 == 1
    first = (index * rows).astype(jnp.int32).reshape(1)
    bf16, f32 = jnp.bfloat16, jnp.float32
    chunks = range(KEY_VALUE_HEADS // CHUNK)
    owns, mids, nears, fars = [], [], [], []
    for chunk in chunks:
        parts = []
        for head in range(chunk * CHUNK, (chunk + 1) * CHUNK):
            span = slice(head * HEAD_SIZE, (head + 1) * HEAD_SIZE)
            parts += [keys[:, span], values[:, span]]
        owns.append(jnp.concatenate(parts, axis=1))
        mids.append(passed_along(owns[chunk], 2))
        nears.append(swapped(jnp.where(odd, mids[chunk], owns[chunk])))
        fars.append(passed_along(nears[chunk], 2))
    grads = (None, None)
    totals = []
    for chunk in chunks:
        parts = (None,) * 4
        for head in range(chunk * CHUNK, (chunk + 1) * CHUNK):
            blocks = (fars[chunk], mids[chunk], nears[chunk], owns[chunk])
            grads, parts = attention(head, first, doc_lengths, queries, out_grad, blocks, grads, parts)
        far, mid, near, own = parts
        near = (near + passed_along(far, -2).astype(f32)).astype(bf16)
        got = swapped(near).astype(f32)
        mid = (mid + jnp.where(odd, got, 0.0)).astype(bf16)
        own = own + jnp.where(odd, 0.0, got)
        totals.append((own + passed_along(mid, -2).astype(f32)).astype(bf16))
    key_parts, value_parts = [], []
    for total in totals:
        for head in range(CHUNK):
            start = head * 2 * HEAD_SIZE
            key_parts.append(total[:, start : start + HEAD_SIZE])
            value_parts.append(total[:, start + HEAD_SIZE : start + 2 * HEAD_SIZE])
    return (
        grads[0],
        grads[1],
        jnp.concatenate(key_parts, axis=1),
        jnp.concatenate(value_parts, axis=1),
    )


def solution(mesh):
    spec = P(AXES, None)
    return jax.shard_map(
        local,
        mesh=mesh,
        in_specs=(spec, spec, spec, spec, P()),
        out_specs=(spec, spec, spec, spec),
        check_vma=False,
    )
```

```python
import math

import jax
import jax.numpy as jnp
from jax import lax
from jax.experimental import pallas as pl
from jax.experimental.pallas import tpu as pltpu
from jax.sharding import PartitionSpec as P

HEAD_SIZE = 128
QUERY_HEADS = 32
KEY_VALUE_HEADS = 4
GROUP = QUERY_HEADS // KEY_VALUE_HEADS
SPAN = 4
AXES = ("blk", "inner")
CHUNK = 2
UNITS = 2
MASKED = -1e30
SCALE = 1.0 / math.sqrt(HEAD_SIZE)
EXP2_SCALE = SCALE * math.log2(math.e)

NN = (((1,), (0,)), ((), ()))


def dot(a, b, dims=NN):
    return lax.dot_general(a, b, dims, preferred_element_type=jnp.float32)


def device_count():
    return lax.axis_size("blk") * lax.axis_size("inner")


def passed_along(value, steps):
    count = device_count()
    first, last = (max(0, -steps), min(count, count - steps))
    return lax.ppermute(value, AXES, [(source, source + steps) for source in range(first, last)])


def swapped(value):
    return lax.ppermute(value, AXES, [(source, source ^ 1) for source in range(device_count())])


def write_bias(bias_ref, lengths_ref, first_ref, rows):
    docs = lengths_ref.shape[0]
    first = first_ref[0]
    query_pos = first + lax.broadcasted_iota(jnp.int32, (rows, 128), 0)

    def step(doc, carry):
        end, start = carry
        end = end + lengths_ref[doc]
        return end, jnp.where(query_pos >= end, end, start)

    _, start = lax.fori_loop(0, docs, step, (jnp.int32(0), jnp.zeros((rows, 128), jnp.int32)))
    lane = lax.broadcasted_iota(jnp.int32, (rows, 128), 1)
    for part in range(SPAN * rows // 128):
        key_pos = first - (SPAN - 1) * rows + part * 128 + lane
        allowed = (key_pos >= start) & (key_pos <= query_pos)
        bias_ref[:, part * 128 : (part + 1) * 128] = jnp.where(allowed, 0.0, MASKED)


def attention_kernel(first_ref, lengths_ref, q_ref, g_ref, far_ref, mid_ref, near_ref, own_ref, *refs):
    (
        out_ref, dq_ref, dfar_ref, dmid_ref, dnear_ref, down_ref,
        bias_ref, key_ref, value_ref, key_t_ref, value_t_ref, p_ref, d_ref, dk_ref, dv_ref,
    ) = refs[-15:]
    rows = q_ref.shape[0]

    @pl.when(pl.program_id(0) == 0)
    def _():
        write_bias(bias_ref, lengths_ref, first_ref, rows)
        value_ref[:, HEAD_SIZE:] = jnp.ones((SPAN * rows, HEAD_SIZE), jnp.bfloat16)

    for j, block in enumerate((far_ref, mid_ref, near_ref, own_ref)):
        span = slice(j * rows, (j + 1) * rows)
        key_ref[span] = block[:, :HEAD_SIZE]
        value_ref[span, :HEAD_SIZE] = block[:, HEAD_SIZE:]
        key_t_ref[:, span] = block[:, :HEAD_SIZE].T
        value_t_ref[:, span] = block[:, HEAD_SIZE:].T
    dk_ref[...] = jnp.zeros_like(dk_ref)
    dv_ref[...] = jnp.zeros_like(dv_ref)

    def step(index, carry):
        qs, gs = [], []
        for unit in range(UNITS):
            cols = pl.ds(pl.multiple_of((index * UNITS + unit) * HEAD_SIZE, HEAD_SIZE), HEAD_SIZE)
            here = slice(unit * rows, (unit + 1) * rows)
            q = q_ref[:, cols]
            g = g_ref[:, cols].astype(jnp.float32)
            s = dot(q, key_t_ref[...]) * EXP2_SCALE + bias_ref[...]
            p = jnp.exp2(s - jnp.max(s, axis=1, keepdims=True)).astype(jnp.bfloat16)
            p_ref[here] = p
            mixed = dot(p, value_ref[...])
            inv = 1.0 / mixed[:, HEAD_SIZE:]
            out = (mixed[:, :HEAD_SIZE] * inv).astype(jnp.bfloat16)
            out_ref[:, cols] = out
            g = g * inv
            delta = jnp.sum(g * out.astype(jnp.float32), axis=1, keepdims=True)
            g = g.astype(jnp.bfloat16)
            d = (p.astype(jnp.float32) * (dot(g, value_t_ref[...]) - delta)).astype(jnp.bfloat16)
            d_ref[here] = d
            dq_ref[:, cols] = (dot(d, key_ref[...]) * SCALE).astype(jnp.bfloat16)
            qs.append(q.T)
            gs.append(g.T)
        dk_ref[...] += dot(jnp.concatenate(qs, axis=1), d_ref[...])
        dv_ref[...] += dot(jnp.concatenate(gs, axis=1), p_ref[...])
        return carry

    lax.fori_loop(0, GROUP // UNITS, step, 0)
    for j, target in enumerate((dfar_ref, dmid_ref, dnear_ref, down_ref)):
        span = slice(j * rows, (j + 1) * rows)
        target[:, :HEAD_SIZE] = (dk_ref[:, span].T * SCALE).astype(target.dtype)
        target[:, HEAD_SIZE:] = dv_ref[:, span].T.astype(target.dtype)


def attention(chunk, first, lengths, queries, out_grad, blocks, grads):
    rows = queries.shape[0]
    wide = GROUP * HEAD_SIZE
    pair = 2 * HEAD_SIZE
    window = SPAN * rows
    query_spec = pl.BlockSpec((rows, wide), lambda i, *_: (0, chunk * CHUNK + i))
    block_spec = pl.BlockSpec((rows, pair), lambda i, *_: (0, i))
    operands = [first, lengths, queries, out_grad, *blocks]
    in_specs = [query_spec] * 2 + [block_spec] * 4
    aliases = {}
    for at, array in enumerate(grads):
        if array is not None:
            aliases[len(operands)] = at
            operands.append(array)
            in_specs.append(pl.BlockSpec(memory_space=pl.ANY))
    bf16, f32 = jnp.bfloat16, jnp.float32
    results = pl.pallas_call(
        attention_kernel,
        out_shape=[jax.ShapeDtypeStruct(queries.shape, bf16)] * 2
        + [jax.ShapeDtypeStruct((rows, CHUNK * pair), kind) for kind in (bf16, f32, f32, f32)],
        grid_spec=pltpu.PrefetchScalarGridSpec(
            num_scalar_prefetch=2,
            grid=(CHUNK,),
            in_specs=in_specs,
            out_specs=[query_spec] * 2 + [block_spec] * 4,
            scratch_shapes=[
                pltpu.VMEM((rows, window), f32),
                pltpu.VMEM((window, HEAD_SIZE), bf16),
                pltpu.VMEM((window, 2 * HEAD_SIZE), bf16),
                pltpu.VMEM((HEAD_SIZE, window), bf16),
                pltpu.VMEM((HEAD_SIZE, window), bf16),
                pltpu.VMEM((UNITS * rows, window), bf16),
                pltpu.VMEM((UNITS * rows, window), bf16),
                pltpu.VMEM((HEAD_SIZE, window), f32),
                pltpu.VMEM((HEAD_SIZE, window), f32),
            ],
        ),
        input_output_aliases=aliases,
        compiler_params=pltpu.CompilerParams(vmem_limit_bytes=48 * 1024 * 1024),
        cost_estimate=pl.CostEstimate(
            flops=12 * CHUNK * rows * GROUP * window * HEAD_SIZE * 2,
            bytes_accessed=CHUNK * (4 * rows * wide * 2 + 22 * rows * pair),
            transcendentals=0,
        ),
        name="attention",
    )(*operands)
    return results[:2], results[2:]


def local(queries, keys, values, out_grad, doc_lengths):
    rows = queries.shape[0]
    index = lax.axis_index(AXES)
    odd = index % 2 == 1
    first = (index * rows).astype(jnp.int32).reshape(1)
    bf16, f32 = jnp.bfloat16, jnp.float32
    chunks = range(KEY_VALUE_HEADS // CHUNK)
    owns, mids, nears, fars = [], [], [], []
    for chunk in chunks:
        parts = []
        for head in range(chunk * CHUNK, (chunk + 1) * CHUNK):
            span = slice(head * HEAD_SIZE, (head + 1) * HEAD_SIZE)
            parts += [keys[:, span], values[:, span]]
        owns.append(jnp.concatenate(parts, axis=1))
        mids.append(passed_along(owns[chunk], 2))
        nears.append(swapped(jnp.where(odd, mids[chunk], owns[chunk])))
        fars.append(passed_along(nears[chunk], 2))
    grads = (None, None)
    totals = []
    for chunk in chunks:
        blocks = (fars[chunk], mids[chunk], nears[chunk], owns[chunk])
        grads, parts = attention(chunk, first, doc_lengths, queries, out_grad, blocks, grads)
        far, mid, near, own = parts
        near = (near + passed_along(far, -2).astype(f32)).astype(bf16)
        got = swapped(near).astype(f32)
        mid = (mid + jnp.where(odd, got, 0.0)).astype(bf16)
        own = own + jnp.where(odd, 0.0, got)
        totals.append((own + passed_along(mid, -2).astype(f32)).astype(bf16))
    key_parts, value_parts = [], []
    for total in totals:
        for head in range(CHUNK):
            start = head * 2 * HEAD_SIZE
            key_parts.append(total[:, start : start + HEAD_SIZE])
            value_parts.append(total[:, start + HEAD_SIZE : start + 2 * HEAD_SIZE])
    return (
        grads[0],
        grads[1],
        jnp.concatenate(key_parts, axis=1),
        jnp.concatenate(value_parts, axis=1),
    )


def solution(mesh):
    spec = P(AXES, None)
    return jax.shard_map(
        local,
        mesh=mesh,
        in_specs=(spec, spec, spec, spec, P()),
        out_specs=(spec, spec, spec, spec),
        check_vma=False,
    )
```

```python
import math

import jax
import jax.numpy as jnp
from jax import lax
from jax.experimental import pallas as pl
from jax.experimental.pallas import tpu as pltpu
from jax.sharding import PartitionSpec as P

HEAD_SIZE = 128
QUERY_HEADS = 32
KEY_VALUE_HEADS = 4
GROUP = QUERY_HEADS // KEY_VALUE_HEADS
SPAN = 4
AXES = ("blk", "inner")
CHUNK = 2
ROWS = 32
MASKED = -1e30
SCALE = 1.0 / math.sqrt(HEAD_SIZE)
EXP2_SCALE = SCALE * math.log2(math.e)

NN = (((1,), (0,)), ((), ()))


def dot(a, b, dims=NN):
    return lax.dot_general(a, b, dims, preferred_element_type=jnp.float32)


def device_count():
    return lax.axis_size("blk") * lax.axis_size("inner")


def passed_along(value, steps):
    count = device_count()
    first, last = (max(0, -steps), min(count, count - steps))
    return lax.ppermute(value, AXES, [(source, source + steps) for source in range(first, last)])


def swapped(value):
    return lax.ppermute(value, AXES, [(source, source ^ 1) for source in range(device_count())])


def write_bias(bias_ref, lengths_ref, first_ref, rows):
    docs = lengths_ref.shape[0]
    first = first_ref[0]
    query_pos = first + lax.broadcasted_iota(jnp.int32, (rows, 128), 0)

    def step(doc, carry):
        end, start = carry
        end = end + lengths_ref[doc]
        return end, jnp.where(query_pos >= end, end, start)

    _, start = lax.fori_loop(0, docs, step, (jnp.int32(0), jnp.zeros((rows, 128), jnp.int32)))
    lane = lax.broadcasted_iota(jnp.int32, (rows, 128), 1)
    for part in range(SPAN * rows // 128):
        key_pos = first - (SPAN - 1) * rows + part * 128 + lane
        allowed = (key_pos >= start) & (key_pos <= query_pos)
        bias_ref[:, part * 128 : (part + 1) * 128] = jnp.where(allowed, 0.0, MASKED)


def attention_kernel(first_ref, lengths_ref, q_ref, g_ref, far_ref, mid_ref, near_ref, own_ref, *refs):
    (
        out_ref, dq_ref, dfar_ref, dmid_ref, dnear_ref, down_ref,
        bias_ref, key_ref, value_ref, key_t_ref, value_t_ref, dk_ref, dv_ref, inv_ref, *slots,
    ) = refs[-26:]
    s_refs, p_refs, dp_refs, d_refs, g_refs, delta_refs = (slots[i : i + 2] for i in range(0, 12, 2))
    rows = q_ref.shape[0]
    window = SPAN * rows

    @pl.when(pl.program_id(0) == 0)
    def _():
        write_bias(bias_ref, lengths_ref, first_ref, rows)
        for ref in (*p_refs, *d_refs):
            ref[...] = jnp.zeros_like(ref)

    for j, block in enumerate((far_ref, mid_ref, near_ref, own_ref)):
        span = slice(j * rows, (j + 1) * rows)
        key_ref[span] = block[:, :HEAD_SIZE]
        value_ref[span] = block[:, HEAD_SIZE:]
        key_t_ref[:, span] = block[:, :HEAD_SIZE].T
        value_t_ref[:, span] = block[:, HEAD_SIZE:].T
    dk_ref[...] = jnp.zeros_like(dk_ref)
    dv_ref[...] = jnp.zeros_like(dv_ref)
    p_refs[1][...] = jnp.zeros_like(p_refs[1])
    dp_refs[1][...] = jnp.zeros_like(dp_refs[1])
    g_refs[1][...] = jnp.zeros_like(g_refs[1])
    delta_refs[1][...] = jnp.zeros_like(delta_refs[1])

    chunks = [
        (slice(r, r + ROWS), slice((r + 1) // 128 * 128, -(-(window - rows + r + ROWS) // 128) * 128))
        for r in range(0, rows, ROWS)
    ]

    def columns(head):
        return pl.ds(pl.multiple_of(head * HEAD_SIZE, HEAD_SIZE), HEAD_SIZE)

    def scores(head, slot):
        s_refs[slot][...] = dot(q_ref[:, columns(head)], key_t_ref[...])

    def softmax(slot):
        for here, keys in chunks:
            s = s_refs[slot][here, keys] * EXP2_SCALE + bias_ref[here, keys]
            e = jnp.exp2(s - jnp.max(s, axis=1, keepdims=True))
            inv = 1.0 / jnp.sum(e, axis=1, keepdims=True)
            inv_ref[here] = jnp.broadcast_to(inv, (ROWS, HEAD_SIZE))
            p_refs[slot][here, keys] = e.astype(jnp.bfloat16)

    def mix(head, slot):
        cols = columns(head)
        mixed = dot(p_refs[slot][...], value_ref[...])
        inv = inv_ref[...]
        out = (mixed * inv).astype(jnp.bfloat16)
        out_ref[:, cols] = out
        g = g_ref[:, cols].astype(jnp.float32) * inv
        delta = jnp.sum(g * out.astype(jnp.float32), axis=1, keepdims=True)
        delta_refs[slot][...] = jnp.broadcast_to(delta, (rows, HEAD_SIZE))
        g_refs[slot][...] = g.astype(jnp.bfloat16)
        dp_refs[slot][...] = dot(g_refs[slot][...], value_t_ref[...])

    def score_grad(slot):
        for here, keys in chunks:
            repeat = (keys.stop - keys.start) // HEAD_SIZE
            delta = jnp.concatenate([delta_refs[slot][here]] * repeat, axis=1)
            p = p_refs[slot][here, keys].astype(jnp.float32)
            d_refs[slot][here, keys] = (p * (dp_refs[slot][here, keys] - delta)).astype(jnp.bfloat16)

    def spread(head, slot):
        cols = columns(head)
        dq_ref[:, cols] = (dot(d_refs[slot][...], key_ref[...]) * SCALE).astype(jnp.bfloat16)
        dk_ref[...] += dot(q_ref[:, cols].T, d_refs[slot][...])
        dv_ref[...] += dot(g_refs[slot][...].T, p_refs[slot][...])

    scores(0, 0)

    def step(index, carry):
        for slot in range(2):
            head = 2 * index + slot
            before = jnp.maximum(head - 1, 0)
            scores(jnp.minimum(head + 1, GROUP - 1), 1 - slot)
            score_grad(1 - slot)
            softmax(slot)
            spread(before, 1 - slot)
            mix(head, slot)
        return carry

    lax.fori_loop(0, GROUP // 2, step, 0)
    score_grad(1)
    spread(GROUP - 1, 1)
    for j, target in enumerate((dfar_ref, dmid_ref, dnear_ref, down_ref)):
        span = slice(j * rows, (j + 1) * rows)
        target[:, :HEAD_SIZE] = (dk_ref[:, span].T * SCALE).astype(target.dtype)
        target[:, HEAD_SIZE:] = dv_ref[:, span].T.astype(target.dtype)


def attention(chunk, first, lengths, queries, out_grad, blocks, grads):
    rows = queries.shape[0]
    wide = GROUP * HEAD_SIZE
    pair = 2 * HEAD_SIZE
    window = SPAN * rows
    query_spec = pl.BlockSpec((rows, wide), lambda i, *_: (0, chunk * CHUNK + i))
    block_spec = pl.BlockSpec((rows, pair), lambda i, *_: (0, i))
    operands = [first, lengths, queries, out_grad, *blocks]
    in_specs = [query_spec] * 2 + [block_spec] * 4
    aliases = {}
    for at, array in enumerate(grads):
        if array is not None:
            aliases[len(operands)] = at
            operands.append(array)
            in_specs.append(pl.BlockSpec(memory_space=pl.ANY))
    bf16, f32 = jnp.bfloat16, jnp.float32
    results = pl.pallas_call(
        attention_kernel,
        out_shape=[jax.ShapeDtypeStruct(queries.shape, bf16)] * 2
        + [jax.ShapeDtypeStruct((rows, CHUNK * pair), kind) for kind in (bf16, f32, f32, f32)],
        grid_spec=pltpu.PrefetchScalarGridSpec(
            num_scalar_prefetch=2,
            grid=(CHUNK,),
            in_specs=in_specs,
            out_specs=[query_spec] * 2 + [block_spec] * 4,
            scratch_shapes=[
                pltpu.VMEM((rows, window), f32),
                pltpu.VMEM((window, HEAD_SIZE), bf16),
                pltpu.VMEM((window, HEAD_SIZE), bf16),
                pltpu.VMEM((HEAD_SIZE, window), bf16),
                pltpu.VMEM((HEAD_SIZE, window), bf16),
                pltpu.VMEM((HEAD_SIZE, window), f32),
                pltpu.VMEM((HEAD_SIZE, window), f32),
                pltpu.VMEM((rows, HEAD_SIZE), f32),
            ]
            + [
                pltpu.VMEM((rows, columns), kind)
                for columns, kind in (
                    (window, f32),
                    (window, bf16),
                    (window, f32),
                    (window, bf16),
                    (HEAD_SIZE, bf16),
                    (HEAD_SIZE, f32),
                )
                for _ in range(2)
            ],
        ),
        input_output_aliases=aliases,
        compiler_params=pltpu.CompilerParams(vmem_limit_bytes=48 * 1024 * 1024),
        cost_estimate=pl.CostEstimate(
            flops=12 * CHUNK * rows * GROUP * window * HEAD_SIZE * 2,
            bytes_accessed=CHUNK * (4 * rows * wide * 2 + 22 * rows * pair),
            transcendentals=0,
        ),
        name="attention",
    )(*operands)
    return results[:2], results[2:]


def local(queries, keys, values, out_grad, doc_lengths):
    rows = queries.shape[0]
    index = lax.axis_index(AXES)
    odd = index % 2 == 1
    first = (index * rows).astype(jnp.int32).reshape(1)
    bf16, f32 = jnp.bfloat16, jnp.float32
    chunks = range(KEY_VALUE_HEADS // CHUNK)
    owns, mids, nears, fars = [], [], [], []
    for chunk in chunks:
        parts = []
        for head in range(chunk * CHUNK, (chunk + 1) * CHUNK):
            span = slice(head * HEAD_SIZE, (head + 1) * HEAD_SIZE)
            parts += [keys[:, span], values[:, span]]
        owns.append(jnp.concatenate(parts, axis=1))
        mids.append(passed_along(owns[chunk], 2))
        nears.append(swapped(jnp.where(odd, mids[chunk], owns[chunk])))
        fars.append(passed_along(nears[chunk], 2))
    grads = (None, None)
    totals = []
    for chunk in chunks:
        blocks = (fars[chunk], mids[chunk], nears[chunk], owns[chunk])
        grads, parts = attention(chunk, first, doc_lengths, queries, out_grad, blocks, grads)
        far, mid, near, own = parts
        near = (near + passed_along(far, -2).astype(f32)).astype(bf16)
        got = swapped(near).astype(f32)
        mid = (mid + jnp.where(odd, got, 0.0)).astype(bf16)
        own = own + jnp.where(odd, 0.0, got)
        totals.append((own + passed_along(mid, -2).astype(f32)).astype(bf16))
    key_parts, value_parts = [], []
    for total in totals:
        for head in range(CHUNK):
            start = head * 2 * HEAD_SIZE
            key_parts.append(total[:, start : start + HEAD_SIZE])
            value_parts.append(total[:, start + HEAD_SIZE : start + 2 * HEAD_SIZE])
    return (
        grads[0],
        grads[1],
        jnp.concatenate(key_parts, axis=1),
        jnp.concatenate(value_parts, axis=1),
    )


def solution(mesh):
    spec = P(AXES, None)
    return jax.shard_map(
        local,
        mesh=mesh,
        in_specs=(spec, spec, spec, spec, P()),
        out_specs=(spec, spec, spec, spec),
        check_vma=False,
    )
```

```python
import functools
import math

import jax
import jax.numpy as jnp
from jax import lax
from jax.experimental import pallas as pl
from jax.experimental.pallas import tpu as pltpu
from jax.sharding import PartitionSpec as P

HEAD_SIZE = 128
QUERY_HEADS = 32
KEY_VALUE_HEADS = 4
GROUP = QUERY_HEADS // KEY_VALUE_HEADS
SPAN = 4
AXES = ("blk", "inner")
CHUNK = 2
ROWS = 32
MASKED = -1e30
SCALE = 1.0 / math.sqrt(HEAD_SIZE)
EXP2_SCALE = SCALE * math.log2(math.e)

NN = (((1,), (0,)), ((), ()))


def dot(a, b, dims=NN):
    return lax.dot_general(a, b, dims, preferred_element_type=jnp.float32)


def device_count():
    return lax.axis_size("blk") * lax.axis_size("inner")


def passed_along(value, steps):
    count = device_count()
    first, last = (max(0, -steps), min(count, count - steps))
    return lax.ppermute(value, AXES, [(source, source + steps) for source in range(first, last)])


def swapped(value):
    return lax.ppermute(value, AXES, [(source, source ^ 1) for source in range(device_count())])


def run(first, second):
    order = sorted(
        [((i + 0.5) / len(part), k, piece) for k, part in enumerate((second, first)) for i, piece in enumerate(part)],
        key=lambda entry: entry[:2],
    )
    for entry in order:
        entry[2]()


def write_bias(bias_ref, lengths_ref, first_ref, rows):
    docs = lengths_ref.shape[0]
    first = first_ref[0]
    query_pos = first + lax.broadcasted_iota(jnp.int32, (rows, 128), 0)

    def step(doc, carry):
        end, start = carry
        end = end + lengths_ref[doc]
        return end, jnp.where(query_pos >= end, end, start)

    _, start = lax.fori_loop(0, docs, step, (jnp.int32(0), jnp.zeros((rows, 128), jnp.int32)))
    lane = lax.broadcasted_iota(jnp.int32, (rows, 128), 1)
    for part in range(SPAN * rows // 128):
        key_pos = first - (SPAN - 1) * rows + part * 128 + lane
        allowed = (key_pos >= start) & (key_pos <= query_pos)
        bias_ref[:, part * 128 : (part + 1) * 128] = jnp.where(allowed, 0.0, MASKED)


def attention_kernel(first_ref, lengths_ref, q_ref, g_ref, far_ref, mid_ref, near_ref, own_ref, *refs):
    (
        out_ref, dq_ref, dfar_ref, dmid_ref, dnear_ref, down_ref,
        bias_ref, key_ref, value_ref, key_t_ref, value_t_ref, dk_ref, dv_ref, inv_ref, *slots,
    ) = refs[-26:]
    s_refs, p_refs, dp_refs, d_refs, g_refs, delta_refs = (slots[i : i + 2] for i in range(0, 12, 2))
    rows = q_ref.shape[0]
    window = SPAN * rows

    @pl.when(pl.program_id(0) == 0)
    def _():
        write_bias(bias_ref, lengths_ref, first_ref, rows)
        for ref in p_refs:
            ref[...] = jnp.zeros_like(ref)

    for j, block in enumerate((far_ref, mid_ref, near_ref, own_ref)):
        span = slice(j * rows, (j + 1) * rows)
        key_ref[span] = block[:, :HEAD_SIZE]
        value_ref[span] = block[:, HEAD_SIZE:]
        key_t_ref[:, span] = block[:, :HEAD_SIZE].T
        value_t_ref[:, span] = block[:, HEAD_SIZE:].T
    dk_ref[...] = jnp.zeros_like(dk_ref)
    dv_ref[...] = jnp.zeros_like(dv_ref)
    p_refs[1][...] = jnp.zeros_like(p_refs[1])
    for ref in d_refs:
        ref[...] = jnp.zeros_like(ref)
    dp_refs[1][...] = jnp.zeros_like(dp_refs[1])
    g_refs[1][...] = jnp.zeros_like(g_refs[1])
    delta_refs[1][...] = jnp.zeros_like(delta_refs[1])

    chunks = [
        (slice(r, r + ROWS), slice((r + 1) // 128 * 128, -(-(window - rows + r + ROWS) // 128) * 128))
        for r in range(0, rows, ROWS)
    ]

    def columns(head):
        return pl.ds(pl.multiple_of(head * HEAD_SIZE, HEAD_SIZE), HEAD_SIZE)

    tiles = [slice(j * rows, (j + 1) * rows) for j in range(SPAN)]

    def scores(head, slot):
        def piece(tile):
            s_refs[slot][:, tile] = dot(q_ref[:, columns(head)], key_t_ref[:, tile])

        return [functools.partial(piece, tile) for tile in tiles]

    def softmax(slot):
        def piece(here, keys):
            s = s_refs[slot][here, keys] * EXP2_SCALE + bias_ref[here, keys]
            e = jnp.exp2(s - jnp.max(s, axis=1, keepdims=True))
            inv = 1.0 / jnp.sum(e, axis=1, keepdims=True)
            inv_ref[here] = jnp.broadcast_to(inv, (ROWS, HEAD_SIZE))
            p_refs[slot][here, keys] = e.astype(jnp.bfloat16)

        return [functools.partial(piece, *chunk) for chunk in chunks]

    def mix(head, slot):
        cols = columns(head)
        mixed = dot(p_refs[slot][...], value_ref[...])
        inv = inv_ref[...]
        out = (mixed * inv).astype(jnp.bfloat16)
        out_ref[:, cols] = out
        g = g_ref[:, cols].astype(jnp.float32) * inv
        delta = jnp.sum(g * out.astype(jnp.float32), axis=1, keepdims=True)
        delta_refs[slot][...] = jnp.broadcast_to(delta, (rows, HEAD_SIZE))
        g_refs[slot][...] = g.astype(jnp.bfloat16)

    def prob_grad(slot):
        def piece(tile):
            dp_refs[slot][:, tile] = dot(g_refs[slot][...], value_t_ref[:, tile])

        return [functools.partial(piece, tile) for tile in tiles]

    def score_grad(slot):
        def piece(here, keys):
            repeat = (keys.stop - keys.start) // HEAD_SIZE
            delta = jnp.concatenate([delta_refs[slot][here]] * repeat, axis=1)
            p = p_refs[slot][here, keys].astype(jnp.float32)
            d_refs[slot][here, keys] = (p * (dp_refs[slot][here, keys] - delta)).astype(jnp.bfloat16)

        return [functools.partial(piece, *chunk) for chunk in chunks]

    def query_grad(head, slot):
        dq = dot(d_refs[slot][...], key_ref[...]) * SCALE
        dq_ref[:, columns(head)] = dq.astype(jnp.bfloat16)

    def key_grad(head, slot):
        def piece(tile):
            dk_ref[:, tile] += dot(q_ref[:, columns(head)].T, d_refs[slot][:, tile])

        return [functools.partial(piece, tile) for tile in tiles]

    def value_grad(slot):
        def piece(tile):
            dv_ref[:, tile] += dot(g_refs[slot][...].T, p_refs[slot][:, tile])

        return [functools.partial(piece, tile) for tile in tiles]

    run([], scores(0, 0))

    def step(index, carry):
        for slot in range(2):
            head = 2 * index + slot
            older = jnp.maximum(head - 2, 0)
            run(
                softmax(slot),
                scores(jnp.minimum(head + 1, GROUP - 1), 1 - slot) + value_grad(1 - slot),
            )
            run(
                score_grad(1 - slot),
                [functools.partial(mix, head, slot)]
                + [functools.partial(query_grad, older, slot)]
                + key_grad(older, slot)
                + prob_grad(slot),
            )
        return carry

    lax.fori_loop(0, GROUP // 2, step, 0)
    run(
        score_grad(1),
        value_grad(1) + [functools.partial(query_grad, GROUP - 2, 0)] + key_grad(GROUP - 2, 0),
    )
    query_grad(GROUP - 1, 1)
    run([], key_grad(GROUP - 1, 1))
    for j, target in enumerate((dfar_ref, dmid_ref, dnear_ref, down_ref)):
        span = slice(j * rows, (j + 1) * rows)
        target[:, :HEAD_SIZE] = (dk_ref[:, span].T * SCALE).astype(target.dtype)
        target[:, HEAD_SIZE:] = dv_ref[:, span].T.astype(target.dtype)


def attention(chunk, first, lengths, queries, out_grad, blocks, grads):
    rows = queries.shape[0]
    wide = GROUP * HEAD_SIZE
    pair = 2 * HEAD_SIZE
    window = SPAN * rows
    query_spec = pl.BlockSpec((rows, wide), lambda i, *_: (0, chunk * CHUNK + i))
    block_spec = pl.BlockSpec((rows, pair), lambda i, *_: (0, i))
    operands = [first, lengths, queries, out_grad, *blocks]
    in_specs = [query_spec] * 2 + [block_spec] * 4
    aliases = {}
    for at, array in enumerate(grads):
        if array is not None:
            aliases[len(operands)] = at
            operands.append(array)
            in_specs.append(pl.BlockSpec(memory_space=pl.ANY))
    bf16, f32 = jnp.bfloat16, jnp.float32
    results = pl.pallas_call(
        attention_kernel,
        out_shape=[jax.ShapeDtypeStruct(queries.shape, bf16)] * 2
        + [jax.ShapeDtypeStruct((rows, CHUNK * pair), kind) for kind in (bf16, f32, f32, f32)],
        grid_spec=pltpu.PrefetchScalarGridSpec(
            num_scalar_prefetch=2,
            grid=(CHUNK,),
            in_specs=in_specs,
            out_specs=[query_spec] * 2 + [block_spec] * 4,
            scratch_shapes=[
                pltpu.VMEM((rows, window), f32),
                pltpu.VMEM((window, HEAD_SIZE), bf16),
                pltpu.VMEM((window, HEAD_SIZE), bf16),
                pltpu.VMEM((HEAD_SIZE, window), bf16),
                pltpu.VMEM((HEAD_SIZE, window), bf16),
                pltpu.VMEM((HEAD_SIZE, window), f32),
                pltpu.VMEM((HEAD_SIZE, window), f32),
                pltpu.VMEM((rows, HEAD_SIZE), f32),
            ]
            + [
                pltpu.VMEM((rows, columns), kind)
                for columns, kind in (
                    (window, f32),
                    (window, bf16),
                    (window, f32),
                    (window, bf16),
                    (HEAD_SIZE, bf16),
                    (HEAD_SIZE, f32),
                )
                for _ in range(2)
            ],
        ),
        input_output_aliases=aliases,
        compiler_params=pltpu.CompilerParams(vmem_limit_bytes=48 * 1024 * 1024),
        cost_estimate=pl.CostEstimate(
            flops=12 * CHUNK * rows * GROUP * window * HEAD_SIZE * 2,
            bytes_accessed=CHUNK * (4 * rows * wide * 2 + 22 * rows * pair),
            transcendentals=0,
        ),
        name="attention",
    )(*operands)
    return results[:2], results[2:]


def local(queries, keys, values, out_grad, doc_lengths):
    rows = queries.shape[0]
    index = lax.axis_index(AXES)
    odd = index % 2 == 1
    first = (index * rows).astype(jnp.int32).reshape(1)
    bf16, f32 = jnp.bfloat16, jnp.float32
    chunks = range(KEY_VALUE_HEADS // CHUNK)
    owns, mids, nears, fars = [], [], [], []
    for chunk in chunks:
        parts = []
        for head in range(chunk * CHUNK, (chunk + 1) * CHUNK):
            span = slice(head * HEAD_SIZE, (head + 1) * HEAD_SIZE)
            parts += [keys[:, span], values[:, span]]
        owns.append(jnp.concatenate(parts, axis=1))
        mids.append(passed_along(owns[chunk], 2))
        nears.append(swapped(jnp.where(odd, mids[chunk], owns[chunk])))
        fars.append(passed_along(nears[chunk], 2))
    grads = (None, None)
    totals = []
    for chunk in chunks:
        blocks = (fars[chunk], mids[chunk], nears[chunk], owns[chunk])
        grads, parts = attention(chunk, first, doc_lengths, queries, out_grad, blocks, grads)
        far, mid, near, own = parts
        near = (near + passed_along(far, -2).astype(f32)).astype(bf16)
        got = swapped(near).astype(f32)
        mid = (mid + jnp.where(odd, got, 0.0)).astype(bf16)
        own = own + jnp.where(odd, 0.0, got)
        totals.append((own + passed_along(mid, -2).astype(f32)).astype(bf16))
    key_parts, value_parts = [], []
    for total in totals:
        for head in range(CHUNK):
            start = head * 2 * HEAD_SIZE
            key_parts.append(total[:, start : start + HEAD_SIZE])
            value_parts.append(total[:, start + HEAD_SIZE : start + 2 * HEAD_SIZE])
    return (
        grads[0],
        grads[1],
        jnp.concatenate(key_parts, axis=1),
        jnp.concatenate(value_parts, axis=1),
    )


def solution(mesh):
    spec = P(AXES, None)
    return jax.shard_map(
        local,
        mesh=mesh,
        in_specs=(spec, spec, spec, spec, P()),
        out_specs=(spec, spec, spec, spec),
        check_vma=False,
    )
```

```python
import math

import jax
import jax.numpy as jnp
from jax import lax
from jax.experimental import pallas as pl
from jax.experimental.pallas import tpu as pltpu
from jax.sharding import PartitionSpec as P

HEAD_SIZE = 128
QUERY_HEADS = 32
KEY_VALUE_HEADS = 4
GROUP = QUERY_HEADS // KEY_VALUE_HEADS
SPAN = 4
AXES = ("blk", "inner")
CHUNK = 2
ROWS = 32
UNIT = 2
MASKED = -1e30
SCALE = 1.0 / math.sqrt(HEAD_SIZE)
EXP2_SCALE = SCALE * math.log2(math.e)

NN = (((1,), (0,)), ((), ()))
TN = (((0,), (0,)), ((), ()))


def dot(a, b, dims=NN):
    return lax.dot_general(a, b, dims, preferred_element_type=jnp.float32)


def device_count():
    return lax.axis_size("blk") * lax.axis_size("inner")


def passed_along(value, steps):
    count = device_count()
    first, last = (max(0, -steps), min(count, count - steps))
    return lax.ppermute(value, AXES, [(source, source + steps) for source in range(first, last)])


def swapped(value):
    return lax.ppermute(value, AXES, [(source, source ^ 1) for source in range(device_count())])


def write_bias(bias_ref, lengths_ref, first_ref, rows):
    docs = lengths_ref.shape[0]
    first = first_ref[0]
    query_pos = first + lax.broadcasted_iota(jnp.int32, (rows, 128), 0)

    def step(doc, carry):
        end, start = carry
        end = end + lengths_ref[doc]
        return end, jnp.where(query_pos >= end, end, start)

    _, start = lax.fori_loop(0, docs, step, (jnp.int32(0), jnp.zeros((rows, 128), jnp.int32)))
    lane = lax.broadcasted_iota(jnp.int32, (rows, 128), 1)
    for part in range(SPAN * rows // 128):
        key_pos = first - (SPAN - 1) * rows + part * 128 + lane
        allowed = (key_pos >= start) & (key_pos <= query_pos)
        bias_ref[:, part * 128 : (part + 1) * 128] = jnp.where(allowed, 0.0, MASKED)


def attention_kernel(first_ref, lengths_ref, q_ref, g_ref, far_ref, mid_ref, near_ref, own_ref, *refs):
    (
        out_ref, dq_ref, dfar_ref, dmid_ref, dnear_ref, down_ref,
        bias_ref, key_ref, value_ref, key_t_ref, value_t_ref, dk_ref, dv_ref, inv_ref, q_all_ref, *slots,
    ) = refs[-27:]
    s_refs, p_refs, dp_refs, d_refs, g_refs, delta_refs = (slots[i : i + 2] for i in range(0, 12, 2))
    rows = q_ref.shape[0]
    window = SPAN * rows
    stack = UNIT * rows

    @pl.when(pl.program_id(0) == 0)
    def _():
        write_bias(bias_ref, lengths_ref, first_ref, rows)
        for ref in (*p_refs, *d_refs):
            ref[...] = jnp.zeros_like(ref)

    for j, block in enumerate((far_ref, mid_ref, near_ref, own_ref)):
        span = slice(j * rows, (j + 1) * rows)
        key_ref[span] = block[:, :HEAD_SIZE]
        value_ref[span] = block[:, HEAD_SIZE:]
        key_t_ref[:, span] = block[:, :HEAD_SIZE].T
        value_t_ref[:, span] = block[:, HEAD_SIZE:].T
    for head in range(GROUP):
        q_all_ref[head * rows : (head + 1) * rows] = q_ref[:, head * HEAD_SIZE : (head + 1) * HEAD_SIZE]
    dk_ref[...] = jnp.zeros_like(dk_ref)
    dv_ref[...] = jnp.zeros_like(dv_ref)
    p_refs[1][...] = jnp.zeros_like(p_refs[1])
    dp_refs[1][...] = jnp.zeros_like(dp_refs[1])
    g_refs[1][...] = jnp.zeros_like(g_refs[1])
    delta_refs[1][...] = jnp.zeros_like(delta_refs[1])

    chunks = [
        (
            slice(r, r + ROWS),
            slice(h * rows + r, h * rows + r + ROWS),
            slice((r + 1) // 128 * 128, -(-(window - rows + r + ROWS) // 128) * 128),
        )
        for h in range(UNIT)
        for r in range(0, rows, ROWS)
    ]

    def queries(unit):
        return q_all_ref[pl.ds(pl.multiple_of(unit * stack, stack), stack)]

    def heads(unit):
        return [
            (
                slice(i * rows, (i + 1) * rows),
                pl.ds(pl.multiple_of((unit * UNIT + i) * HEAD_SIZE, HEAD_SIZE), HEAD_SIZE),
            )
            for i in range(UNIT)
        ]

    def scores(unit, slot):
        s_refs[slot][...] = dot(queries(unit), key_t_ref[...])

    def softmax(slot):
        for row, here, keys in chunks:
            s = s_refs[slot][here, keys] * EXP2_SCALE + bias_ref[row, keys]
            e = jnp.exp2(s - jnp.max(s, axis=1, keepdims=True))
            inv = 1.0 / jnp.sum(e, axis=1, keepdims=True)
            inv_ref[here] = jnp.broadcast_to(inv, (ROWS, HEAD_SIZE))
            p_refs[slot][here, keys] = e.astype(jnp.bfloat16)

    def mix(unit, slot):
        mixed = dot(p_refs[slot][...], value_ref[...])
        for here, cols in heads(unit):
            inv = inv_ref[here]
            out = (mixed[here] * inv).astype(jnp.bfloat16)
            out_ref[:, cols] = out
            g = g_ref[:, cols].astype(jnp.float32) * inv
            delta = jnp.sum(g * out.astype(jnp.float32), axis=1, keepdims=True)
            delta_refs[slot][here] = jnp.broadcast_to(delta, (rows, HEAD_SIZE))
            g_refs[slot][here] = g.astype(jnp.bfloat16)
        dp_refs[slot][...] = dot(g_refs[slot][...], value_t_ref[...])

    def score_grad(slot):
        for row, here, keys in chunks:
            repeat = (keys.stop - keys.start) // HEAD_SIZE
            delta = jnp.concatenate([delta_refs[slot][here]] * repeat, axis=1)
            p = p_refs[slot][here, keys].astype(jnp.float32)
            d_refs[slot][here, keys] = (p * (dp_refs[slot][here, keys] - delta)).astype(jnp.bfloat16)

    def spread(unit, slot):
        dq = (dot(d_refs[slot][...], key_ref[...]) * SCALE).astype(jnp.bfloat16)
        for here, cols in heads(unit):
            dq_ref[:, cols] = dq[here]
        dk_ref[...] += dot(d_refs[slot][...], queries(unit), TN)
        dv_ref[...] += dot(p_refs[slot][...], g_refs[slot][...], TN)

    scores(0, 0)
    units = GROUP // UNIT

    def step(index, carry):
        for slot in range(2):
            unit = 2 * index + slot
            before = jnp.maximum(unit - 1, 0)
            scores(jnp.minimum(unit + 1, units - 1), 1 - slot)
            score_grad(1 - slot)
            softmax(slot)
            spread(before, 1 - slot)
            mix(unit, slot)
        return carry

    lax.fori_loop(0, units // 2, step, 0)
    score_grad(1)
    spread(units - 1, 1)
    for j, target in enumerate((dfar_ref, dmid_ref, dnear_ref, down_ref)):
        span = slice(j * rows, (j + 1) * rows)
        target[:, :HEAD_SIZE] = (dk_ref[span] * SCALE).astype(target.dtype)
        target[:, HEAD_SIZE:] = dv_ref[span].astype(target.dtype)


def attention(chunk, first, lengths, queries, out_grad, blocks, grads):
    rows = queries.shape[0]
    wide = GROUP * HEAD_SIZE
    pair = 2 * HEAD_SIZE
    window = SPAN * rows
    query_spec = pl.BlockSpec((rows, wide), lambda i, *_: (0, chunk * CHUNK + i))
    block_spec = pl.BlockSpec((rows, pair), lambda i, *_: (0, i))
    operands = [first, lengths, queries, out_grad, *blocks]
    in_specs = [query_spec] * 2 + [block_spec] * 4
    aliases = {}
    for at, array in enumerate(grads):
        if array is not None:
            aliases[len(operands)] = at
            operands.append(array)
            in_specs.append(pl.BlockSpec(memory_space=pl.ANY))
    bf16, f32 = jnp.bfloat16, jnp.float32
    results = pl.pallas_call(
        attention_kernel,
        out_shape=[jax.ShapeDtypeStruct(queries.shape, bf16)] * 2
        + [jax.ShapeDtypeStruct((rows, CHUNK * pair), kind) for kind in (bf16, f32, f32, f32)],
        grid_spec=pltpu.PrefetchScalarGridSpec(
            num_scalar_prefetch=2,
            grid=(CHUNK,),
            in_specs=in_specs,
            out_specs=[query_spec] * 2 + [block_spec] * 4,
            scratch_shapes=[
                pltpu.VMEM((rows, window), f32),
                pltpu.VMEM((window, HEAD_SIZE), bf16),
                pltpu.VMEM((window, HEAD_SIZE), bf16),
                pltpu.VMEM((HEAD_SIZE, window), bf16),
                pltpu.VMEM((HEAD_SIZE, window), bf16),
                pltpu.VMEM((window, HEAD_SIZE), f32),
                pltpu.VMEM((window, HEAD_SIZE), f32),
                pltpu.VMEM((UNIT * rows, HEAD_SIZE), f32),
                pltpu.VMEM((GROUP * rows, HEAD_SIZE), bf16),
            ]
            + [
                pltpu.VMEM((UNIT * rows, columns), kind)
                for columns, kind in (
                    (window, f32),
                    (window, bf16),
                    (window, f32),
                    (window, bf16),
                    (HEAD_SIZE, bf16),
                    (HEAD_SIZE, f32),
                )
                for _ in range(2)
            ],
        ),
        input_output_aliases=aliases,
        compiler_params=pltpu.CompilerParams(vmem_limit_bytes=48 * 1024 * 1024),
        cost_estimate=pl.CostEstimate(
            flops=12 * CHUNK * rows * GROUP * window * HEAD_SIZE * 2,
            bytes_accessed=CHUNK * (4 * rows * wide * 2 + 22 * rows * pair),
            transcendentals=0,
        ),
        name="attention",
    )(*operands)
    return results[:2], results[2:]


def local(queries, keys, values, out_grad, doc_lengths):
    rows = queries.shape[0]
    index = lax.axis_index(AXES)
    odd = index % 2 == 1
    first = (index * rows).astype(jnp.int32).reshape(1)
    bf16, f32 = jnp.bfloat16, jnp.float32
    chunks = range(KEY_VALUE_HEADS // CHUNK)
    owns, mids, nears, fars = [], [], [], []
    for chunk in chunks:
        parts = []
        for head in range(chunk * CHUNK, (chunk + 1) * CHUNK):
            span = slice(head * HEAD_SIZE, (head + 1) * HEAD_SIZE)
            parts += [keys[:, span], values[:, span]]
        owns.append(jnp.concatenate(parts, axis=1))
        mids.append(passed_along(owns[chunk], 2))
        nears.append(swapped(jnp.where(odd, mids[chunk], owns[chunk])))
        fars.append(passed_along(nears[chunk], 2))
    grads = (None, None)
    totals = []
    for chunk in chunks:
        blocks = (fars[chunk], mids[chunk], nears[chunk], owns[chunk])
        grads, parts = attention(chunk, first, doc_lengths, queries, out_grad, blocks, grads)
        far, mid, near, own = parts
        near = (near + passed_along(far, -2).astype(f32)).astype(bf16)
        got = swapped(near).astype(f32)
        mid = (mid + jnp.where(odd, got, 0.0)).astype(bf16)
        own = own + jnp.where(odd, 0.0, got)
        totals.append((own + passed_along(mid, -2).astype(f32)).astype(bf16))
    key_parts, value_parts = [], []
    for total in totals:
        for head in range(CHUNK):
            start = head * 2 * HEAD_SIZE
            key_parts.append(total[:, start : start + HEAD_SIZE])
            value_parts.append(total[:, start + HEAD_SIZE : start + 2 * HEAD_SIZE])
    return (
        grads[0],
        grads[1],
        jnp.concatenate(key_parts, axis=1),
        jnp.concatenate(value_parts, axis=1),
    )


def solution(mesh):
    spec = P(AXES, None)
    return jax.shard_map(
        local,
        mesh=mesh,
        in_specs=(spec, spec, spec, spec, P()),
        out_specs=(spec, spec, spec, spec),
        check_vma=False,
    )
```

```python
import math

import jax
import jax.numpy as jnp
from jax import lax
from jax.experimental import pallas as pl
from jax.experimental.pallas import tpu as pltpu
from jax.sharding import PartitionSpec as P

HEAD_SIZE = 128
QUERY_HEADS = 32
KEY_VALUE_HEADS = 4
GROUP = QUERY_HEADS // KEY_VALUE_HEADS
SPAN = 4
AXES = ("blk", "inner")
CHUNK = 2
ROWS = 32
MASKED = -1e30
SCALE = 1.0 / math.sqrt(HEAD_SIZE)
EXP2_SCALE = SCALE * math.log2(math.e)

NN = (((1,), (0,)), ((), ()))


def dot(a, b, dims=NN):
    return lax.dot_general(a, b, dims, preferred_element_type=jnp.float32)


def device_count():
    return lax.axis_size("blk") * lax.axis_size("inner")


def passed_along(value, steps):
    count = device_count()
    first, last = (max(0, -steps), min(count, count - steps))
    return lax.ppermute(value, AXES, [(source, source + steps) for source in range(first, last)])


def swapped(value):
    return lax.ppermute(value, AXES, [(source, source ^ 1) for source in range(device_count())])


def write_masks(bias_ref, old_ref, cut_ref, lengths_ref, first_ref, rows):
    docs = lengths_ref.shape[0]
    first = first_ref[0]
    row = lax.broadcasted_iota(jnp.int32, (rows, 128), 0)
    query_pos = first + row

    def step(doc, carry):
        end, start = carry
        end = end + lengths_ref[doc]
        return end, jnp.where(query_pos >= end, end, start)

    _, start = lax.fori_loop(0, docs, step, (jnp.int32(0), jnp.zeros((rows, 128), jnp.int32)))
    lane = lax.broadcasted_iota(jnp.int32, (rows, 128), 1)
    old = start < first - (SPAN - 2) * rows
    old_ref[...] = jnp.where(old, 1.0, 0.0)
    cut = jnp.min(jnp.where(old, start - (first - (SPAN - 1) * rows), rows), axis=0, keepdims=True)
    cut_ref[...] = jnp.broadcast_to(cut, cut_ref.shape)
    cut = jnp.broadcast_to(cut, (rows, 128))
    for part in range((SPAN - 1) * rows // 128):
        offset = part * 128 + lane
        if part < rows // 128:
            own = (offset <= row) & ((first + offset >= start) | (old & (offset < cut)))
            allowed = own | (old & (offset >= cut))
        else:
            allowed = first - (SPAN - 1) * rows + offset >= start
        bias_ref[:, part * 128 : (part + 1) * 128] = jnp.where(allowed, 0.0, MASKED)


def attention_kernel(first_ref, lengths_ref, q_ref, g_ref, far_ref, mid_ref, near_ref, own_ref, *refs):
    (
        out_ref, dq_ref, dfar_ref, dmid_ref, dnear_ref, down_ref,
        bias_ref, old_ref, cut_ref,
        key_ref, value_ref, key_t_ref, value_t_ref, key2_ref, value2_ref, key2_t_ref, value2_t_ref,
        dk_ref, dv_ref, dk2_ref, dv2_ref, inv_ref, *slots,
    ) = refs[-34:]
    s_refs, p_refs, dp_refs, d_refs, g_refs, delta_refs = (slots[i : i + 2] for i in range(0, 12, 2))
    rows = q_ref.shape[0]
    window = (SPAN - 1) * rows
    two = slice(0, rows)
    rest = slice(rows, window)

    @pl.when(pl.program_id(0) == 0)
    def _():
        write_masks(bias_ref, old_ref, cut_ref, lengths_ref, first_ref, rows)

    for j, block in enumerate((mid_ref, near_ref)):
        span = slice(j * rows, (j + 1) * rows)
        key_ref[span] = block[:, :HEAD_SIZE]
        value_ref[span] = block[:, HEAD_SIZE:]
        key_t_ref[:, span] = block[:, :HEAD_SIZE].T
        value_t_ref[:, span] = block[:, HEAD_SIZE:].T
    from_far = lax.broadcasted_iota(jnp.int32, (rows, 2 * HEAD_SIZE), 0) >= cut_ref[0, 0]
    mixed = jnp.where(from_far, far_ref[...].astype(jnp.float32), own_ref[...].astype(jnp.float32))
    mixed = mixed.astype(jnp.bfloat16)
    for j, block in enumerate((mixed, own_ref)):
        span = slice(j * HEAD_SIZE, (j + 1) * HEAD_SIZE)
        key2_ref[:, span] = block[:, :HEAD_SIZE]
        value2_ref[:, span] = block[:, HEAD_SIZE:]
        key2_t_ref[span] = block[:, :HEAD_SIZE].T
        value2_t_ref[span] = block[:, HEAD_SIZE:].T
    for ref in (dk_ref, dv_ref, dk2_ref, dv2_ref, p_refs[1], dp_refs[1], g_refs[1], delta_refs[1]):
        ref[...] = jnp.zeros_like(ref)

    def columns(head):
        return pl.ds(pl.multiple_of(head * HEAD_SIZE, HEAD_SIZE), HEAD_SIZE)

    def doubled(x):
        old = old_ref[...].astype(jnp.bfloat16)
        return jnp.concatenate([x * old, x * (1 - old)], axis=1)

    def picked(x):
        return jnp.where(old_ref[...] > 0.5, x[:, :HEAD_SIZE], x[:, HEAD_SIZE:])

    def scores(head, slot):
        q = q_ref[:, columns(head)]
        s_refs[slot][:, two] = dot(doubled(q), key2_t_ref[...])
        s_refs[slot][:, rest] = dot(q, key_t_ref[...])

    def softmax(slot):
        for r in range(0, rows, ROWS):
            here = slice(r, r + ROWS)
            s = s_refs[slot][here] * EXP2_SCALE + bias_ref[here]
            e = jnp.exp2(s - jnp.max(s, axis=1, keepdims=True))
            inv = 1.0 / jnp.sum(e, axis=1, keepdims=True)
            inv_ref[here] = jnp.broadcast_to(inv, (ROWS, HEAD_SIZE))
            p_refs[slot][here] = e.astype(jnp.bfloat16)

    def mix(head, slot):
        cols = columns(head)
        total = picked(dot(p_refs[slot][:, two], value2_ref[...])) + dot(p_refs[slot][:, rest], value_ref[...])
        inv = inv_ref[...]
        out = (total * inv).astype(jnp.bfloat16)
        out_ref[:, cols] = out
        g = g_ref[:, cols].astype(jnp.float32) * inv
        delta = jnp.sum(g * out.astype(jnp.float32), axis=1, keepdims=True)
        delta_refs[slot][...] = jnp.broadcast_to(delta, (rows, HEAD_SIZE))
        g = g.astype(jnp.bfloat16)
        g_refs[slot][...] = g
        dp_refs[slot][:, two] = dot(doubled(g), value2_t_ref[...])
        dp_refs[slot][:, rest] = dot(g, value_t_ref[...])

    def score_grad(slot):
        for r in range(0, rows, ROWS):
            here = slice(r, r + ROWS)
            delta = jnp.concatenate([delta_refs[slot][here]] * (window // HEAD_SIZE), axis=1)
            d_refs[slot][here] = p_refs[slot][here] * (dp_refs[slot][here] - delta).astype(jnp.bfloat16)

    def spread(head, slot):
        cols = columns(head)
        total = picked(dot(d_refs[slot][:, two], key2_ref[...])) + dot(d_refs[slot][:, rest], key_ref[...])
        dq_ref[:, cols] = (total * SCALE).astype(jnp.bfloat16)
        q = q_ref[:, cols]
        g = g_refs[slot][...]
        dk2_ref[...] += dot(doubled(q).T, d_refs[slot][:, two])
        dk_ref[...] += dot(q.T, d_refs[slot][:, rest])
        dv2_ref[...] += dot(doubled(g).T, p_refs[slot][:, two])
        dv_ref[...] += dot(g.T, p_refs[slot][:, rest])

    scores(0, 0)

    def step(index, carry):
        for slot in range(2):
            head = 2 * index + slot
            before = jnp.maximum(head - 1, 0)
            scores(jnp.minimum(head + 1, GROUP - 1), 1 - slot)
            score_grad(1 - slot)
            softmax(slot)
            spread(before, 1 - slot)
            mix(head, slot)
        return carry

    lax.fori_loop(0, GROUP // 2, step, 0)
    score_grad(1)
    spread(GROUP - 1, 1)
    from_far = from_far[:, :HEAD_SIZE]
    for part, grad, grad2, scale in ((0, dk_ref, dk2_ref, SCALE), (1, dv_ref, dv2_ref, 1.0)):
        span = slice(part * HEAD_SIZE, (part + 1) * HEAD_SIZE)
        either = grad2[:HEAD_SIZE].T * scale
        own = grad2[HEAD_SIZE:].T * scale
        dfar_ref[:, span] = jnp.where(from_far, either, 0.0).astype(dfar_ref.dtype)
        down_ref[:, span] = own + jnp.where(from_far, 0.0, either)
        dmid_ref[:, span] = grad[:, :rows].T * scale
        dnear_ref[:, span] = grad[:, rows:].T * scale


def attention(chunk, first, lengths, queries, out_grad, blocks, grads):
    rows = queries.shape[0]
    wide = GROUP * HEAD_SIZE
    pair = 2 * HEAD_SIZE
    window = (SPAN - 1) * rows
    query_spec = pl.BlockSpec((rows, wide), lambda i, *_: (0, chunk * CHUNK + i))
    block_spec = pl.BlockSpec((rows, pair), lambda i, *_: (0, i))
    operands = [first, lengths, queries, out_grad, *blocks]
    in_specs = [query_spec] * 2 + [block_spec] * 4
    aliases = {}
    for at, array in enumerate(grads):
        if array is not None:
            aliases[len(operands)] = at
            operands.append(array)
            in_specs.append(pl.BlockSpec(memory_space=pl.ANY))
    bf16, f32 = jnp.bfloat16, jnp.float32
    results = pl.pallas_call(
        attention_kernel,
        out_shape=[jax.ShapeDtypeStruct(queries.shape, bf16)] * 2
        + [jax.ShapeDtypeStruct((rows, CHUNK * pair), kind) for kind in (bf16, f32, f32, f32)],
        grid_spec=pltpu.PrefetchScalarGridSpec(
            num_scalar_prefetch=2,
            grid=(CHUNK,),
            in_specs=in_specs,
            out_specs=[query_spec] * 2 + [block_spec] * 4,
            scratch_shapes=[
                pltpu.VMEM(shape, kind)
                for shape, kind, count in (
                    ((rows, window), f32, 1),
                    ((rows, HEAD_SIZE), f32, 1),
                    ((8, HEAD_SIZE), jnp.int32, 1),
                    ((2 * rows, HEAD_SIZE), bf16, 2),
                    ((HEAD_SIZE, 2 * rows), bf16, 2),
                    ((rows, pair), bf16, 2),
                    ((pair, rows), bf16, 2),
                    ((HEAD_SIZE, 2 * rows), f32, 2),
                    ((pair, rows), f32, 2),
                    ((rows, HEAD_SIZE), f32, 1),
                    ((rows, window), f32, 2),
                    ((rows, window), bf16, 2),
                    ((rows, window), f32, 2),
                    ((rows, window), bf16, 2),
                    ((rows, HEAD_SIZE), bf16, 2),
                    ((rows, HEAD_SIZE), f32, 2),
                )
                for _ in range(count)
            ],
        ),
        input_output_aliases=aliases,
        compiler_params=pltpu.CompilerParams(vmem_limit_bytes=48 * 1024 * 1024),
        cost_estimate=pl.CostEstimate(
            flops=12 * CHUNK * rows * GROUP * window * HEAD_SIZE * 2,
            bytes_accessed=CHUNK * (4 * rows * wide * 2 + 22 * rows * pair),
            transcendentals=0,
        ),
        name="attention",
    )(*operands)
    return results[:2], results[2:]


def local(queries, keys, values, out_grad, doc_lengths):
    rows = queries.shape[0]
    index = lax.axis_index(AXES)
    odd = index % 2 == 1
    first = (index * rows).astype(jnp.int32).reshape(1)
    bf16, f32 = jnp.bfloat16, jnp.float32
    chunks = range(KEY_VALUE_HEADS // CHUNK)
    owns, mids, nears, fars = [], [], [], []
    for chunk in chunks:
        parts = []
        for head in range(chunk * CHUNK, (chunk + 1) * CHUNK):
            span = slice(head * HEAD_SIZE, (head + 1) * HEAD_SIZE)
            parts += [keys[:, span], values[:, span]]
        owns.append(jnp.concatenate(parts, axis=1))
        mids.append(passed_along(owns[chunk], 2))
        nears.append(swapped(jnp.where(odd, mids[chunk], owns[chunk])))
        fars.append(passed_along(nears[chunk], 2))
    grads = (None, None)
    totals = []
    for chunk in chunks:
        blocks = (fars[chunk], mids[chunk], nears[chunk], owns[chunk])
        grads, parts = attention(chunk, first, doc_lengths, queries, out_grad, blocks, grads)
        far, mid, near, own = parts
        near = (near + passed_along(far, -2).astype(f32)).astype(bf16)
        got = swapped(near).astype(f32)
        mid = (mid + jnp.where(odd, got, 0.0)).astype(bf16)
        own = own + jnp.where(odd, 0.0, got)
        totals.append((own + passed_along(mid, -2).astype(f32)).astype(bf16))
    key_parts, value_parts = [], []
    for total in totals:
        for head in range(CHUNK):
            start = head * 2 * HEAD_SIZE
            key_parts.append(total[:, start : start + HEAD_SIZE])
            value_parts.append(total[:, start + HEAD_SIZE : start + 2 * HEAD_SIZE])
    return (
        grads[0],
        grads[1],
        jnp.concatenate(key_parts, axis=1),
        jnp.concatenate(value_parts, axis=1),
    )


def solution(mesh):
    spec = P(AXES, None)
    return jax.shard_map(
        local,
        mesh=mesh,
        in_specs=(spec, spec, spec, spec, P()),
        out_specs=(spec, spec, spec, spec),
        check_vma=False,
    )
```

```python
import math

import jax
import jax.numpy as jnp
from jax import lax
from jax.experimental import pallas as pl
from jax.experimental.pallas import tpu as pltpu
from jax.sharding import PartitionSpec as P

HEAD_SIZE = 128
QUERY_HEADS = 32
KEY_VALUE_HEADS = 4
GROUP = QUERY_HEADS // KEY_VALUE_HEADS
SPAN = 4
AXES = ("blk", "inner")
CHUNK = 2
ROWS = 32
MASKED = -1e30
SCALE = 1.0 / math.sqrt(HEAD_SIZE)
EXP2_SCALE = SCALE * math.log2(math.e)

NN = (((1,), (0,)), ((), ()))


def dot(a, b, dims=NN):
    return lax.dot_general(a, b, dims, preferred_element_type=jnp.float32)


def device_count():
    return lax.axis_size("blk") * lax.axis_size("inner")


def passed_along(value, steps):
    count = device_count()
    first, last = (max(0, -steps), min(count, count - steps))
    return lax.ppermute(value, AXES, [(source, source + steps) for source in range(first, last)])


def swapped(value):
    return lax.ppermute(value, AXES, [(source, source ^ 1) for source in range(device_count())])


def write_masks(bias_ref, old_ref, cut_ref, lengths_ref, first_ref, rows):
    docs = lengths_ref.shape[0]
    first = first_ref[0]
    row = lax.broadcasted_iota(jnp.int32, (rows, 128), 0)
    query_pos = first + row

    def step(doc, carry):
        end, start = carry
        end = end + lengths_ref[doc]
        return end, jnp.where(query_pos >= end, end, start)

    _, start = lax.fori_loop(0, docs, step, (jnp.int32(0), jnp.zeros((rows, 128), jnp.int32)))
    lane = lax.broadcasted_iota(jnp.int32, (rows, 128), 1)
    old = start < first - (SPAN - 2) * rows
    old_ref[...] = jnp.where(old, 1.0, 0.0)
    cut = jnp.min(jnp.where(old, start - (first - (SPAN - 1) * rows), rows), axis=0, keepdims=True)
    cut_ref[...] = jnp.broadcast_to(cut, cut_ref.shape)
    cut = jnp.broadcast_to(cut, (rows, 128))
    for part in range((SPAN - 1) * rows // 128):
        offset = part * 128 + lane
        if part < rows // 128:
            own = (offset <= row) & ((first + offset >= start) | (old & (offset < cut)))
            allowed = own | (old & (offset >= cut))
        else:
            allowed = first - (SPAN - 1) * rows + offset >= start
        bias_ref[:, part * 128 : (part + 1) * 128] = jnp.where(allowed, 0.0, MASKED)


def attention_kernel(first_ref, lengths_ref, q_ref, g_ref, far_ref, mid_ref, near_ref, own_ref, *refs):
    (
        out_ref, dq_ref, dfar_ref, dmid_ref, dnear_ref, down_ref,
        bias_ref, old_ref, cut_ref,
        key_ref, value_ref, key_t_ref, value_t_ref, key2_ref, value2_ref, key2_t_ref, value2_t_ref,
        dk_ref, dv_ref, dk2_ref, dv2_ref, *slots,
    ) = refs[-37:]
    p_refs, (s_refs, dp_refs, d_refs, g_refs, delta_refs, inv_refs) = (
        slots[:4],
        (slots[i : i + 2] for i in range(4, 16, 2)),
    )
    rows = q_ref.shape[0]
    window = (SPAN - 1) * rows
    heads = CHUNK * GROUP
    two = slice(0, rows)
    rest = slice(rows, window)

    write_masks(bias_ref, old_ref, cut_ref, lengths_ref, first_ref, rows)
    from_far = lax.broadcasted_iota(jnp.int32, (rows, 2 * HEAD_SIZE), 0) >= cut_ref[0, 0]
    for kv in range(CHUNK):
        pair = slice(kv * 2 * HEAD_SIZE, (kv + 1) * 2 * HEAD_SIZE)
        far, mid, near, own = (ref[:, pair] for ref in (far_ref, mid_ref, near_ref, own_ref))
        for j, block in enumerate((mid, near)):
            span = slice(j * rows, (j + 1) * rows)
            key_ref[kv, span] = block[:, :HEAD_SIZE]
            value_ref[kv, span] = block[:, HEAD_SIZE:]
            key_t_ref[kv, :, span] = block[:, :HEAD_SIZE].T
            value_t_ref[kv, :, span] = block[:, HEAD_SIZE:].T
        mixed = jnp.where(from_far, far.astype(jnp.float32), own.astype(jnp.float32))
        for j, block in enumerate((mixed.astype(jnp.bfloat16), own)):
            span = slice(j * HEAD_SIZE, (j + 1) * HEAD_SIZE)
            key2_ref[kv, :, span] = block[:, :HEAD_SIZE]
            value2_ref[kv, :, span] = block[:, HEAD_SIZE:]
            key2_t_ref[kv, span] = block[:, :HEAD_SIZE].T
            value2_t_ref[kv, span] = block[:, HEAD_SIZE:].T
    for ref in (dk_ref, dv_ref, dk2_ref, dv2_ref, p_refs[2], p_refs[3], dp_refs[0], delta_refs[0], g_refs[0]):
        ref[...] = jnp.zeros_like(ref)
    inv_refs[1][...] = jnp.ones_like(inv_refs[1])

    def columns(head):
        return pl.ds(pl.multiple_of(head * HEAD_SIZE, HEAD_SIZE), HEAD_SIZE)

    def doubled(x):
        old = old_ref[...].astype(jnp.bfloat16)
        return jnp.concatenate([x * old, x * (1 - old)], axis=1)

    def picked(x):
        return jnp.where(old_ref[...] > 0.5, x[:, :HEAD_SIZE], x[:, HEAD_SIZE:])

    def scores(head, slot):
        kv = head // GROUP
        q = q_ref[:, columns(head)]
        s_refs[slot % 2][:, two] = dot(doubled(q), key2_t_ref[kv])
        s_refs[slot % 2][:, rest] = dot(q, key_t_ref[kv])

    def softmax(slot):
        for r in range(0, rows, ROWS):
            here = slice(r, r + ROWS)
            s = s_refs[slot % 2][here] * EXP2_SCALE + bias_ref[here]
            e = jnp.exp2(s - jnp.max(s, axis=1, keepdims=True))
            inv = 1.0 / jnp.sum(e, axis=1, keepdims=True)
            inv_refs[slot % 2][here] = jnp.broadcast_to(inv, (ROWS, HEAD_SIZE))
            p_refs[slot][here] = e.astype(jnp.bfloat16)

    def mix(head, slot):
        kv, cols = head // GROUP, columns(head)
        p_ref, at = p_refs[slot], slot % 2
        total = picked(dot(p_ref[:, two], value2_ref[kv])) + dot(p_ref[:, rest], value_ref[kv])
        inv = inv_refs[at][...]
        out = (total * inv).astype(jnp.bfloat16)
        out_ref[:, cols] = out
        g = g_ref[:, cols].astype(jnp.float32) * inv
        delta = jnp.sum(g * out.astype(jnp.float32), axis=1, keepdims=True)
        delta_refs[at][...] = jnp.broadcast_to(delta, (rows, HEAD_SIZE))
        g = g.astype(jnp.bfloat16)
        g_refs[at][...] = g
        dp_refs[at][:, two] = dot(doubled(g), value2_t_ref[kv])
        dp_refs[at][:, rest] = dot(g, value_t_ref[kv])

    def score_grad(slot):
        p_ref, at = p_refs[slot], slot % 2
        for r in range(0, rows, ROWS):
            here = slice(r, r + ROWS)
            delta = jnp.concatenate([delta_refs[at][here]] * (window // HEAD_SIZE), axis=1)
            d_refs[at][here] = p_ref[here] * (dp_refs[at][here] - delta).astype(jnp.bfloat16)

    def spread(head, slot):
        kv, cols = head // GROUP, columns(head)
        p_ref, at = p_refs[slot], slot % 2
        d_ref = d_refs[at]
        total = picked(dot(d_ref[:, two], key2_ref[kv])) + dot(d_ref[:, rest], key_ref[kv])
        dq_ref[:, cols] = (total * SCALE).astype(jnp.bfloat16)
        q = q_ref[:, cols]
        g = g_refs[at][...]
        dk2_ref[kv] += dot(doubled(q).T, d_ref[:, two])
        dk_ref[kv] += dot(q.T, d_ref[:, rest])
        dv2_ref[kv] += dot(doubled(g).T, p_ref[:, two])
        dv_ref[kv] += dot(g.T, p_ref[:, rest])

    scores(0, 0)

    def step(index, carry):
        for slot in range(4):
            head = 4 * index + slot
            scores(jnp.minimum(head + 1, heads - 1), (slot + 1) % 4)
            score_grad((slot + 2) % 4)
            softmax(slot)
            spread(jnp.maximum(head - 2, 0), (slot + 2) % 4)
            mix(jnp.maximum(head - 1, 0), (slot + 3) % 4)
        return carry

    lax.fori_loop(0, heads // 4, step, 0)
    score_grad(2)
    mix(heads - 1, 3)
    spread(heads - 2, 2)
    score_grad(3)
    spread(heads - 1, 3)
    from_far = from_far[:, :HEAD_SIZE]
    for kv in range(CHUNK):
        for part, grad, grad2, scale in ((0, dk_ref, dk2_ref, SCALE), (1, dv_ref, dv2_ref, 1.0)):
            start = (2 * kv + part) * HEAD_SIZE
            span = slice(start, start + HEAD_SIZE)
            either = grad2[kv, :HEAD_SIZE].T * scale
            own = grad2[kv, HEAD_SIZE:].T * scale
            dfar_ref[:, span] = jnp.where(from_far, either, 0.0).astype(dfar_ref.dtype)
            down_ref[:, span] = own + jnp.where(from_far, 0.0, either)
            dmid_ref[:, span] = grad[kv, :, :rows].T * scale
            dnear_ref[:, span] = grad[kv, :, rows:].T * scale


def attention(chunk, first, lengths, queries, out_grad, blocks, grads):
    rows = queries.shape[0]
    wide = CHUNK * GROUP * HEAD_SIZE
    pair = 2 * HEAD_SIZE
    window = (SPAN - 1) * rows
    query_spec = pl.BlockSpec((rows, wide), lambda i, *_: (0, chunk))
    block_spec = pl.BlockSpec((rows, CHUNK * pair), lambda i, *_: (0, 0))
    operands = [first, lengths, queries, out_grad, *blocks]
    in_specs = [query_spec] * 2 + [block_spec] * 4
    aliases = {}
    for at, array in enumerate(grads):
        if array is not None:
            aliases[len(operands)] = at
            operands.append(array)
            in_specs.append(pl.BlockSpec(memory_space=pl.ANY))
    bf16, f32 = jnp.bfloat16, jnp.float32
    results = pl.pallas_call(
        attention_kernel,
        out_shape=[jax.ShapeDtypeStruct(queries.shape, bf16)] * 2
        + [jax.ShapeDtypeStruct((rows, CHUNK * pair), kind) for kind in (bf16, f32, f32, f32)],
        grid_spec=pltpu.PrefetchScalarGridSpec(
            num_scalar_prefetch=2,
            grid=(1,),
            in_specs=in_specs,
            out_specs=[query_spec] * 2 + [block_spec] * 4,
            scratch_shapes=[
                pltpu.VMEM(shape, kind)
                for shape, kind, count in (
                    ((rows, window), f32, 1),
                    ((rows, HEAD_SIZE), f32, 1),
                    ((8, HEAD_SIZE), jnp.int32, 1),
                    ((CHUNK, 2 * rows, HEAD_SIZE), bf16, 2),
                    ((CHUNK, HEAD_SIZE, 2 * rows), bf16, 2),
                    ((CHUNK, rows, pair), bf16, 2),
                    ((CHUNK, pair, rows), bf16, 2),
                    ((CHUNK, HEAD_SIZE, 2 * rows), f32, 2),
                    ((CHUNK, pair, rows), f32, 2),
                    ((rows, window), bf16, 4),
                    ((rows, window), f32, 2),
                    ((rows, window), f32, 2),
                    ((rows, window), bf16, 2),
                    ((rows, HEAD_SIZE), bf16, 2),
                    ((rows, HEAD_SIZE), f32, 2),
                    ((rows, HEAD_SIZE), f32, 2),
                )
                for _ in range(count)
            ],
        ),
        input_output_aliases=aliases,
        compiler_params=pltpu.CompilerParams(vmem_limit_bytes=48 * 1024 * 1024),
        cost_estimate=pl.CostEstimate(
            flops=12 * CHUNK * rows * GROUP * window * HEAD_SIZE * 2,
            bytes_accessed=4 * rows * wide * 2 + CHUNK * 22 * rows * pair,
            transcendentals=0,
        ),
        name="attention",
    )(*operands)
    return results[:2], results[2:]


def local(queries, keys, values, out_grad, doc_lengths):
    rows = queries.shape[0]
    index = lax.axis_index(AXES)
    odd = index % 2 == 1
    first = (index * rows).astype(jnp.int32).reshape(1)
    bf16, f32 = jnp.bfloat16, jnp.float32
    chunks = range(KEY_VALUE_HEADS // CHUNK)
    owns, mids, nears, fars = [], [], [], []
    for chunk in chunks:
        parts = []
        for head in range(chunk * CHUNK, (chunk + 1) * CHUNK):
            span = slice(head * HEAD_SIZE, (head + 1) * HEAD_SIZE)
            parts += [keys[:, span], values[:, span]]
        owns.append(jnp.concatenate(parts, axis=1))
        mids.append(passed_along(owns[chunk], 2))
        nears.append(swapped(jnp.where(odd, mids[chunk], owns[chunk])))
        fars.append(passed_along(nears[chunk], 2))
    grads = (None, None)
    totals = []
    for chunk in chunks:
        blocks = (fars[chunk], mids[chunk], nears[chunk], owns[chunk])
        grads, parts = attention(chunk, first, doc_lengths, queries, out_grad, blocks, grads)
        far, mid, near, own = parts
        near = (near + passed_along(far, -2).astype(f32)).astype(bf16)
        got = swapped(near).astype(f32)
        mid = (mid + jnp.where(odd, got, 0.0)).astype(bf16)
        own = own + jnp.where(odd, 0.0, got)
        totals.append((own + passed_along(mid, -2).astype(f32)).astype(bf16))
    key_parts, value_parts = [], []
    for total in totals:
        for head in range(CHUNK):
            start = head * 2 * HEAD_SIZE
            key_parts.append(total[:, start : start + HEAD_SIZE])
            value_parts.append(total[:, start + HEAD_SIZE : start + 2 * HEAD_SIZE])
    return (
        grads[0],
        grads[1],
        jnp.concatenate(key_parts, axis=1),
        jnp.concatenate(value_parts, axis=1),
    )


def solution(mesh):
    spec = P(AXES, None)
    return jax.shard_map(
        local,
        mesh=mesh,
        in_specs=(spec, spec, spec, spec, P()),
        out_specs=(spec, spec, spec, spec),
        check_vma=False,
    )
```

```python
import math

import jax
import jax.numpy as jnp
from jax import lax
from jax.experimental import pallas as pl
from jax.experimental.pallas import tpu as pltpu
from jax.sharding import PartitionSpec as P

HEAD_SIZE = 128
QUERY_HEADS = 32
KEY_VALUE_HEADS = 4
GROUP = QUERY_HEADS // KEY_VALUE_HEADS
SPAN = 4
AXES = ("blk", "inner")
CHUNK = 2
ROWS = 32
UNIT = 2
MASKED = -1e30
SCALE = 1.0 / math.sqrt(HEAD_SIZE)
EXP2_SCALE = SCALE * math.log2(math.e)

NN = (((1,), (0,)), ((), ()))


def dot(a, b, dims=NN):
    return lax.dot_general(a, b, dims, preferred_element_type=jnp.float32)


def device_count():
    return lax.axis_size("blk") * lax.axis_size("inner")


def passed_along(value, steps):
    count = device_count()
    first, last = (max(0, -steps), min(count, count - steps))
    return lax.ppermute(value, AXES, [(source, source + steps) for source in range(first, last)])


def swapped(value):
    return lax.ppermute(value, AXES, [(source, source ^ 1) for source in range(device_count())])


def write_masks(bias_ref, old_ref, cut_ref, lengths_ref, first_ref, rows):
    docs = lengths_ref.shape[0]
    first = first_ref[0]
    row = lax.broadcasted_iota(jnp.int32, (rows, 128), 0)
    query_pos = first + row

    def step(doc, carry):
        end, start = carry
        end = end + lengths_ref[doc]
        return end, jnp.where(query_pos >= end, end, start)

    _, start = lax.fori_loop(0, docs, step, (jnp.int32(0), jnp.zeros((rows, 128), jnp.int32)))
    lane = lax.broadcasted_iota(jnp.int32, (rows, 128), 1)
    old = start < first - (SPAN - 2) * rows
    old_ref[...] = jnp.where(old, 1.0, 0.0)
    cut = jnp.min(jnp.where(old, start - (first - (SPAN - 1) * rows), rows), axis=0, keepdims=True)
    cut_ref[...] = jnp.broadcast_to(cut, cut_ref.shape)
    cut = jnp.broadcast_to(cut, (rows, 128))
    for part in range((SPAN - 1) * rows // 128):
        offset = part * 128 + lane
        if part < rows // 128:
            own = (offset <= row) & ((first + offset >= start) | (old & (offset < cut)))
            allowed = own | (old & (offset >= cut))
        else:
            allowed = first - (SPAN - 1) * rows + offset >= start
        bias_ref[:, part * 128 : (part + 1) * 128] = jnp.where(allowed, 0.0, MASKED)


def attention_kernel(first_ref, lengths_ref, q_ref, g_ref, far_ref, mid_ref, near_ref, own_ref, *refs):
    (
        out_ref, dq_ref, dfar_ref, dmid_ref, dnear_ref, down_ref,
        bias_ref, old_ref, cut_ref,
        key_ref, value_ref, key_t_ref, value_t_ref, key2_ref, value2_ref, key2_t_ref, value2_t_ref,
        dk_ref, dv_ref, dk2_ref, dv2_ref, *slots,
    ) = refs[-34:]
    s_refs, p_refs, dp_refs, d_refs, g_refs, delta_refs = (slots[i : i + 2] for i in range(0, 12, 2))
    (inv_ref,) = slots[12:]
    rows = q_ref.shape[0]
    window = (SPAN - 1) * rows
    units = CHUNK * GROUP // UNIT
    stack = UNIT * rows
    two = slice(0, rows)
    rest = slice(rows, window)

    write_masks(bias_ref, old_ref, cut_ref, lengths_ref, first_ref, rows)
    from_far = lax.broadcasted_iota(jnp.int32, (rows, 2 * HEAD_SIZE), 0) >= cut_ref[0, 0]
    for kv in range(CHUNK):
        pair = slice(kv * 2 * HEAD_SIZE, (kv + 1) * 2 * HEAD_SIZE)
        far, mid, near, own = (ref[:, pair] for ref in (far_ref, mid_ref, near_ref, own_ref))
        for j, block in enumerate((mid, near)):
            span = slice(j * rows, (j + 1) * rows)
            key_ref[kv, span] = block[:, :HEAD_SIZE]
            value_ref[kv, span] = block[:, HEAD_SIZE:]
            key_t_ref[kv, :, span] = block[:, :HEAD_SIZE].T
            value_t_ref[kv, :, span] = block[:, HEAD_SIZE:].T
        mixed = jnp.where(from_far, far.astype(jnp.float32), own.astype(jnp.float32))
        for j, block in enumerate((mixed.astype(jnp.bfloat16), own)):
            span = slice(j * HEAD_SIZE, (j + 1) * HEAD_SIZE)
            key2_ref[kv, :, span] = block[:, :HEAD_SIZE]
            value2_ref[kv, :, span] = block[:, HEAD_SIZE:]
            key2_t_ref[kv, span] = block[:, :HEAD_SIZE].T
            value2_t_ref[kv, span] = block[:, HEAD_SIZE:].T
    for ref in (dk_ref, dv_ref, dk2_ref, dv2_ref, p_refs[1], dp_refs[1], delta_refs[1], g_refs[1]):
        ref[...] = jnp.zeros_like(ref)

    def places(unit):
        return [
            (
                slice(i * rows, (i + 1) * rows),
                pl.ds(pl.multiple_of((unit * UNIT + i) * HEAD_SIZE, HEAD_SIZE), HEAD_SIZE),
            )
            for i in range(UNIT)
        ]

    def stacked(ref, unit):
        return jnp.concatenate([ref[:, cols] for _, cols in places(unit)], axis=0)

    def doubled(x):
        old = jnp.concatenate([old_ref[...].astype(jnp.bfloat16)] * UNIT, axis=0)
        return jnp.concatenate([x * old, x * (1 - old)], axis=1)

    def picked(x):
        old = jnp.concatenate([old_ref[...]] * UNIT, axis=0)
        return jnp.where(old > 0.5, x[:, :HEAD_SIZE], x[:, HEAD_SIZE:])

    def scores(unit, slot):
        kv = unit * UNIT // GROUP
        q = stacked(q_ref, unit)
        s_refs[slot][:, two] = dot(doubled(q), key2_t_ref[kv])
        s_refs[slot][:, rest] = dot(q, key_t_ref[kv])

    def softmax(slot):
        for r in range(0, stack, ROWS):
            here = slice(r, r + ROWS)
            row = slice(r % rows, r % rows + ROWS)
            s = s_refs[slot][here] * EXP2_SCALE + bias_ref[row]
            e = jnp.exp2(s - jnp.max(s, axis=1, keepdims=True))
            inv = 1.0 / jnp.sum(e, axis=1, keepdims=True)
            inv_ref[here] = jnp.broadcast_to(inv, (ROWS, HEAD_SIZE))
            p_refs[slot][here] = e.astype(jnp.bfloat16)

    def mix(unit, slot):
        kv = unit * UNIT // GROUP
        p_ref, g_ref_here = p_refs[slot], g_refs[slot]
        total = picked(dot(p_ref[:, two], value2_ref[kv])) + dot(p_ref[:, rest], value_ref[kv])
        for here, cols in places(unit):
            inv = inv_ref[here]
            out = (total[here] * inv).astype(jnp.bfloat16)
            out_ref[:, cols] = out
            g = g_ref[:, cols].astype(jnp.float32) * inv
            delta = jnp.sum(g * out.astype(jnp.float32), axis=1, keepdims=True)
            delta_refs[slot][here] = jnp.broadcast_to(delta, (rows, HEAD_SIZE))
            g_ref_here[here] = g.astype(jnp.bfloat16)
        g = g_ref_here[...]
        dp_refs[slot][:, two] = dot(doubled(g), value2_t_ref[kv])
        dp_refs[slot][:, rest] = dot(g, value_t_ref[kv])

    def score_grad(slot):
        for r in range(0, stack, ROWS):
            here = slice(r, r + ROWS)
            delta = jnp.concatenate([delta_refs[slot][here]] * (window // HEAD_SIZE), axis=1)
            d_refs[slot][here] = p_refs[slot][here] * (dp_refs[slot][here] - delta).astype(jnp.bfloat16)

    def spread(unit, slot):
        kv = unit * UNIT // GROUP
        p_ref, d_ref = p_refs[slot], d_refs[slot]
        total = picked(dot(d_ref[:, two], key2_ref[kv])) + dot(d_ref[:, rest], key_ref[kv])
        for here, cols in places(unit):
            dq_ref[:, cols] = (total[here] * SCALE).astype(jnp.bfloat16)
        q = stacked(q_ref, unit)
        g = g_refs[slot][...]
        dk2_ref[kv] += dot(doubled(q).T, d_ref[:, two])
        dk_ref[kv] += dot(q.T, d_ref[:, rest])
        dv2_ref[kv] += dot(doubled(g).T, p_ref[:, two])
        dv_ref[kv] += dot(g.T, p_ref[:, rest])

    scores(0, 0)

    def step(index, carry):
        for slot in range(2):
            unit = 2 * index + slot
            scores(jnp.minimum(unit + 1, units - 1), 1 - slot)
            score_grad(1 - slot)
            softmax(slot)
            spread(jnp.maximum(unit - 1, 0), 1 - slot)
            mix(unit, slot)
        return carry

    lax.fori_loop(0, units // 2, step, 0)
    score_grad(1)
    spread(units - 1, 1)
    from_far = from_far[:, :HEAD_SIZE]
    for kv in range(CHUNK):
        for part, grad, grad2, scale in ((0, dk_ref, dk2_ref, SCALE), (1, dv_ref, dv2_ref, 1.0)):
            start = (2 * kv + part) * HEAD_SIZE
            span = slice(start, start + HEAD_SIZE)
            either = grad2[kv, :HEAD_SIZE].T * scale
            own = grad2[kv, HEAD_SIZE:].T * scale
            dfar_ref[:, span] = jnp.where(from_far, either, 0.0).astype(dfar_ref.dtype)
            down_ref[:, span] = own + jnp.where(from_far, 0.0, either)
            dmid_ref[:, span] = grad[kv, :, :rows].T * scale
            dnear_ref[:, span] = grad[kv, :, rows:].T * scale


def attention(chunk, first, lengths, queries, out_grad, blocks, grads):
    rows = queries.shape[0]
    wide = CHUNK * GROUP * HEAD_SIZE
    pair = 2 * HEAD_SIZE
    window = (SPAN - 1) * rows
    query_spec = pl.BlockSpec((rows, wide), lambda i, *_: (0, chunk))
    block_spec = pl.BlockSpec((rows, CHUNK * pair), lambda i, *_: (0, 0))
    operands = [first, lengths, queries, out_grad, *blocks]
    in_specs = [query_spec] * 2 + [block_spec] * 4
    aliases = {}
    for at, array in enumerate(grads):
        if array is not None:
            aliases[len(operands)] = at
            operands.append(array)
            in_specs.append(pl.BlockSpec(memory_space=pl.ANY))
    bf16, f32 = jnp.bfloat16, jnp.float32
    results = pl.pallas_call(
        attention_kernel,
        out_shape=[jax.ShapeDtypeStruct(queries.shape, bf16)] * 2
        + [jax.ShapeDtypeStruct((rows, CHUNK * pair), kind) for kind in (bf16, f32, f32, f32)],
        grid_spec=pltpu.PrefetchScalarGridSpec(
            num_scalar_prefetch=2,
            grid=(1,),
            in_specs=in_specs,
            out_specs=[query_spec] * 2 + [block_spec] * 4,
            scratch_shapes=[
                pltpu.VMEM(shape, kind)
                for shape, kind, count in (
                    ((rows, window), f32, 1),
                    ((rows, HEAD_SIZE), f32, 1),
                    ((8, HEAD_SIZE), jnp.int32, 1),
                    ((CHUNK, 2 * rows, HEAD_SIZE), bf16, 2),
                    ((CHUNK, HEAD_SIZE, 2 * rows), bf16, 2),
                    ((CHUNK, rows, pair), bf16, 2),
                    ((CHUNK, pair, rows), bf16, 2),
                    ((CHUNK, HEAD_SIZE, 2 * rows), f32, 2),
                    ((CHUNK, pair, rows), f32, 2),
                    ((UNIT * rows, window), f32, 2),
                    ((UNIT * rows, window), bf16, 2),
                    ((UNIT * rows, window), f32, 2),
                    ((UNIT * rows, window), bf16, 2),
                    ((UNIT * rows, HEAD_SIZE), bf16, 2),
                    ((UNIT * rows, HEAD_SIZE), f32, 2),
                    ((UNIT * rows, HEAD_SIZE), f32, 1),
                )
                for _ in range(count)
            ],
        ),
        input_output_aliases=aliases,
        compiler_params=pltpu.CompilerParams(vmem_limit_bytes=32 * 1024 * 1024),
        cost_estimate=pl.CostEstimate(
            flops=12 * CHUNK * rows * GROUP * window * HEAD_SIZE * 2,
            bytes_accessed=4 * rows * wide * 2 + CHUNK * 22 * rows * pair,
            transcendentals=0,
        ),
        name="attention",
    )(*operands)
    return results[:2], results[2:]


def local(queries, keys, values, out_grad, doc_lengths):
    rows = queries.shape[0]
    index = lax.axis_index(AXES)
    odd = index % 2 == 1
    first = (index * rows).astype(jnp.int32).reshape(1)
    bf16, f32 = jnp.bfloat16, jnp.float32
    chunks = range(KEY_VALUE_HEADS // CHUNK)
    owns, mids, nears, fars = [], [], [], []
    for chunk in chunks:
        parts = []
        for head in range(chunk * CHUNK, (chunk + 1) * CHUNK):
            span = slice(head * HEAD_SIZE, (head + 1) * HEAD_SIZE)
            parts += [keys[:, span], values[:, span]]
        owns.append(jnp.concatenate(parts, axis=1))
        mids.append(passed_along(owns[chunk], 2))
        nears.append(swapped(jnp.where(odd, mids[chunk], owns[chunk])))
        fars.append(passed_along(nears[chunk], 2))
    grads = (None, None)
    totals = []
    for chunk in chunks:
        blocks = (fars[chunk], mids[chunk], nears[chunk], owns[chunk])
        grads, parts = attention(chunk, first, doc_lengths, queries, out_grad, blocks, grads)
        far, mid, near, own = parts
        near = (near + passed_along(far, -2).astype(f32)).astype(bf16)
        got = swapped(near).astype(f32)
        mid = (mid + jnp.where(odd, got, 0.0)).astype(bf16)
        own = own + jnp.where(odd, 0.0, got)
        totals.append((own + passed_along(mid, -2).astype(f32)).astype(bf16))
    key_parts, value_parts = [], []
    for total in totals:
        for head in range(CHUNK):
            start = head * 2 * HEAD_SIZE
            key_parts.append(total[:, start : start + HEAD_SIZE])
            value_parts.append(total[:, start + HEAD_SIZE : start + 2 * HEAD_SIZE])
    return (
        grads[0],
        grads[1],
        jnp.concatenate(key_parts, axis=1),
        jnp.concatenate(value_parts, axis=1),
    )


def solution(mesh):
    spec = P(AXES, None)
    return jax.shard_map(
        local,
        mesh=mesh,
        in_specs=(spec, spec, spec, spec, P()),
        out_specs=(spec, spec, spec, spec),
        check_vma=False,
    )
```

```python
import math

import jax
import jax.numpy as jnp
from jax import lax
from jax.experimental import pallas as pl
from jax.experimental.pallas import tpu as pltpu
from jax.sharding import PartitionSpec as P

HEAD_SIZE = 128
QUERY_HEADS = 32
KEY_VALUE_HEADS = 4
GROUP = QUERY_HEADS // KEY_VALUE_HEADS
SPAN = 4
AXES = ("blk", "inner")
CHUNK = 1
ROWS = 32
UNIT = 2
FORWARD = ((0,), (1,), (2, 3))
BACKWARD = ((0, 1), (2,), (3,))
MASKED = -1e30
SCALE = 1.0 / math.sqrt(HEAD_SIZE)
EXP2_SCALE = SCALE * math.log2(math.e)

NN = (((1,), (0,)), ((), ()))


def dot(a, b, dims=NN):
    return lax.dot_general(a, b, dims, preferred_element_type=jnp.float32)


def device_count():
    return lax.axis_size("blk") * lax.axis_size("inner")


def passed_along(value, steps):
    count = device_count()
    first, last = (max(0, -steps), min(count, count - steps))
    return lax.ppermute(value, AXES, [(source, source + steps) for source in range(first, last)])


def write_masks(bias_ref, old_ref, cut_ref, lengths_ref, first_ref, rows):
    docs = lengths_ref.shape[0]
    first = first_ref[0]
    row = lax.broadcasted_iota(jnp.int32, (rows, 128), 0)
    query_pos = first + row

    def step(doc, carry):
        end, start = carry
        end = end + lengths_ref[doc]
        return end, jnp.where(query_pos >= end, end, start)

    _, start = lax.fori_loop(0, docs, step, (jnp.int32(0), jnp.zeros((rows, 128), jnp.int32)))
    lane = lax.broadcasted_iota(jnp.int32, (rows, 128), 1)
    old = start < first - (SPAN - 2) * rows
    old_ref[...] = jnp.where(old, 1.0, 0.0)
    cut = jnp.min(jnp.where(old, start - (first - (SPAN - 1) * rows), rows), axis=0, keepdims=True)
    cut_ref[...] = jnp.broadcast_to(cut, cut_ref.shape)
    cut = jnp.broadcast_to(cut, (rows, 128))
    for part in range((SPAN - 1) * rows // 128):
        offset = part * 128 + lane
        if part < rows // 128:
            own = (offset <= row) & ((first + offset >= start) | (old & (offset < cut)))
            allowed = own | (old & (offset >= cut))
        else:
            allowed = first - (SPAN - 1) * rows + offset >= start
        bias_ref[:, part * 128 : (part + 1) * 128] = jnp.where(allowed, 0.0, MASKED)


def attention_kernel(first_ref, lengths_ref, q_ref, g_ref, behind_ref, near_ref, own_ref, *refs):
    (
        out_ref, dq_ref, dbehind_ref, dnear_ref, down_ref,
        bias_ref, old_ref, cut_ref,
        key_ref, value_ref, key_t_ref, value_t_ref, key2_ref, value2_ref, key2_t_ref, value2_t_ref,
        dk_ref, dv_ref, dk2_ref, dv2_ref, *slots,
    ) = refs[-33:]
    s_refs, p_refs, dp_refs, d_refs, g_refs, delta_refs = (slots[i : i + 2] for i in range(0, 12, 2))
    (inv_ref,) = slots[12:]
    rows = q_ref.shape[0]
    window = (SPAN - 1) * rows
    units = CHUNK * GROUP // UNIT
    stack = UNIT * rows
    two = slice(0, rows)
    rest = slice(rows, window)

    write_masks(bias_ref, old_ref, cut_ref, lengths_ref, first_ref, rows)
    from_far = lax.broadcasted_iota(jnp.int32, (rows, 2 * HEAD_SIZE), 0) >= cut_ref[0, 0]
    for kv in range(CHUNK):
        mid, far, near, own = behind_ref[0], behind_ref[1], near_ref[...], own_ref[...]
        for j, block in enumerate((mid, near)):
            span = slice(j * rows, (j + 1) * rows)
            key_ref[kv, span] = block[:, :HEAD_SIZE]
            value_ref[kv, span] = block[:, HEAD_SIZE:]
            key_t_ref[kv, :, span] = block[:, :HEAD_SIZE].T
            value_t_ref[kv, :, span] = block[:, HEAD_SIZE:].T
        mixed = jnp.where(from_far, far.astype(jnp.float32), own.astype(jnp.float32))
        for j, block in enumerate((mixed.astype(jnp.bfloat16), own)):
            span = slice(j * HEAD_SIZE, (j + 1) * HEAD_SIZE)
            key2_ref[kv, :, span] = block[:, :HEAD_SIZE]
            value2_ref[kv, :, span] = block[:, HEAD_SIZE:]
            key2_t_ref[kv, span] = block[:, :HEAD_SIZE].T
            value2_t_ref[kv, span] = block[:, HEAD_SIZE:].T
    for ref in (dk_ref, dv_ref, dk2_ref, dv2_ref, p_refs[1], dp_refs[1], delta_refs[1], g_refs[1]):
        ref[...] = jnp.zeros_like(ref)

    def places(unit):
        return [
            (
                slice(i * rows, (i + 1) * rows),
                pl.ds(pl.multiple_of((unit * UNIT + i) * HEAD_SIZE, HEAD_SIZE), HEAD_SIZE),
            )
            for i in range(UNIT)
        ]

    def stacked(ref, unit):
        return jnp.concatenate([ref[:, cols] for _, cols in places(unit)], axis=0)

    def doubled(x):
        old = jnp.concatenate([old_ref[...].astype(jnp.bfloat16)] * UNIT, axis=0)
        return jnp.concatenate([x * old, x * (1 - old)], axis=1)

    def picked(x):
        old = jnp.concatenate([old_ref[...]] * UNIT, axis=0)
        return jnp.where(old > 0.5, x[:, :HEAD_SIZE], x[:, HEAD_SIZE:])

    def scores(unit, slot):
        kv = unit * UNIT // GROUP
        q = stacked(q_ref, unit)
        s_refs[slot][:, two] = dot(doubled(q), key2_t_ref[kv])
        s_refs[slot][:, rest] = dot(q, key_t_ref[kv])

    def softmax(slot):
        for r in range(0, stack, ROWS):
            here = slice(r, r + ROWS)
            row = slice(r % rows, r % rows + ROWS)
            s = s_refs[slot][here] * EXP2_SCALE + bias_ref[row]
            e = jnp.exp2(s - jnp.max(s, axis=1, keepdims=True))
            inv = 1.0 / jnp.sum(e, axis=1, keepdims=True)
            inv_ref[here] = jnp.broadcast_to(inv, (ROWS, HEAD_SIZE))
            p_refs[slot][here] = e.astype(jnp.bfloat16)

    def mix(unit, slot):
        kv = unit * UNIT // GROUP
        p_ref, g_ref_here = p_refs[slot], g_refs[slot]
        total = picked(dot(p_ref[:, two], value2_ref[kv])) + dot(p_ref[:, rest], value_ref[kv])
        for here, cols in places(unit):
            inv = inv_ref[here]
            out = (total[here] * inv).astype(jnp.bfloat16)
            out_ref[:, cols] = out
            g = g_ref[:, cols].astype(jnp.float32) * inv
            delta = jnp.sum(g * out.astype(jnp.float32), axis=1, keepdims=True)
            delta_refs[slot][here] = jnp.broadcast_to(delta, (rows, HEAD_SIZE))
            g_ref_here[here] = g.astype(jnp.bfloat16)
        g = g_ref_here[...]
        dp_refs[slot][:, two] = dot(doubled(g), value2_t_ref[kv])
        dp_refs[slot][:, rest] = dot(g, value_t_ref[kv])

    def score_grad(slot):
        for r in range(0, stack, ROWS):
            here = slice(r, r + ROWS)
            delta = jnp.concatenate([delta_refs[slot][here]] * (window // HEAD_SIZE), axis=1)
            d_refs[slot][here] = p_refs[slot][here] * (dp_refs[slot][here] - delta).astype(jnp.bfloat16)

    def spread(unit, slot):
        kv = unit * UNIT // GROUP
        p_ref, d_ref = p_refs[slot], d_refs[slot]
        total = picked(dot(d_ref[:, two], key2_ref[kv])) + dot(d_ref[:, rest], key_ref[kv])
        for here, cols in places(unit):
            dq_ref[:, cols] = (total[here] * SCALE).astype(jnp.bfloat16)
        q = stacked(q_ref, unit)
        g = g_refs[slot][...]
        dk2_ref[kv] += dot(doubled(q).T, d_ref[:, two])
        dk_ref[kv] += dot(q.T, d_ref[:, rest])
        dv2_ref[kv] += dot(doubled(g).T, p_ref[:, two])
        dv_ref[kv] += dot(g.T, p_ref[:, rest])

    scores(0, 0)

    def step(index, carry):
        for slot in range(2):
            unit = 2 * index + slot
            scores(jnp.minimum(unit + 1, units - 1), 1 - slot)
            score_grad(1 - slot)
            softmax(slot)
            spread(jnp.maximum(unit - 1, 0), 1 - slot)
            mix(unit, slot)
        return carry

    lax.fori_loop(0, units // 2, step, 0)
    score_grad(1)
    spread(units - 1, 1)
    from_far = from_far[:, :HEAD_SIZE]
    for kv in range(CHUNK):
        for part, grad, grad2, scale in ((0, dk_ref, dk2_ref, SCALE), (1, dv_ref, dv2_ref, 1.0)):
            start = (2 * kv + part) * HEAD_SIZE
            span = slice(start, start + HEAD_SIZE)
            either = grad2[kv, :HEAD_SIZE].T * scale
            own = grad2[kv, HEAD_SIZE:].T * scale
            dbehind_ref[1, :, span] = jnp.where(from_far, either, 0.0).astype(jnp.bfloat16)
            down_ref[:, span] = own + jnp.where(from_far, 0.0, either)
            dbehind_ref[0, :, span] = (grad[kv, :, :rows].T * scale).astype(jnp.bfloat16)
            dnear_ref[:, span] = grad[kv, :, rows:].T * scale


def attention(head, first, lengths, queries, out_grad, blocks, place, grads, parts, back, back_place):
    rows = queries.shape[0]
    wide = GROUP * HEAD_SIZE
    pair = 2 * HEAD_SIZE
    window = (SPAN - 1) * rows
    query_spec = pl.BlockSpec((rows, wide), lambda i, *_: (0, head))

    def pair_specs(at):
        one = pl.BlockSpec((rows, pair), lambda i, *_: (0, at))
        return [pl.BlockSpec((2, rows, pair), lambda i, *_: (0, 0, at)), one, one]

    operands = [first, lengths, queries, out_grad, *blocks]
    in_specs = [query_spec] * 2 + pair_specs(place)
    aliases = {}
    for at, array in enumerate((*grads, *parts)):
        if array is not None:
            aliases[len(operands)] = at
            operands.append(array)
            in_specs.append(pl.BlockSpec(memory_space=pl.ANY))
    bf16, f32 = jnp.bfloat16, jnp.float32
    results = pl.pallas_call(
        attention_kernel,
        out_shape=[
            jax.ShapeDtypeStruct(queries.shape, bf16),
            jax.ShapeDtypeStruct(queries.shape, bf16),
            jax.ShapeDtypeStruct((2, rows, back * pair), bf16),
            jax.ShapeDtypeStruct((rows, back * pair), f32),
            jax.ShapeDtypeStruct((rows, back * pair), f32),
        ],
        grid_spec=pltpu.PrefetchScalarGridSpec(
            num_scalar_prefetch=2,
            grid=(1,),
            in_specs=in_specs,
            out_specs=[query_spec] * 2 + pair_specs(back_place),
            scratch_shapes=[
                pltpu.VMEM(shape, kind)
                for shape, kind, count in (
                    ((rows, window), f32, 1),
                    ((rows, HEAD_SIZE), f32, 1),
                    ((8, HEAD_SIZE), jnp.int32, 1),
                    ((CHUNK, 2 * rows, HEAD_SIZE), bf16, 2),
                    ((CHUNK, HEAD_SIZE, 2 * rows), bf16, 2),
                    ((CHUNK, rows, pair), bf16, 2),
                    ((CHUNK, pair, rows), bf16, 2),
                    ((CHUNK, HEAD_SIZE, 2 * rows), f32, 2),
                    ((CHUNK, pair, rows), f32, 2),
                    ((UNIT * rows, window), f32, 2),
                    ((UNIT * rows, window), bf16, 2),
                    ((UNIT * rows, window), f32, 2),
                    ((UNIT * rows, window), bf16, 2),
                    ((UNIT * rows, HEAD_SIZE), bf16, 2),
                    ((UNIT * rows, HEAD_SIZE), f32, 2),
                    ((UNIT * rows, HEAD_SIZE), f32, 1),
                )
                for _ in range(count)
            ],
        ),
        input_output_aliases=aliases,
        compiler_params=pltpu.CompilerParams(vmem_limit_bytes=32 * 1024 * 1024),
        cost_estimate=pl.CostEstimate(
            flops=12 * CHUNK * rows * GROUP * window * HEAD_SIZE * 2,
            bytes_accessed=4 * rows * wide * 2 + CHUNK * 22 * rows * pair,
            transcendentals=0,
        ),
        name="attention",
    )(*operands)
    return results[:2], results[2:]


def local(queries, keys, values, out_grad, doc_lengths):
    rows = queries.shape[0]
    index = lax.axis_index(AXES)
    first = (index * rows).astype(jnp.int32).reshape(1)
    bf16, f32 = jnp.bfloat16, jnp.float32
    blocks = {}
    owns, nears = [], []
    for heads in FORWARD:
        parts = []
        for head in heads:
            span = slice(head * HEAD_SIZE, (head + 1) * HEAD_SIZE)
            parts += [keys[:, span], values[:, span]]
        owns.append(jnp.concatenate(parts, axis=1))
    for own in owns:
        nears.append(passed_along(own, 1))
    for heads, own, near in zip(FORWARD, owns, nears):
        behind = passed_along(jnp.stack([own, near]), 2)
        for place, head in enumerate(heads):
            blocks[head] = ((behind, near, own), place)
    grads = (None, None)
    totals = []
    for heads in BACKWARD:
        parts = (None,) * 3
        for at, head in enumerate(heads):
            grads, parts = attention(
                head, first, doc_lengths, queries, out_grad, *blocks[head], grads, parts, len(heads), at
            )
        behind, near, own = parts
        got = passed_along(behind, -2).astype(f32)
        last = passed_along((near + got[1]).astype(bf16), -1).astype(f32)
        total = (own + got[0] + last).astype(bf16)
        totals += [total[:, i * HEAD_SIZE : (i + 1) * HEAD_SIZE] for i in range(2 * len(heads))]
    return (
        grads[0],
        grads[1],
        jnp.concatenate(totals[0::2], axis=1),
        jnp.concatenate(totals[1::2], axis=1),
    )


def solution(mesh):
    spec = P(AXES, None)
    return jax.shard_map(
        local,
        mesh=mesh,
        in_specs=(spec, spec, spec, spec, P()),
        out_specs=(spec, spec, spec, spec),
        check_vma=False,
    )
```

```python
import functools
import math

import jax
import jax.numpy as jnp
from jax import lax
from jax.experimental import pallas as pl
from jax.experimental.pallas import tpu as pltpu
from jax.sharding import PartitionSpec as P

HEAD_SIZE = 128
QUERY_HEADS = 32
KEY_VALUE_HEADS = 4
GROUP = QUERY_HEADS // KEY_VALUE_HEADS
SPAN = 4
AXES = ("blk", "inner")
ROWS = 32
UNIT = 4
FORWARD = ((0,), (1,), (2, 3))
BACKWARD = ((0, 1), (2,), (3,))
MASKED = -1e30
SCALE = 1.0 / math.sqrt(HEAD_SIZE)
EXP2_SCALE = SCALE * math.log2(math.e)

NN = (((1,), (0,)), ((), ()))


def dot(a, b, dims=NN):
    return lax.dot_general(a, b, dims, preferred_element_type=jnp.float32)


def device_count():
    return lax.axis_size("blk") * lax.axis_size("inner")


def passed_along(value, steps):
    count = device_count()
    first, last = (max(0, -steps), min(count, count - steps))
    return lax.ppermute(value, AXES, [(source, source + steps) for source in range(first, last)])


def write_masks(bias_ref, old_ref, cut_ref, lengths_ref, first_ref, rows):
    docs = lengths_ref.shape[0]
    first = first_ref[0]
    row = lax.broadcasted_iota(jnp.int32, (rows, 128), 0)
    query_pos = first + row

    def step(doc, carry):
        end, start = carry
        end = end + lengths_ref[doc]
        return end, jnp.where(query_pos >= end, end, start)

    _, start = lax.fori_loop(0, docs, step, (jnp.int32(0), jnp.zeros((rows, 128), jnp.int32)))
    lane = lax.broadcasted_iota(jnp.int32, (rows, 128), 1)
    old = start < first - (SPAN - 2) * rows
    old_ref[...] = jnp.where(old, 1.0, 0.0)
    cut = jnp.min(jnp.where(old, start - (first - (SPAN - 1) * rows), rows), axis=0, keepdims=True)
    cut_ref[...] = jnp.broadcast_to(cut, cut_ref.shape)
    cut = jnp.broadcast_to(cut, (rows, 128))
    for part in range((SPAN - 1) * rows // 128):
        offset = part * 128 + lane
        if part < rows // 128:
            own = (offset <= row) & ((first + offset >= start) | (old & (offset < cut)))
            allowed = own | (old & (offset >= cut))
        else:
            allowed = first - (SPAN - 1) * rows + offset >= start
        bias_ref[:, part * 128 : (part + 1) * 128] = jnp.where(allowed, 0.0, MASKED)


def attention_kernel(places, first_ref, lengths_ref, q_ref, g_ref, behind_ref, near_ref, own_ref, *refs):
    (
        out_ref, dq_ref, dbehind_ref, dnear_ref, down_ref,
        bias_ref, old_ref, cut_ref,
        key_ref, value_ref, key_t_ref, value_t_ref, key2_ref, value2_ref, key2_t_ref, value2_t_ref,
        dk_ref, dv_ref, dk2_ref, dv2_ref, *slots,
    ) = refs[-33:]
    s_refs, p_refs, dp_refs, d_refs, g_refs, delta_refs = (slots[i : i + 2] for i in range(0, 12, 2))
    (inv_ref,) = slots[12:]
    rows = q_ref.shape[0]
    window = (SPAN - 1) * rows
    units = GROUP // UNIT
    key_in, value_in, key_out, value_out = (slice(at, at + HEAD_SIZE) for at in places)
    stack = UNIT * rows
    two = slice(0, rows)
    rest = slice(rows, window)

    write_masks(bias_ref, old_ref, cut_ref, lengths_ref, first_ref, rows)
    from_far = lax.broadcasted_iota(jnp.int32, (rows, HEAD_SIZE), 0) >= cut_ref[0, 0]
    mid, far, near, own = behind_ref.at[0], behind_ref.at[1], near_ref, own_ref
    for j, block in enumerate((mid, near)):
        span = slice(j * rows, (j + 1) * rows)
        key_ref[span] = block[:, key_in]
        value_ref[span] = block[:, value_in]
        key_t_ref[:, span] = block[:, key_in].T
        value_t_ref[:, span] = block[:, value_in].T
    for which, plain_ref, turned_ref in ((key_in, key2_ref, key2_t_ref), (value_in, value2_ref, value2_t_ref)):
        mine = own[:, which]
        either = jnp.where(from_far, far[:, which].astype(jnp.float32), mine.astype(jnp.float32))
        for j, block in enumerate((either.astype(jnp.bfloat16), mine)):
            span = slice(j * HEAD_SIZE, (j + 1) * HEAD_SIZE)
            plain_ref[:, span] = block
            turned_ref[span] = block.T
    for ref in (dk_ref, dv_ref, dk2_ref, dv2_ref):
        ref[...] = jnp.zeros_like(ref)

    def places(unit):
        return [
            (
                slice(i * rows, (i + 1) * rows),
                slice((unit * UNIT + i) * HEAD_SIZE, (unit * UNIT + i + 1) * HEAD_SIZE),
            )
            for i in range(UNIT)
        ]

    def stacked(ref, unit):
        return jnp.concatenate([ref[:, cols] for _, cols in places(unit)], axis=0)

    def doubled(x):
        old = jnp.concatenate([old_ref[...].astype(jnp.bfloat16)] * UNIT, axis=0)
        return jnp.concatenate([x * old, x * (1 - old)], axis=1)

    def picked(x):
        old = jnp.concatenate([old_ref[...]] * UNIT, axis=0)
        return jnp.where(old > 0.5, x[:, :HEAD_SIZE], x[:, HEAD_SIZE:])

    def scores(unit, slot):
        q = stacked(q_ref, unit)
        s_refs[slot][:, two] = dot(doubled(q), key2_t_ref[...])
        s_refs[slot][:, rest] = dot(q, key_t_ref[...])

    def softmax(slot):
        for r in range(0, stack, ROWS):
            here = slice(r, r + ROWS)
            row = slice(r % rows, r % rows + ROWS)
            s = s_refs[slot][here] * EXP2_SCALE + bias_ref[row]
            e = jnp.exp2(s - jnp.max(s, axis=1, keepdims=True))
            inv = 1.0 / jnp.sum(e, axis=1, keepdims=True)
            inv_ref[here] = jnp.broadcast_to(inv, (ROWS, HEAD_SIZE))
            p_refs[slot][here] = e.astype(jnp.bfloat16)

    def mix(unit, slot):
        p_ref, g_ref_here = p_refs[slot], g_refs[slot]
        total = picked(dot(p_ref[:, two], value2_ref[...])) + dot(p_ref[:, rest], value_ref[...])
        for here, cols in places(unit):
            inv = inv_ref[here]
            out = (total[here] * inv).astype(jnp.bfloat16)
            out_ref[:, cols] = out
            g = g_ref[:, cols].astype(jnp.float32) * inv
            delta = jnp.sum(g * out.astype(jnp.float32), axis=1, keepdims=True)
            delta_refs[slot][here] = jnp.broadcast_to(delta, (rows, HEAD_SIZE))
            g_ref_here[here] = g.astype(jnp.bfloat16)
        g = g_ref_here[...]
        dp_refs[slot][:, two] = dot(doubled(g), value2_t_ref[...])
        dp_refs[slot][:, rest] = dot(g, value_t_ref[...])

    def score_grad(slot):
        for r in range(0, stack, ROWS):
            here = slice(r, r + ROWS)
            delta = jnp.concatenate([delta_refs[slot][here]] * (window // HEAD_SIZE), axis=1)
            d_refs[slot][here] = p_refs[slot][here] * (dp_refs[slot][here] - delta).astype(jnp.bfloat16)

    def spread(unit, slot):
        p_ref, d_ref = p_refs[slot], d_refs[slot]
        total = picked(dot(d_ref[:, two], key2_ref[...])) + dot(d_ref[:, rest], key_ref[...])
        for here, cols in places(unit):
            dq_ref[:, cols] = (total[here] * SCALE).astype(jnp.bfloat16)
        q = stacked(q_ref, unit)
        g = g_refs[slot][...]
        dk2_ref[...] += dot(doubled(q).T, d_ref[:, two])
        dk_ref[...] += dot(q.T, d_ref[:, rest])
        dv2_ref[...] += dot(doubled(g).T, p_ref[:, two])
        dv_ref[...] += dot(g.T, p_ref[:, rest])

    scores(0, 0)
    for unit in range(units):
        slot = unit % 2
        if unit + 1 < units:
            scores(unit + 1, 1 - slot)
        if unit > 0:
            score_grad(1 - slot)
        softmax(slot)
        if unit > 0:
            spread(unit - 1, 1 - slot)
        mix(unit, slot)
    score_grad((units - 1) % 2)
    spread(units - 1, (units - 1) % 2)
    for span, grad, grad2, scale in ((key_out, dk_ref, dk2_ref, SCALE), (value_out, dv_ref, dv2_ref, 1.0)):
        either = grad2[:HEAD_SIZE].T * scale
        own = grad2[HEAD_SIZE:].T * scale
        dbehind_ref[0, :, span] = (grad[:, :rows].T * scale).astype(jnp.bfloat16)
        dbehind_ref[1, :, span] = jnp.where(from_far, either, 0.0).astype(jnp.bfloat16)
        dnear_ref[:, span] = grad[:, rows:].T * scale
        down_ref[:, span] = own + jnp.where(from_far, 0.0, either)


def attention(head, first, lengths, queries, out_grad, blocks, place, grads, parts, back, back_place):
    rows = queries.shape[0]
    wide = GROUP * HEAD_SIZE
    pair = 2 * HEAD_SIZE
    window = (SPAN - 1) * rows
    query_spec = pl.BlockSpec((rows, wide), lambda i, *_: (0, head))

    def pair_specs(heads, at):
        one = pl.BlockSpec((rows, heads * pair), lambda i, *_: (0, at))
        return [pl.BlockSpec((2, rows, heads * pair), lambda i, *_: (0, 0, at)), one, one]

    fore = blocks[-1].shape[1] // pair
    places = [at * HEAD_SIZE for at in (place, fore + place, 0, 1)]
    operands = [first, lengths, queries, out_grad, *blocks]
    in_specs = [query_spec] * 2 + pair_specs(fore, 0)
    aliases = {}
    for at, array in enumerate((*grads, *parts)):
        if array is not None:
            aliases[len(operands)] = at
            operands.append(array)
            in_specs.append(pl.BlockSpec(memory_space=pl.ANY))
    bf16, f32 = jnp.bfloat16, jnp.float32
    results = pl.pallas_call(
        functools.partial(attention_kernel, places),
        out_shape=[
            jax.ShapeDtypeStruct(queries.shape, bf16),
            jax.ShapeDtypeStruct(queries.shape, bf16),
            jax.ShapeDtypeStruct((2, rows, back * pair), bf16),
            jax.ShapeDtypeStruct((rows, back * pair), f32),
            jax.ShapeDtypeStruct((rows, back * pair), f32),
        ],
        grid_spec=pltpu.PrefetchScalarGridSpec(
            num_scalar_prefetch=2,
            grid=(1,),
            in_specs=in_specs,
            out_specs=[query_spec] * 2 + pair_specs(1, back_place),
            scratch_shapes=[
                pltpu.VMEM(shape, kind)
                for shape, kind, count in (
                    ((rows, window), f32, 1),
                    ((rows, HEAD_SIZE), f32, 1),
                    ((8, HEAD_SIZE), jnp.int32, 1),
                    ((2 * rows, HEAD_SIZE), bf16, 2),
                    ((HEAD_SIZE, 2 * rows), bf16, 2),
                    ((rows, pair), bf16, 2),
                    ((pair, rows), bf16, 2),
                    ((HEAD_SIZE, 2 * rows), f32, 2),
                    ((pair, rows), f32, 2),
                    ((UNIT * rows, window), f32, 2),
                    ((UNIT * rows, window), bf16, 2),
                    ((UNIT * rows, window), f32, 2),
                    ((UNIT * rows, window), bf16, 2),
                    ((UNIT * rows, HEAD_SIZE), bf16, 2),
                    ((UNIT * rows, HEAD_SIZE), f32, 2),
                    ((UNIT * rows, HEAD_SIZE), f32, 1),
                )
                for _ in range(count)
            ],
        ),
        input_output_aliases=aliases,
        compiler_params=pltpu.CompilerParams(vmem_limit_bytes=48 * 1024 * 1024),
        cost_estimate=pl.CostEstimate(
            flops=12 * rows * GROUP * window * HEAD_SIZE * 2,
            bytes_accessed=4 * rows * wide * 2 + 22 * rows * pair,
            transcendentals=0,
        ),
        name="attention",
    )(*operands)
    return results[:2], results[2:]


def local(queries, keys, values, out_grad, doc_lengths):
    rows = queries.shape[0]
    index = lax.axis_index(AXES)
    first = (index * rows).astype(jnp.int32).reshape(1)
    bf16, f32 = jnp.bfloat16, jnp.float32
    blocks = {}
    owns, nears = [], []
    for heads in FORWARD:
        span = slice(heads[0] * HEAD_SIZE, (heads[-1] + 1) * HEAD_SIZE)
        owns.append(jnp.concatenate([keys[:, span], values[:, span]], axis=1))
    for own in owns:
        nears.append(passed_along(own, 1))
    for heads, own, near in zip(FORWARD, owns, nears):
        behind = passed_along(jnp.stack([own, near]), 2)
        for place, head in enumerate(heads):
            blocks[head] = ((behind, near, own), place)
    grads = (None, None)
    sent = []

    def second(own, near, got):
        got = got.astype(f32)
        return [own + got[0], (near + got[1]).astype(bf16)]

    for heads in BACKWARD:
        parts = (None,) * 3
        for at, head in enumerate(heads):
            (behind, near, own), place = blocks[head]
            if head == KEY_VALUE_HEADS - 1:
                own, *sent[0] = lax.optimization_barrier((own, *sent[0]))
                last = passed_along(sent[0][1], -1)
            grads, parts = attention(
                head, first, doc_lengths, queries, out_grad, (behind, near, own), place, grads, parts, len(heads), at
            )
        behind, near, own = parts
        if heads == BACKWARD[-1]:
            behind, near, last, middle = lax.optimization_barrier((behind, near, last, sent[1][2]))
            sent[1] = [*sent[1][:2], middle]
        sent.append([own, near, passed_along(behind, -2)])
        if len(sent) == 1:
            sent[0] = second(*sent[0])
    rest = [second(*sent[1]), second(*sent[2])]
    own = [sent[0][0], *(piece[0] for piece in rest)]
    near = passed_along(jnp.concatenate([piece[1] for piece in rest], axis=1), -1)
    total = (jnp.concatenate(own, axis=1) + jnp.concatenate([last, near], axis=1).astype(f32)).astype(bf16)
    parts = [total[:, at : at + HEAD_SIZE] for at in range(0, total.shape[1], HEAD_SIZE)]
    key_grads, value_grads = parts[0::2], parts[1::2]
    return (
        grads[0],
        grads[1],
        jnp.concatenate(key_grads, axis=1),
        jnp.concatenate(value_grads, axis=1),
    )


def solution(mesh):
    spec = P(AXES, None)
    return jax.shard_map(
        local,
        mesh=mesh,
        in_specs=(spec, spec, spec, spec, P()),
        out_specs=(spec, spec, spec, spec),
        check_vma=False,
    )
```

```python
import functools
import math

import jax
import jax.numpy as jnp
from jax import lax
from jax.experimental import pallas as pl
from jax.experimental.pallas import tpu as pltpu
from jax.sharding import PartitionSpec as P

HEAD_SIZE = 128
QUERY_HEADS = 32
KEY_VALUE_HEADS = 4
GROUP = QUERY_HEADS // KEY_VALUE_HEADS
SPAN = 4
AXES = ("blk", "inner")
ROWS = 32
UNIT = 4
FORWARD = ((0,), (1,), (2, 3))
OUTS = 5
SCRATCH = 30
MASKED = -1e30
SCALE = 1.0 / math.sqrt(HEAD_SIZE)
EXP2_SCALE = SCALE * math.log2(math.e)

NN = (((1,), (0,)), ((), ()))


def dot(a, b, dims=NN):
    return lax.dot_general(a, b, dims, preferred_element_type=jnp.float32)


def device_count():
    return lax.axis_size("blk") * lax.axis_size("inner")


def passed_along(value, steps):
    count = device_count()
    first, last = (max(0, -steps), min(count, count - steps))
    return lax.ppermute(value, AXES, [(source, source + steps) for source in range(first, last)])


def write_masks(bias_ref, old_ref, cut_ref, lengths_ref, first_ref, rows):
    docs = lengths_ref.shape[0]
    first = first_ref[0]
    row = lax.broadcasted_iota(jnp.int32, (rows, 128), 0)
    query_pos = first + row

    def step(doc, carry):
        end, start = carry
        end = end + lengths_ref[doc]
        return end, jnp.where(query_pos >= end, end, start)

    _, start = lax.fori_loop(0, docs, step, (jnp.int32(0), jnp.zeros((rows, 128), jnp.int32)))
    lane = lax.broadcasted_iota(jnp.int32, (rows, 128), 1)
    old = start < first - (SPAN - 2) * rows
    old_ref[...] = jnp.where(old, 1.0, 0.0)
    cut = jnp.min(jnp.where(old, start - (first - (SPAN - 1) * rows), rows), axis=0, keepdims=True)
    cut_ref[...] = jnp.broadcast_to(cut, cut_ref.shape)
    cut = jnp.broadcast_to(cut, (rows, 128))
    for part in range((SPAN - 1) * rows // 128):
        offset = part * 128 + lane
        if part < rows // 128:
            own = (offset <= row) & ((first + offset >= start) | (old & (offset < cut)))
            allowed = own | (old & (offset >= cut))
        else:
            allowed = first - (SPAN - 1) * rows + offset >= start
        bias_ref[:, part * 128 : (part + 1) * 128] = jnp.where(allowed, 0.0, MASKED)


def attention_kernel(where, leads, first_ref, lengths_ref, q_ref, g_ref, behind_ref, near_ref, own_ref, *refs):
    if not leads:
        bias_ref, old_ref, cut_ref, *refs = refs
    made = 3 if leads else 0
    out_ref, dq_ref, dbehind_ref, dnear_ref, down_ref, *masks = refs[-(OUTS + SCRATCH + made) : -SCRATCH]
    if leads:
        bias_ref, old_ref, cut_ref = masks
    (
        key_ref, value_ref, key_t_ref, value_t_ref, key2_ref, value2_ref, key2_t_ref, value2_t_ref,
        dk_ref, dv_ref, dk2_ref, dv2_ref, *slots,
    ) = refs[-SCRATCH:]
    slots, copies = slots[:13], slots[13:]
    s_refs, p_refs, dp_refs, d_refs, g_refs, delta_refs = (slots[i : i + 2] for i in range(0, 12, 2))
    (inv_ref,) = slots[12:]
    head, *offsets = where
    key_in, value_in, key_out, value_out = (slice(at, at + HEAD_SIZE) for at in offsets)
    q_full_ref, g_full_ref, out_full_ref, dq_full_ref = q_ref, g_ref, out_ref, dq_ref
    q_ref, g_ref, out_ref, dq_ref, sem = copies
    rows, wide = q_ref.shape
    mine = slice(head * wide, (head + 1) * wide)
    q_copy = pltpu.make_async_copy(q_full_ref.at[:, mine], q_ref, sem.at[0])
    g_copy = pltpu.make_async_copy(g_full_ref.at[:, mine], g_ref, sem.at[1])
    q_copy.start()
    g_copy.start()
    window = (SPAN - 1) * rows
    units = GROUP // UNIT
    stack = UNIT * rows
    two = slice(0, rows)
    rest = slice(rows, window)

    if leads:
        write_masks(bias_ref, old_ref, cut_ref, lengths_ref, first_ref, rows)
    from_far = lax.broadcasted_iota(jnp.int32, (rows, HEAD_SIZE), 0) >= cut_ref[0, 0]
    mid, far, near, own = behind_ref.at[0], behind_ref.at[1], near_ref, own_ref
    for j, block in enumerate((mid, near)):
        span = slice(j * rows, (j + 1) * rows)
        key_ref[span] = block[:, key_in]
        value_ref[span] = block[:, value_in]
        key_t_ref[:, span] = block[:, key_in].T
        value_t_ref[:, span] = block[:, value_in].T
    for which, plain_ref, turned_ref in ((key_in, key2_ref, key2_t_ref), (value_in, value2_ref, value2_t_ref)):
        mine = own[:, which]
        either = jnp.where(from_far, far[:, which].astype(jnp.float32), mine.astype(jnp.float32))
        for j, block in enumerate((either.astype(jnp.bfloat16), mine)):
            span = slice(j * HEAD_SIZE, (j + 1) * HEAD_SIZE)
            plain_ref[:, span] = block
            turned_ref[span] = block.T

    def places(unit):
        return [
            (
                slice(i * rows, (i + 1) * rows),
                slice((unit * UNIT + i) * HEAD_SIZE, (unit * UNIT + i + 1) * HEAD_SIZE),
            )
            for i in range(UNIT)
        ]

    def stacked(ref, unit):
        return jnp.concatenate([ref[:, cols] for _, cols in places(unit)], axis=0)

    def doubled(x):
        old = jnp.concatenate([old_ref[...].astype(jnp.bfloat16)] * UNIT, axis=0)
        return jnp.concatenate([x * old, x * (1 - old)], axis=1)

    def picked(x):
        old = jnp.concatenate([old_ref[...]] * UNIT, axis=0)
        return jnp.where(old > 0.5, x[:, :HEAD_SIZE], x[:, HEAD_SIZE:])

    def scores(unit, slot):
        q = stacked(q_ref, unit)
        s_refs[slot][:, two] = dot(doubled(q), key2_t_ref[...])
        s_refs[slot][:, rest] = dot(q, key_t_ref[...])

    def softmax(slot):
        for r in range(0, stack, ROWS):
            here = slice(r, r + ROWS)
            row = slice(r % rows, r % rows + ROWS)
            s = s_refs[slot][here] * EXP2_SCALE + bias_ref[row]
            e = jnp.exp2(s - jnp.max(s, axis=1, keepdims=True))
            inv = 1.0 / jnp.sum(e, axis=1, keepdims=True)
            inv_ref[here] = jnp.broadcast_to(inv, (ROWS, HEAD_SIZE))
            p_refs[slot][here] = e.astype(jnp.bfloat16)

    def mix(unit, slot):
        p_ref, g_ref_here = p_refs[slot], g_refs[slot]
        total = picked(dot(p_ref[:, two], value2_ref[...])) + dot(p_ref[:, rest], value_ref[...])
        for here, cols in places(unit):
            inv = inv_ref[here]
            out = (total[here] * inv).astype(jnp.bfloat16)
            out_ref[:, cols] = out
            g = g_ref[:, cols].astype(jnp.float32) * inv
            delta = jnp.sum(g * out.astype(jnp.float32), axis=1, keepdims=True)
            delta_refs[slot][here] = jnp.broadcast_to(delta, (rows, HEAD_SIZE))
            g_ref_here[here] = g.astype(jnp.bfloat16)
        g = g_ref_here[...]
        dp_refs[slot][:, two] = dot(doubled(g), value2_t_ref[...])
        dp_refs[slot][:, rest] = dot(g, value_t_ref[...])

    def score_grad(slot):
        for r in range(0, stack, ROWS):
            here = slice(r, r + ROWS)
            delta = jnp.concatenate([delta_refs[slot][here]] * (window // HEAD_SIZE), axis=1)
            d_refs[slot][here] = p_refs[slot][here] * (dp_refs[slot][here] - delta).astype(jnp.bfloat16)

    def spread(unit, slot):
        p_ref, d_ref = p_refs[slot], d_refs[slot]
        total = picked(dot(d_ref[:, two], key2_ref[...])) + dot(d_ref[:, rest], key_ref[...])
        for here, cols in places(unit):
            dq_ref[:, cols] = (total[here] * SCALE).astype(jnp.bfloat16)
        q = stacked(q_ref, unit)
        g = g_refs[slot][...]
        for total_ref, left, right in (
            (dk2_ref, doubled(q), d_ref[:, two]),
            (dk_ref, q, d_ref[:, rest]),
            (dv2_ref, doubled(g), p_ref[:, two]),
            (dv_ref, g, p_ref[:, rest]),
        ):
            term = dot(left.T, right)
            total_ref[...] = term if unit == 0 else total_ref[...] + term

    def send(unit, scratch_ref, full_ref, at):
        part = slice(unit * UNIT * HEAD_SIZE, (unit + 1) * UNIT * HEAD_SIZE)
        place = slice(head * wide + part.start, head * wide + part.stop)
        copy = pltpu.make_async_copy(scratch_ref.at[:, part], full_ref.at[:, place], sem.at[at])
        copy.start()
        return copy

    q_copy.wait()
    scores(0, 0)
    sent = []
    for unit in range(units):
        slot = unit % 2
        if unit + 1 < units:
            scores(unit + 1, 1 - slot)
        if unit > 0:
            score_grad(1 - slot)
        softmax(slot)
        if unit > 0:
            spread(unit - 1, 1 - slot)
            sent.append(send(unit - 1, dq_ref, dq_full_ref, 2 + 2 * (unit - 1)))
        if unit == 0:
            g_copy.wait()
        mix(unit, slot)
        sent.append(send(unit, out_ref, out_full_ref, 3 + 2 * unit))
    score_grad((units - 1) % 2)
    spread(units - 1, (units - 1) % 2)
    sent.append(send(units - 1, dq_ref, dq_full_ref, 2 * units))
    for span, grad, grad2, scale in ((key_out, dk_ref, dk2_ref, SCALE), (value_out, dv_ref, dv2_ref, 1.0)):
        either = grad2[:HEAD_SIZE].T * scale
        own = grad2[HEAD_SIZE:].T * scale
        dbehind_ref[0, :, span] = (grad[:, :rows].T * scale).astype(jnp.bfloat16)
        dbehind_ref[1, :, span] = jnp.where(from_far, either, 0.0).astype(jnp.bfloat16)
        dnear_ref[:, span] = grad[:, rows:].T * scale
        down_ref[:, span] = own + jnp.where(from_far, 0.0, either)
    for copy in sent:
        copy.wait()


def attention(head, first, lengths, queries, out_grad, blocks, place, grads, masks):
    rows = queries.shape[0]
    wide = GROUP * HEAD_SIZE
    pair = 2 * HEAD_SIZE
    window = (SPAN - 1) * rows
    leads = masks is None
    query_spec = pl.BlockSpec(memory_space=pl.ANY)

    def whole(shape):
        return pl.BlockSpec(shape, lambda i, *_: (0,) * len(shape))

    mask_shapes = ((rows, window), (rows, HEAD_SIZE), (8, HEAD_SIZE))
    mask_specs = [whole(shape) for shape in mask_shapes]
    fore = blocks[-1].shape[1] // pair
    where = [head, *(at * HEAD_SIZE for at in (place, fore + place, 0, 1))]
    operands = [first, lengths, queries, out_grad, *blocks]
    in_specs = [query_spec] * 2 + [whole(block.shape) for block in blocks]
    aliases = {}
    if not leads:
        operands += masks
        in_specs += mask_specs
    for at, array in enumerate(grads):
        if array is not None:
            aliases[len(operands)] = at
            operands.append(array)
            in_specs.append(pl.BlockSpec(memory_space=pl.ANY))
    bf16, f32 = jnp.bfloat16, jnp.float32
    results = pl.pallas_call(
        functools.partial(attention_kernel, where, leads),
        out_shape=[
            jax.ShapeDtypeStruct(queries.shape, bf16),
            jax.ShapeDtypeStruct(queries.shape, bf16),
            jax.ShapeDtypeStruct((2, rows, pair), bf16),
            jax.ShapeDtypeStruct((rows, pair), f32),
            jax.ShapeDtypeStruct((rows, pair), f32),
        ]
        + [jax.ShapeDtypeStruct(*mask) for mask in zip(mask_shapes, (f32, f32, jnp.int32)) if leads],
        grid_spec=pltpu.PrefetchScalarGridSpec(
            num_scalar_prefetch=2,
            grid=(1,),
            in_specs=in_specs,
            out_specs=[query_spec] * 2
            + [whole((2, rows, pair)), whole((rows, pair)), whole((rows, pair))]
            + (mask_specs if leads else []),
            scratch_shapes=[
                pltpu.VMEM(shape, kind)
                for shape, kind, count in (
                    ((2 * rows, HEAD_SIZE), bf16, 2),
                    ((HEAD_SIZE, 2 * rows), bf16, 2),
                    ((rows, pair), bf16, 2),
                    ((pair, rows), bf16, 2),
                    ((HEAD_SIZE, 2 * rows), f32, 2),
                    ((pair, rows), f32, 2),
                    ((UNIT * rows, window), f32, 2),
                    ((UNIT * rows, window), bf16, 2),
                    ((UNIT * rows, window), f32, 2),
                    ((UNIT * rows, window), bf16, 2),
                    ((UNIT * rows, HEAD_SIZE), bf16, 2),
                    ((UNIT * rows, HEAD_SIZE), f32, 2),
                    ((UNIT * rows, HEAD_SIZE), f32, 1),
                )
                for _ in range(count)
            ]
            + [pltpu.VMEM((rows, wide), bf16)] * 4
            + [pltpu.SemaphoreType.DMA((2 + 2 * GROUP // UNIT,))],
        ),
        input_output_aliases=aliases,
        compiler_params=pltpu.CompilerParams(vmem_limit_bytes=48 * 1024 * 1024),
        cost_estimate=pl.CostEstimate(
            flops=12 * rows * GROUP * window * HEAD_SIZE * 2,
            bytes_accessed=4 * rows * wide * 2 + 22 * rows * pair,
            transcendentals=0,
        ),
        name="attention",
    )(*operands)
    return results[:2], results[2:OUTS], results[OUTS:] if leads else masks


def pack_kernel(keys_ref, values_ref, *out_refs):
    for heads, out_ref in zip(FORWARD, out_refs):
        span = slice(heads[0] * HEAD_SIZE, (heads[-1] + 1) * HEAD_SIZE)
        width = span.stop - span.start
        out_ref[:, :width] = keys_ref[:, span]
        out_ref[:, width:] = values_ref[:, span]


def pack(keys, values):
    rows = keys.shape[0]
    return pl.pallas_call(
        pack_kernel,
        out_shape=[
            jax.ShapeDtypeStruct((rows, 2 * HEAD_SIZE * len(heads)), keys.dtype) for heads in FORWARD
        ],
        name="pack",
    )(keys, values)


def local(queries, keys, values, out_grad, doc_lengths):
    rows = queries.shape[0]
    index = lax.axis_index(AXES)
    first = (index * rows).astype(jnp.int32).reshape(1)
    bf16, f32 = jnp.bfloat16, jnp.float32
    blocks, nears = {}, []
    owns = pack(keys, values)
    for own in owns:
        nears.append(passed_along(own, 1))
    pairs = [jnp.stack([own, near]) for own, near in zip(owns, nears)]
    for heads, own, near, pair in zip(FORWARD, owns, nears, pairs):
        behind = passed_along(pair, 2)
        for place, head in enumerate(heads):
            blocks[head] = ((behind, near, own), place)
    grads, masks = (None, None), None
    parts = []

    def attend(head, after=()):
        nonlocal grads, masks
        (behind, near, own), place = blocks[head]
        own, *after = lax.optimization_barrier((own, *after))
        grads, part, masks = attention(
            head, first, doc_lengths, queries, out_grad, (behind, near, own), place, grads, masks
        )
        parts.append(part)
        return after

    def first_hop(head):
        behind, near, own = parts[head]
        return near, own, passed_along(behind, -2)

    def second_hop(near, own, got):
        got = got.astype(f32)
        return (near + got[1]).astype(bf16), own + got[0]

    attend(0, pairs)
    zero = first_hop(0)
    attend(1)
    one = first_hop(1)
    attend(2)
    two = first_hop(2)
    got, _ = lax.optimization_barrier((one[2], parts[2][0]))
    nears, owns = zip(second_hop(*zero), second_hop(*one[:2], got))
    nears = jnp.concatenate(nears, axis=1)
    (nears,) = attend(3, (nears,))
    early = passed_along(nears, -1)
    behind, near, own = parts[3]
    behind, near, own, early, got = lax.optimization_barrier((behind, near, own, early, two[2]))
    far = passed_along(behind[1], -3)
    mid = passed_along(behind[0], -2)
    near_two, own_two = second_hop(two[0], two[1], got)
    late = passed_along(jnp.concatenate([near_two, near.astype(bf16)], axis=1), -1)
    own = own + mid.astype(f32) + far.astype(f32)
    total = jnp.concatenate([*owns, own_two, own], axis=1)
    total = (total + jnp.concatenate([early, late], axis=1).astype(f32)).astype(bf16)
    columns = [total[:, at : at + HEAD_SIZE] for at in range(0, total.shape[1], HEAD_SIZE)]
    return (
        grads[0],
        grads[1],
        jnp.concatenate(columns[0::2], axis=1),
        jnp.concatenate(columns[1::2], axis=1),
    )


def solution(mesh):
    spec = P(AXES, None)
    return jax.shard_map(
        local,
        mesh=mesh,
        in_specs=(spec, spec, spec, spec, P()),
        out_specs=(spec, spec, spec, spec),
        check_vma=False,
    )
```

```python
import functools
import math

import jax
import jax.numpy as jnp
from jax import lax
from jax.experimental import pallas as pl
from jax.experimental.pallas import tpu as pltpu
from jax.sharding import PartitionSpec as P

HEAD_SIZE = 128
QUERY_HEADS = 32
KEY_VALUE_HEADS = 4
GROUP = QUERY_HEADS // KEY_VALUE_HEADS
SPAN = 4
AXES = ("blk", "inner")
ROWS = 32
UNIT = 4
FORWARD = ((0,), (1,), (2, 3))
OUTS = 5
SCRATCH = 32
MASKED = -1e30
SCALE = 1.0 / math.sqrt(HEAD_SIZE)
EXP2_SCALE = SCALE * math.log2(math.e)

NN = (((1,), (0,)), ((), ()))


def dot(a, b, dims=NN):
    return lax.dot_general(a, b, dims, preferred_element_type=jnp.float32)


def device_count():
    return lax.axis_size("blk") * lax.axis_size("inner")


def passed_along(value, steps):
    count = device_count()
    first, last = (max(0, -steps), min(count, count - steps))
    return lax.ppermute(value, AXES, [(source, source + steps) for source in range(first, last)])


def next_group(value):
    groups, inner = lax.axis_size("blk"), lax.axis_size("inner")
    pairs = [
        (group * inner + place, (group + 1) * inner + place)
        for group in range(groups - 1)
        for place in range(SPAN - 1)
    ]
    return lax.ppermute(value, AXES, pairs)


def write_masks(bias_ref, old_ref, cut_ref, lengths_ref, first_ref, rows):
    docs = lengths_ref.shape[0]
    first = first_ref[0]
    row = lax.broadcasted_iota(jnp.int32, (rows, 128), 0)
    query_pos = first + row

    def step(doc, carry):
        end, start = carry
        end = end + lengths_ref[doc]
        return end, jnp.where(query_pos >= end, end, start)

    _, start = lax.fori_loop(0, docs, step, (jnp.int32(0), jnp.zeros((rows, 128), jnp.int32)))
    lane = lax.broadcasted_iota(jnp.int32, (rows, 128), 1)
    old = start < first - (SPAN - 2) * rows
    old_ref[...] = jnp.where(old, 1.0, 0.0)
    cut = jnp.min(jnp.where(old, start - (first - (SPAN - 1) * rows), rows), axis=0, keepdims=True)
    cut_ref[...] = jnp.broadcast_to(cut, cut_ref.shape)
    cut = jnp.broadcast_to(cut, (rows, 128))
    for part in range((SPAN - 1) * rows // 128):
        offset = part * 128 + lane
        if part < rows // 128:
            own = (offset <= row) & ((first + offset >= start) | (old & (offset < cut)))
            allowed = own | (old & (offset >= cut))
        else:
            allowed = first - (SPAN - 1) * rows + offset >= start
        bias_ref[:, part * 128 : (part + 1) * 128] = jnp.where(allowed, 0.0, MASKED)


def attention_kernel(where, leads, first_ref, inner_ref, lengths_ref, q_ref, g_ref, halo_ref, wrap_ref, own_ref, *refs):
    if not leads:
        bias_ref, old_ref, cut_ref, *refs = refs
    made = 3 if leads else 0
    out_ref, dq_ref, dbehind_ref, dnear_ref, down_ref, *masks = refs[-(OUTS + SCRATCH + made) : -SCRATCH]
    if leads:
        bias_ref, old_ref, cut_ref = masks
    (
        key_ref, value_ref, key_t_ref, value_t_ref, key2_ref, value2_ref, key2_t_ref, value2_t_ref,
        dk_ref, dv_ref, dk2_ref, dv2_ref, *slots,
    ) = refs[-SCRATCH:]
    slots, copies = slots[:13], slots[13:]
    s_refs, p_refs, dp_refs, d_refs, g_refs, delta_refs = (slots[i : i + 2] for i in range(0, 12, 2))
    (inv_ref,) = slots[12:]
    head, *offsets = where
    key_in, value_in, key_out, value_out = (slice(at, at + HEAD_SIZE) for at in offsets)
    q_full_ref, g_full_ref, out_full_ref, dq_full_ref = q_ref, g_ref, out_ref, dq_ref
    q_ref, g_ref, out_ref, dq_ref, before_ref, sem, before_sem = copies
    rows, wide = q_ref.shape
    mine = slice(head * wide, (head + 1) * wide)
    q_copy = pltpu.make_async_copy(q_full_ref.at[:, mine], q_ref, sem.at[0])
    g_copy = pltpu.make_async_copy(g_full_ref.at[:, mine], g_ref, sem.at[1])
    inner = inner_ref[0]
    before_copies = []
    for back in range(1, SPAN):
        for part, cols in enumerate((key_in, value_in)):
            target = before_ref.at[back - 1, :, part * HEAD_SIZE : (part + 1) * HEAD_SIZE]
            signal = before_sem.at[2 * (back - 1) + part]
            here = pltpu.make_async_copy(halo_ref.at[jnp.maximum(inner - back, 0), :, cols], target, signal)
            there = pltpu.make_async_copy(
                wrap_ref.at[jnp.minimum(inner - back + SPAN - 1, SPAN - 2), :, cols], target, signal
            )
            pl.when(inner >= back)(here.start)
            pl.when(inner < back)(there.start)
            before_copies.append(here)
    q_copy.start()
    g_copy.start()
    window = (SPAN - 1) * rows
    units = GROUP // UNIT
    stack = UNIT * rows
    two = slice(0, rows)
    rest = slice(rows, window)

    if leads:
        write_masks(bias_ref, old_ref, cut_ref, lengths_ref, first_ref, rows)
    from_far = lax.broadcasted_iota(jnp.int32, (rows, HEAD_SIZE), 0) >= cut_ref[0, 0]
    for copy in before_copies:
        copy.wait()
    near, mid, far = (before_ref.at[back] for back in range(SPAN - 1))
    for j, block in enumerate((mid, near)):
        span = slice(j * rows, (j + 1) * rows)
        key_ref[span] = block[:, :HEAD_SIZE]
        value_ref[span] = block[:, HEAD_SIZE:]
        key_t_ref[:, span] = block[:, :HEAD_SIZE].T
        value_t_ref[:, span] = block[:, HEAD_SIZE:].T
    for part, which, plain_ref, turned_ref in (
        (slice(0, HEAD_SIZE), key_in, key2_ref, key2_t_ref),
        (slice(HEAD_SIZE, 2 * HEAD_SIZE), value_in, value2_ref, value2_t_ref),
    ):
        mine = own_ref[:, which]
        either = jnp.where(from_far, far[:, part].astype(jnp.float32), mine.astype(jnp.float32))
        for j, block in enumerate((either.astype(jnp.bfloat16), mine)):
            span = slice(j * HEAD_SIZE, (j + 1) * HEAD_SIZE)
            plain_ref[:, span] = block
            turned_ref[span] = block.T

    def places(unit):
        return [
            (
                slice(i * rows, (i + 1) * rows),
                slice((unit * UNIT + i) * HEAD_SIZE, (unit * UNIT + i + 1) * HEAD_SIZE),
            )
            for i in range(UNIT)
        ]

    def stacked(ref, unit):
        return jnp.concatenate([ref[:, cols] for _, cols in places(unit)], axis=0)

    def doubled(x):
        old = jnp.concatenate([old_ref[...].astype(jnp.bfloat16)] * UNIT, axis=0)
        return jnp.concatenate([x * old, x * (1 - old)], axis=1)

    def picked(x):
        old = jnp.concatenate([old_ref[...]] * UNIT, axis=0)
        return jnp.where(old > 0.5, x[:, :HEAD_SIZE], x[:, HEAD_SIZE:])

    def scores(unit, slot):
        q = stacked(q_ref, unit)
        s_refs[slot][:, two] = dot(doubled(q), key2_t_ref[...])
        s_refs[slot][:, rest] = dot(q, key_t_ref[...])

    def softmax(slot):
        for r in range(0, stack, ROWS):
            here = slice(r, r + ROWS)
            row = slice(r % rows, r % rows + ROWS)
            s = s_refs[slot][here] * EXP2_SCALE + bias_ref[row]
            e = jnp.exp2(s - jnp.max(s, axis=1, keepdims=True))
            inv = 1.0 / jnp.sum(e, axis=1, keepdims=True)
            inv_ref[here] = jnp.broadcast_to(inv, (ROWS, HEAD_SIZE))
            p_refs[slot][here] = e.astype(jnp.bfloat16)

    def mix(unit, slot):
        p_ref, g_ref_here = p_refs[slot], g_refs[slot]
        total = picked(dot(p_ref[:, two], value2_ref[...])) + dot(p_ref[:, rest], value_ref[...])
        for here, cols in places(unit):
            inv = inv_ref[here]
            out = (total[here] * inv).astype(jnp.bfloat16)
            out_ref[:, cols] = out
            g = g_ref[:, cols].astype(jnp.float32) * inv
            delta = jnp.sum(g * out.astype(jnp.float32), axis=1, keepdims=True)
            delta_refs[slot][here] = jnp.broadcast_to(delta, (rows, HEAD_SIZE))
            g_ref_here[here] = g.astype(jnp.bfloat16)
        g = g_ref_here[...]
        dp_refs[slot][:, two] = dot(doubled(g), value2_t_ref[...])
        dp_refs[slot][:, rest] = dot(g, value_t_ref[...])

    def score_grad(slot):
        for r in range(0, stack, ROWS):
            here = slice(r, r + ROWS)
            delta = jnp.concatenate([delta_refs[slot][here]] * (window // HEAD_SIZE), axis=1)
            d_refs[slot][here] = p_refs[slot][here] * (dp_refs[slot][here] - delta).astype(jnp.bfloat16)

    def spread(unit, slot):
        p_ref, d_ref = p_refs[slot], d_refs[slot]
        total = picked(dot(d_ref[:, two], key2_ref[...])) + dot(d_ref[:, rest], key_ref[...])
        for here, cols in places(unit):
            dq_ref[:, cols] = (total[here] * SCALE).astype(jnp.bfloat16)
        q = stacked(q_ref, unit)
        g = g_refs[slot][...]
        for total_ref, left, right in (
            (dk2_ref, doubled(q), d_ref[:, two]),
            (dk_ref, q, d_ref[:, rest]),
            (dv2_ref, doubled(g), p_ref[:, two]),
            (dv_ref, g, p_ref[:, rest]),
        ):
            term = dot(left.T, right)
            total_ref[...] = term if unit == 0 else total_ref[...] + term

    def send(unit, scratch_ref, full_ref, at):
        part = slice(unit * UNIT * HEAD_SIZE, (unit + 1) * UNIT * HEAD_SIZE)
        place = slice(head * wide + part.start, head * wide + part.stop)
        copy = pltpu.make_async_copy(scratch_ref.at[:, part], full_ref.at[:, place], sem.at[at])
        copy.start()
        return copy

    q_copy.wait()
    scores(0, 0)
    sent = []
    for unit in range(units):
        slot = unit % 2
        if unit + 1 < units:
            scores(unit + 1, 1 - slot)
        if unit > 0:
            score_grad(1 - slot)
        softmax(slot)
        if unit > 0:
            spread(unit - 1, 1 - slot)
            sent.append(send(unit - 1, dq_ref, dq_full_ref, 2 + 2 * (unit - 1)))
        if unit == 0:
            g_copy.wait()
        mix(unit, slot)
        sent.append(send(unit, out_ref, out_full_ref, 3 + 2 * unit))
    score_grad((units - 1) % 2)
    spread(units - 1, (units - 1) % 2)
    sent.append(send(units - 1, dq_ref, dq_full_ref, 2 * units))
    for span, grad, grad2, scale in ((key_out, dk_ref, dk2_ref, SCALE), (value_out, dv_ref, dv2_ref, 1.0)):
        either = grad2[:HEAD_SIZE].T * scale
        own = grad2[HEAD_SIZE:].T * scale
        dbehind_ref[0, :, span] = (grad[:, :rows].T * scale).astype(jnp.bfloat16)
        dbehind_ref[1, :, span] = jnp.where(from_far, either, 0.0).astype(jnp.bfloat16)
        dnear_ref[:, span] = grad[:, rows:].T * scale
        down_ref[:, span] = own + jnp.where(from_far, 0.0, either)
    for copy in sent:
        copy.wait()


def attention(head, first, inner, lengths, queries, out_grad, blocks, place, grads, masks):
    rows = queries.shape[0]
    wide = GROUP * HEAD_SIZE
    pair = 2 * HEAD_SIZE
    window = (SPAN - 1) * rows
    leads = masks is None
    query_spec = pl.BlockSpec(memory_space=pl.ANY)

    def whole(shape):
        return pl.BlockSpec(shape, lambda i, *_: (0,) * len(shape))

    mask_shapes = ((rows, window), (rows, HEAD_SIZE), (8, HEAD_SIZE))
    mask_specs = [whole(shape) for shape in mask_shapes]
    fore = blocks[-1].shape[1] // pair
    where = [head, *(at * HEAD_SIZE for at in (place, fore + place, 0, 1))]
    operands = [first, inner, lengths, queries, out_grad, *blocks]
    in_specs = [query_spec] * 4 + [whole(blocks[-1].shape)]
    aliases = {}
    if not leads:
        operands += masks
        in_specs += mask_specs
    for at, array in enumerate(grads):
        if array is not None:
            aliases[len(operands)] = at
            operands.append(array)
            in_specs.append(pl.BlockSpec(memory_space=pl.ANY))
    bf16, f32 = jnp.bfloat16, jnp.float32
    results = pl.pallas_call(
        functools.partial(attention_kernel, where, leads),
        out_shape=[
            jax.ShapeDtypeStruct(queries.shape, bf16),
            jax.ShapeDtypeStruct(queries.shape, bf16),
            jax.ShapeDtypeStruct((2, rows, pair), bf16),
            jax.ShapeDtypeStruct((rows, pair), f32),
            jax.ShapeDtypeStruct((rows, pair), f32),
        ]
        + [jax.ShapeDtypeStruct(*mask) for mask in zip(mask_shapes, (f32, f32, jnp.int32)) if leads],
        grid_spec=pltpu.PrefetchScalarGridSpec(
            num_scalar_prefetch=3,
            grid=(1,),
            in_specs=in_specs,
            out_specs=[query_spec] * 2
            + [whole((2, rows, pair)), whole((rows, pair)), whole((rows, pair))]
            + (mask_specs if leads else []),
            scratch_shapes=[
                pltpu.VMEM(shape, kind)
                for shape, kind, count in (
                    ((2 * rows, HEAD_SIZE), bf16, 2),
                    ((HEAD_SIZE, 2 * rows), bf16, 2),
                    ((rows, pair), bf16, 2),
                    ((pair, rows), bf16, 2),
                    ((HEAD_SIZE, 2 * rows), f32, 2),
                    ((pair, rows), f32, 2),
                    ((UNIT * rows, window), f32, 2),
                    ((UNIT * rows, window), bf16, 2),
                    ((UNIT * rows, window), f32, 2),
                    ((UNIT * rows, window), bf16, 2),
                    ((UNIT * rows, HEAD_SIZE), bf16, 2),
                    ((UNIT * rows, HEAD_SIZE), f32, 2),
                    ((UNIT * rows, HEAD_SIZE), f32, 1),
                )
                for _ in range(count)
            ]
            + [pltpu.VMEM((rows, wide), bf16)] * 4
            + [
                pltpu.VMEM((SPAN - 1, rows, pair), bf16),
                pltpu.SemaphoreType.DMA((2 + 2 * GROUP // UNIT,)),
                pltpu.SemaphoreType.DMA((2 * (SPAN - 1),)),
            ],
        ),
        input_output_aliases=aliases,
        compiler_params=pltpu.CompilerParams(vmem_limit_bytes=48 * 1024 * 1024),
        cost_estimate=pl.CostEstimate(
            flops=12 * rows * GROUP * window * HEAD_SIZE * 2,
            bytes_accessed=4 * rows * wide * 2 + 22 * rows * pair,
            transcendentals=0,
        ),
        name="attention",
    )(*operands)
    return results[:2], results[2:OUTS], results[OUTS:] if leads else masks


def pack_kernel(keys_ref, values_ref, *out_refs):
    for heads, out_ref in zip(FORWARD, out_refs):
        span = slice(heads[0] * HEAD_SIZE, (heads[-1] + 1) * HEAD_SIZE)
        width = span.stop - span.start
        out_ref[:, :width] = keys_ref[:, span]
        out_ref[:, width:] = values_ref[:, span]


def pack(keys, values):
    rows = keys.shape[0]
    return pl.pallas_call(
        pack_kernel,
        out_shape=[
            jax.ShapeDtypeStruct((rows, 2 * HEAD_SIZE * len(heads)), keys.dtype) for heads in FORWARD
        ],
        name="pack",
    )(keys, values)


def local(queries, keys, values, out_grad, doc_lengths):
    rows = queries.shape[0]
    index = lax.axis_index(AXES)
    first = (index * rows).astype(jnp.int32).reshape(1)
    bf16, f32 = jnp.bfloat16, jnp.float32
    inner = lax.axis_index("inner").astype(jnp.int32).reshape(1)
    blocks = {}
    owns = pack(keys, values)
    for heads, own in zip(FORWARD, owns):
        halo = lax.all_gather(own, "inner")
        wrap = next_group(halo[1 - SPAN :])
        for place, head in enumerate(heads):
            blocks[head] = ((halo, wrap, own), place)
    grads, masks = (None, None), None
    parts = []

    def attend(head, after=()):
        nonlocal grads, masks
        (halo, wrap, own), place = blocks[head]
        own, *after = lax.optimization_barrier((own, *after))
        grads, part, masks = attention(
            head, first, inner, doc_lengths, queries, out_grad, (halo, wrap, own), place, grads, masks
        )
        parts.append(part)
        return after

    def first_hop(head):
        behind, near, own = parts[head]
        return near, own, passed_along(behind, -2)

    def second_hop(near, own, got):
        got = got.astype(f32)
        return (near + got[1]).astype(bf16), own + got[0]

    attend(0)
    zero = first_hop(0)
    attend(1)
    one = first_hop(1)
    attend(2)
    two = first_hop(2)
    got, _ = lax.optimization_barrier((one[2], parts[2][0]))
    nears, owns = zip(second_hop(*zero), second_hop(*one[:2], got))
    nears = jnp.concatenate(nears, axis=1)
    (nears,) = attend(3, (nears,))
    early = passed_along(nears, -1)
    behind, near, own = parts[3]
    behind, near, own, got = lax.optimization_barrier((behind, near, own, two[2]))
    far = passed_along(behind[1], -3)
    mid = passed_along(behind[0], -2)
    near_two, own_two = second_hop(two[0], two[1], got)
    late = passed_along(jnp.concatenate([near_two, near.astype(bf16)], axis=1), -1)
    own = own + mid.astype(f32) + far.astype(f32)
    total = jnp.concatenate([*owns, own_two, own], axis=1)
    total = (total + jnp.concatenate([early, late], axis=1).astype(f32)).astype(bf16)
    columns = [total[:, at : at + HEAD_SIZE] for at in range(0, total.shape[1], HEAD_SIZE)]
    return (
        grads[0],
        grads[1],
        jnp.concatenate(columns[0::2], axis=1),
        jnp.concatenate(columns[1::2], axis=1),
    )


def solution(mesh):
    spec = P(AXES, None)
    return jax.shard_map(
        local,
        mesh=mesh,
        in_specs=(spec, spec, spec, spec, P()),
        out_specs=(spec, spec, spec, spec),
        check_vma=False,
    )
```

```python
import functools
import math

import jax
import jax.numpy as jnp
from jax import lax
from jax.experimental import pallas as pl
from jax.experimental.pallas import tpu as pltpu
from jax.sharding import PartitionSpec as P

HEAD_SIZE = 128
QUERY_HEADS = 32
KEY_VALUE_HEADS = 4
GROUP = QUERY_HEADS // KEY_VALUE_HEADS
SPAN = 4
AXES = ("blk", "inner")
ROWS = 32
UNIT = 4
FORWARD = ((0,), (1,), (2, 3))
OUTS = 5
SCRATCH = 30
MASKED = -1e30
SCALE = 1.0 / math.sqrt(HEAD_SIZE)
EXP2_SCALE = SCALE * math.log2(math.e)

NN = (((1,), (0,)), ((), ()))


def dot(a, b, dims=NN):
    return lax.dot_general(a, b, dims, preferred_element_type=jnp.float32)


def device_count():
    return lax.axis_size("blk") * lax.axis_size("inner")


def passed_along(value, steps):
    count = device_count()
    first, last = (max(0, -steps), min(count, count - steps))
    return lax.ppermute(value, AXES, [(source, source + steps) for source in range(first, last)])


def write_masks(bias_ref, old_ref, cut_ref, lengths_ref, first_ref, rows):
    docs = lengths_ref.shape[0]
    first = first_ref[0]
    row = lax.broadcasted_iota(jnp.int32, (rows, 128), 0)
    query_pos = first + row

    def step(doc, carry):
        end, start = carry
        end = end + lengths_ref[doc]
        return end, jnp.where(query_pos >= end, end, start)

    _, start = lax.fori_loop(0, docs, step, (jnp.int32(0), jnp.zeros((rows, 128), jnp.int32)))
    lane = lax.broadcasted_iota(jnp.int32, (rows, 128), 1)
    old = start < first - (SPAN - 2) * rows
    old_ref[...] = jnp.where(old, 1.0, 0.0)
    cut = jnp.min(jnp.where(old, start - (first - (SPAN - 1) * rows), rows), axis=0, keepdims=True)
    cut_ref[...] = jnp.broadcast_to(cut, cut_ref.shape)
    cut = jnp.broadcast_to(cut, (rows, 128))
    for part in range((SPAN - 1) * rows // 128):
        offset = part * 128 + lane
        if part < rows // 128:
            own = (offset <= row) & ((first + offset >= start) | (old & (offset < cut)))
            allowed = own | (old & (offset >= cut))
        else:
            allowed = first - (SPAN - 1) * rows + offset >= start
        bias_ref[:, part * 128 : (part + 1) * 128] = jnp.where(allowed, 0.0, MASKED)


def attention_kernel(where, leads, first_ref, lengths_ref, q_ref, g_ref, behind_ref, near_ref, own_ref, *refs):
    if not leads:
        bias_ref, old_ref, cut_ref, *refs = refs
    made = 3 if leads else 0
    out_ref, dq_ref, dbehind_ref, dnear_ref, down_ref, *masks = refs[-(OUTS + SCRATCH + made) : -SCRATCH]
    if leads:
        bias_ref, old_ref, cut_ref = masks
    (
        key_ref, value_ref, key_t_ref, value_t_ref, key2_ref, value2_ref, key2_t_ref, value2_t_ref,
        dk_ref, dv_ref, dk2_ref, dv2_ref, *slots,
    ) = refs[-SCRATCH:]
    slots, copies = slots[:13], slots[13:]
    s_refs, p_refs, dp_refs, d_refs, g_refs, delta_refs = (slots[i : i + 2] for i in range(0, 12, 2))
    (inv_ref,) = slots[12:]
    head, *offsets = where
    key_in, value_in, key_out, value_out = (slice(at, at + HEAD_SIZE) for at in offsets)
    q_full_ref, g_full_ref, out_full_ref, dq_full_ref = q_ref, g_ref, out_ref, dq_ref
    q_ref, g_ref, out_ref, dq_ref, sem = copies
    rows, wide = q_ref.shape
    mine = slice(head * wide, (head + 1) * wide)
    q_copy = pltpu.make_async_copy(q_full_ref.at[:, mine], q_ref, sem.at[0])
    g_copy = pltpu.make_async_copy(g_full_ref.at[:, mine], g_ref, sem.at[1])
    q_copy.start()
    g_copy.start()
    window = (SPAN - 1) * rows
    units = GROUP // UNIT
    stack = UNIT * rows
    two = slice(0, rows)
    rest = slice(rows, window)

    if leads:
        write_masks(bias_ref, old_ref, cut_ref, lengths_ref, first_ref, rows)
    from_far = lax.broadcasted_iota(jnp.int32, (rows, HEAD_SIZE), 0) >= cut_ref[0, 0]
    mid, far, near, own = behind_ref.at[0], behind_ref.at[1], near_ref, own_ref
    for j, block in enumerate((mid, near)):
        span = slice(j * rows, (j + 1) * rows)
        key_ref[span] = block[:, key_in]
        value_ref[span] = block[:, value_in]
        key_t_ref[:, span] = block[:, key_in].T
        value_t_ref[:, span] = block[:, value_in].T
    for which, plain_ref, turned_ref in ((key_in, key2_ref, key2_t_ref), (value_in, value2_ref, value2_t_ref)):
        mine = own[:, which]
        either = jnp.where(from_far, far[:, which].astype(jnp.float32), mine.astype(jnp.float32))
        for j, block in enumerate((either.astype(jnp.bfloat16), mine)):
            span = slice(j * HEAD_SIZE, (j + 1) * HEAD_SIZE)
            plain_ref[:, span] = block
            turned_ref[span] = block.T

    def places(unit):
        return [
            (
                slice(i * rows, (i + 1) * rows),
                slice((unit * UNIT + i) * HEAD_SIZE, (unit * UNIT + i + 1) * HEAD_SIZE),
            )
            for i in range(UNIT)
        ]

    def stacked(ref, unit):
        return jnp.concatenate([ref[:, cols] for _, cols in places(unit)], axis=0)

    def doubled(x):
        old = jnp.concatenate([old_ref[...].astype(jnp.bfloat16)] * UNIT, axis=0)
        return jnp.concatenate([x * old, x * (1 - old)], axis=1)

    def picked(x):
        old = jnp.concatenate([old_ref[...]] * UNIT, axis=0)
        return jnp.where(old > 0.5, x[:, :HEAD_SIZE], x[:, HEAD_SIZE:])

    def scores(unit, slot):
        q = stacked(q_ref, unit)
        s_refs[slot][:, two] = dot(doubled(q), key2_t_ref[...])
        s_refs[slot][:, rest] = dot(q, key_t_ref[...])

    def softmax(slot):
        for r in range(0, stack, ROWS):
            here = slice(r, r + ROWS)
            row = slice(r % rows, r % rows + ROWS)
            s = s_refs[slot][here] * EXP2_SCALE + bias_ref[row]
            e = jnp.exp2(s - jnp.max(s, axis=1, keepdims=True))
            inv = 1.0 / jnp.sum(e, axis=1, keepdims=True)
            inv_ref[here] = jnp.broadcast_to(inv, (ROWS, HEAD_SIZE))
            p_refs[slot][here] = e.astype(jnp.bfloat16)

    def mix(unit, slot):
        p_ref, g_ref_here = p_refs[slot], g_refs[slot]
        total = picked(dot(p_ref[:, two], value2_ref[...])) + dot(p_ref[:, rest], value_ref[...])
        for here, cols in places(unit):
            inv = inv_ref[here]
            out = (total[here] * inv).astype(jnp.bfloat16)
            out_ref[:, cols] = out
            g = g_ref[:, cols].astype(jnp.float32) * inv
            delta = jnp.sum(g * out.astype(jnp.float32), axis=1, keepdims=True)
            delta_refs[slot][here] = jnp.broadcast_to(delta, (rows, HEAD_SIZE))
            g_ref_here[here] = g.astype(jnp.bfloat16)
        g = g_ref_here[...]
        dp_refs[slot][:, two] = dot(doubled(g), value2_t_ref[...])
        dp_refs[slot][:, rest] = dot(g, value_t_ref[...])

    def score_grad(slot):
        for r in range(0, stack, ROWS):
            here = slice(r, r + ROWS)
            delta = jnp.concatenate([delta_refs[slot][here]] * (window // HEAD_SIZE), axis=1)
            d_refs[slot][here] = p_refs[slot][here] * (dp_refs[slot][here] - delta).astype(jnp.bfloat16)

    def spread(unit, slot):
        p_ref, d_ref = p_refs[slot], d_refs[slot]
        total = picked(dot(d_ref[:, two], key2_ref[...])) + dot(d_ref[:, rest], key_ref[...])
        for here, cols in places(unit):
            dq_ref[:, cols] = (total[here] * SCALE).astype(jnp.bfloat16)
        q = stacked(q_ref, unit)
        g = g_refs[slot][...]
        for total_ref, left, right in (
            (dk2_ref, doubled(q), d_ref[:, two]),
            (dk_ref, q, d_ref[:, rest]),
            (dv2_ref, doubled(g), p_ref[:, two]),
            (dv_ref, g, p_ref[:, rest]),
        ):
            term = dot(left.T, right)
            total_ref[...] = term if unit == 0 else total_ref[...] + term

    def send(unit, scratch_ref, full_ref, at):
        part = slice(unit * UNIT * HEAD_SIZE, (unit + 1) * UNIT * HEAD_SIZE)
        place = slice(head * wide + part.start, head * wide + part.stop)
        copy = pltpu.make_async_copy(scratch_ref.at[:, part], full_ref.at[:, place], sem.at[at])
        copy.start()
        return copy

    q_copy.wait()
    scores(0, 0)
    sent = []
    for unit in range(units):
        slot = unit % 2
        if unit + 1 < units:
            scores(unit + 1, 1 - slot)
        if unit > 0:
            score_grad(1 - slot)
        softmax(slot)
        if unit > 0:
            spread(unit - 1, 1 - slot)
            sent.append(send(unit - 1, dq_ref, dq_full_ref, 2 + 2 * (unit - 1)))
        if unit == 0:
            g_copy.wait()
        mix(unit, slot)
        sent.append(send(unit, out_ref, out_full_ref, 3 + 2 * unit))
    score_grad((units - 1) % 2)
    spread(units - 1, (units - 1) % 2)
    sent.append(send(units - 1, dq_ref, dq_full_ref, 2 * units))
    for span, grad, grad2, scale in ((key_out, dk_ref, dk2_ref, SCALE), (value_out, dv_ref, dv2_ref, 1.0)):
        either = grad2[:HEAD_SIZE].T * scale
        own = grad2[HEAD_SIZE:].T * scale
        dbehind_ref[0, :, span] = (grad[:, :rows].T * scale).astype(jnp.bfloat16)
        dbehind_ref[1, :, span] = jnp.where(from_far, either, 0.0).astype(jnp.bfloat16)
        dnear_ref[:, span] = grad[:, rows:].T * scale
        down_ref[:, span] = own + jnp.where(from_far, 0.0, either)
    for copy in sent:
        copy.wait()


def attention(head, first, lengths, queries, out_grad, blocks, place, grads, masks):
    rows = queries.shape[0]
    wide = GROUP * HEAD_SIZE
    pair = 2 * HEAD_SIZE
    window = (SPAN - 1) * rows
    leads = masks is None
    query_spec = pl.BlockSpec(memory_space=pl.ANY)

    def whole(shape):
        return pl.BlockSpec(shape, lambda i, *_: (0,) * len(shape))

    mask_shapes = ((rows, window), (rows, HEAD_SIZE), (8, HEAD_SIZE))
    mask_specs = [whole(shape) for shape in mask_shapes]
    fore = blocks[-1].shape[1] // pair
    where = [head, *(at * HEAD_SIZE for at in (place, fore + place, 0, 1))]
    operands = [first, lengths, queries, out_grad, *blocks]
    in_specs = [query_spec] * 2 + [whole(block.shape) for block in blocks]
    aliases = {}
    if not leads:
        operands += masks
        in_specs += mask_specs
    for at, array in enumerate(grads):
        if array is not None:
            aliases[len(operands)] = at
            operands.append(array)
            in_specs.append(pl.BlockSpec(memory_space=pl.ANY))
    bf16, f32 = jnp.bfloat16, jnp.float32
    results = pl.pallas_call(
        functools.partial(attention_kernel, where, leads),
        out_shape=[
            jax.ShapeDtypeStruct(queries.shape, bf16),
            jax.ShapeDtypeStruct(queries.shape, bf16),
            jax.ShapeDtypeStruct((2, rows, pair), bf16),
            jax.ShapeDtypeStruct((rows, pair), f32),
            jax.ShapeDtypeStruct((rows, pair), f32),
        ]
        + [jax.ShapeDtypeStruct(*mask) for mask in zip(mask_shapes, (f32, f32, jnp.int32)) if leads],
        grid_spec=pltpu.PrefetchScalarGridSpec(
            num_scalar_prefetch=2,
            grid=(1,),
            in_specs=in_specs,
            out_specs=[query_spec] * 2
            + [whole((2, rows, pair)), whole((rows, pair)), whole((rows, pair))]
            + (mask_specs if leads else []),
            scratch_shapes=[
                pltpu.VMEM(shape, kind)
                for shape, kind, count in (
                    ((2 * rows, HEAD_SIZE), bf16, 2),
                    ((HEAD_SIZE, 2 * rows), bf16, 2),
                    ((rows, pair), bf16, 2),
                    ((pair, rows), bf16, 2),
                    ((HEAD_SIZE, 2 * rows), f32, 2),
                    ((pair, rows), f32, 2),
                    ((UNIT * rows, window), f32, 2),
                    ((UNIT * rows, window), bf16, 2),
                    ((UNIT * rows, window), f32, 2),
                    ((UNIT * rows, window), bf16, 2),
                    ((UNIT * rows, HEAD_SIZE), bf16, 2),
                    ((UNIT * rows, HEAD_SIZE), f32, 2),
                    ((UNIT * rows, HEAD_SIZE), f32, 1),
                )
                for _ in range(count)
            ]
            + [pltpu.VMEM((rows, wide), bf16)] * 4
            + [pltpu.SemaphoreType.DMA((2 + 2 * GROUP // UNIT,))],
        ),
        input_output_aliases=aliases,
        compiler_params=pltpu.CompilerParams(vmem_limit_bytes=48 * 1024 * 1024),
        cost_estimate=pl.CostEstimate(
            flops=12 * rows * GROUP * window * HEAD_SIZE * 2,
            bytes_accessed=4 * rows * wide * 2 + 22 * rows * pair,
            transcendentals=0,
        ),
        name="attention",
    )(*operands)
    return results[:2], results[2:OUTS], results[OUTS:] if leads else masks


def pack_kernel(keys_ref, values_ref, *refs):
    sem = refs[-1]
    copies = []
    for at, heads in enumerate(FORWARD):
        span = slice(heads[0] * HEAD_SIZE, (heads[-1] + 1) * HEAD_SIZE)
        width = span.stop - span.start
        own_ref, pair_ref = refs[2 * at : 2 * at + 2]
        for target_ref in (own_ref, pair_ref.at[0]):
            for source_ref, cols in ((keys_ref, slice(0, width)), (values_ref, slice(width, 2 * width))):
                signal = sem.at[len(copies)]
                copies.append(pltpu.make_async_copy(source_ref.at[:, span], target_ref.at[:, cols], signal))
                copies[-1].start()
    for copy in copies:
        copy.wait()


def pack(keys, values):
    rows = keys.shape[0]
    shapes = []
    for heads in FORWARD:
        own = (rows, 2 * HEAD_SIZE * len(heads))
        shapes += [jax.ShapeDtypeStruct(own, keys.dtype), jax.ShapeDtypeStruct((2, *own), keys.dtype)]
    results = pl.pallas_call(
        pack_kernel,
        out_shape=shapes,
        in_specs=[pl.BlockSpec(memory_space=pl.ANY)] * 2,
        out_specs=[pl.BlockSpec(memory_space=pl.ANY)] * len(shapes),
        scratch_shapes=[pltpu.SemaphoreType.DMA((2 * len(shapes),))],
        name="pack",
    )(keys, values)
    return results[0::2], results[1::2]


def local(queries, keys, values, out_grad, doc_lengths):
    rows = queries.shape[0]
    index = lax.axis_index(AXES)
    first = (index * rows).astype(jnp.int32).reshape(1)
    bf16, f32 = jnp.bfloat16, jnp.float32
    blocks, nears = {}, []
    owns, pairs = pack(keys, values)
    for own in owns:
        nears.append(passed_along(own, 1))
    pairs = [pair.at[1].set(near) for pair, near in zip(pairs, nears)]
    for heads, own, near, pair in zip(FORWARD, owns, nears, pairs):
        behind = passed_along(pair, 2)
        for place, head in enumerate(heads):
            blocks[head] = ((behind, near, own), place)
    grads, masks = (None, None), None
    parts = []

    def attend(head, after=()):
        nonlocal grads, masks
        (behind, near, own), place = blocks[head]
        own, *after = lax.optimization_barrier((own, *after))
        grads, part, masks = attention(
            head, first, doc_lengths, queries, out_grad, (behind, near, own), place, grads, masks
        )
        parts.append(part)
        return after

    def second_hop(near, own, got):
        got = got.astype(f32)
        return (near + got[1]).astype(bf16), own + got[0]

    attend(0, pairs)
    attend(1)
    got_early = passed_along(jnp.concatenate([parts[0][0], parts[1][0]], axis=2), -2)
    attend(2)
    got_two = passed_along(parts[2][0], -2)
    attend(3)
    behind, near, own = parts[3]
    behind, near, own, got_early, got_two = lax.optimization_barrier((behind, near, own, got_early, got_two))
    far = passed_along(behind[1], -3)
    mid = passed_along(behind[0], -2)
    pair = 2 * HEAD_SIZE
    ready = [
        second_hop(*parts[0][1:], got_early[:, :, :pair]),
        second_hop(*parts[1][1:], got_early[:, :, pair:]),
        second_hop(*parts[2][1:], got_two),
        (near.astype(bf16), own + mid.astype(f32) + far.astype(f32)),
    ]
    nears, owns = ([piece[at] for piece in ready] for at in range(2))
    last = passed_along(jnp.concatenate(nears, axis=1), -1)
    total = (jnp.concatenate(owns, axis=1) + last.astype(f32)).astype(bf16)
    columns = [total[:, at : at + HEAD_SIZE] for at in range(0, total.shape[1], HEAD_SIZE)]
    return (
        grads[0],
        grads[1],
        jnp.concatenate(columns[0::2], axis=1),
        jnp.concatenate(columns[1::2], axis=1),
    )


def solution(mesh):
    spec = P(AXES, None)
    return jax.shard_map(
        local,
        mesh=mesh,
        in_specs=(spec, spec, spec, spec, P()),
        out_specs=(spec, spec, spec, spec),
        check_vma=False,
    )
```

```python
import functools
import math

import jax
import jax.numpy as jnp
from jax import lax
from jax.experimental import pallas as pl
from jax.experimental.pallas import tpu as pltpu
from jax.sharding import PartitionSpec as P

HEAD_SIZE = 128
QUERY_HEADS = 32
KEY_VALUE_HEADS = 4
GROUP = QUERY_HEADS // KEY_VALUE_HEADS
SPAN = 4
AXES = ("blk", "inner")
ROWS = 32
UNIT = 4
FORWARD = ((0,), (1,), (2, 3))
OUTS = 5
SCRATCH = 30
MASKED = -1e30
SCALE = 1.0 / math.sqrt(HEAD_SIZE)
EXP2_SCALE = SCALE * math.log2(math.e)

NN = (((1,), (0,)), ((), ()))


def dot(a, b, dims=NN):
    return lax.dot_general(a, b, dims, preferred_element_type=jnp.float32)


def device_count():
    return lax.axis_size("blk") * lax.axis_size("inner")


def passed_along(value, steps):
    count = device_count()
    first, last = (max(0, -steps), min(count, count - steps))
    return lax.ppermute(value, AXES, [(source, source + steps) for source in range(first, last)])


def write_masks(bias_ref, old_ref, cut_ref, lengths_ref, first_ref, rows):
    docs = lengths_ref.shape[0]
    first = first_ref[0]
    row = lax.broadcasted_iota(jnp.int32, (rows, 128), 0)
    query_pos = first + row

    def step(doc, carry):
        end, start = carry
        end = end + lengths_ref[doc]
        return end, jnp.where(query_pos >= end, end, start)

    _, start = lax.fori_loop(0, docs, step, (jnp.int32(0), jnp.zeros((rows, 128), jnp.int32)))
    lane = lax.broadcasted_iota(jnp.int32, (rows, 128), 1)
    old = start < first - (SPAN - 2) * rows
    old_ref[...] = jnp.where(old, 1.0, 0.0)
    cut = jnp.min(jnp.where(old, start - (first - (SPAN - 1) * rows), rows), axis=0, keepdims=True)
    cut_ref[...] = jnp.broadcast_to(cut, cut_ref.shape)
    cut = jnp.broadcast_to(cut, (rows, 128))
    for part in range((SPAN - 1) * rows // 128):
        offset = part * 128 + lane
        if part < rows // 128:
            own = (offset <= row) & ((first + offset >= start) | (old & (offset < cut)))
            allowed = own | (old & (offset >= cut))
        else:
            allowed = first - (SPAN - 1) * rows + offset >= start
        bias_ref[:, part * 128 : (part + 1) * 128] = jnp.where(allowed, 0.0, MASKED)


def attention_kernel(where, leads, first_ref, lengths_ref, q_ref, g_ref, behind_ref, near_ref, own_ref, *refs):
    if not leads:
        bias_ref, old_ref, cut_ref, *refs = refs
    made = 3 if leads else 0
    out_ref, dq_ref, dbehind_ref, dnear_ref, down_ref, *masks = refs[-(OUTS + SCRATCH + made) : -SCRATCH]
    if leads:
        bias_ref, old_ref, cut_ref = masks
    (
        key_ref, value_ref, key_t_ref, value_t_ref, key2_ref, value2_ref, key2_t_ref, value2_t_ref,
        dk_ref, dv_ref, dk2_ref, dv2_ref, *slots,
    ) = refs[-SCRATCH:]
    slots, copies = slots[:13], slots[13:]
    s_refs, p_refs, dp_refs, d_refs, g_refs, delta_refs = (slots[i : i + 2] for i in range(0, 12, 2))
    (inv_ref,) = slots[12:]
    head, *offsets = where
    key_in, value_in, key_out, value_out = (slice(at, at + HEAD_SIZE) for at in offsets)
    q_full_ref, g_full_ref, out_full_ref, dq_full_ref = q_ref, g_ref, out_ref, dq_ref
    q_ref, g_ref, out_ref, dq_ref, sem = copies
    rows, wide = q_ref.shape
    mine = slice(head * wide, (head + 1) * wide)
    q_copy = pltpu.make_async_copy(q_full_ref.at[:, mine], q_ref, sem.at[0])
    g_copy = pltpu.make_async_copy(g_full_ref.at[:, mine], g_ref, sem.at[1])
    q_copy.start()
    g_copy.start()
    window = (SPAN - 1) * rows
    units = GROUP // UNIT
    stack = UNIT * rows
    two = slice(0, rows)
    rest = slice(rows, window)

    if leads:
        write_masks(bias_ref, old_ref, cut_ref, lengths_ref, first_ref, rows)
    from_far = lax.broadcasted_iota(jnp.int32, (rows, HEAD_SIZE), 0) >= cut_ref[0, 0]
    mid, far, near, own = behind_ref.at[0], behind_ref.at[1], near_ref, own_ref
    for j, block in enumerate((mid, near)):
        span = slice(j * rows, (j + 1) * rows)
        key_ref[span] = block[:, key_in]
        value_ref[span] = block[:, value_in]
        key_t_ref[:, span] = block[:, key_in].T
        value_t_ref[:, span] = block[:, value_in].T
    for which, plain_ref, turned_ref in ((key_in, key2_ref, key2_t_ref), (value_in, value2_ref, value2_t_ref)):
        mine = own[:, which]
        either = jnp.where(from_far, far[:, which].astype(jnp.float32), mine.astype(jnp.float32))
        for j, block in enumerate((either.astype(jnp.bfloat16), mine)):
            span = slice(j * HEAD_SIZE, (j + 1) * HEAD_SIZE)
            plain_ref[:, span] = block
            turned_ref[span] = block.T

    def places(unit):
        return [
            (
                slice(i * rows, (i + 1) * rows),
                slice((unit * UNIT + i) * HEAD_SIZE, (unit * UNIT + i + 1) * HEAD_SIZE),
            )
            for i in range(UNIT)
        ]

    def stacked(ref, unit):
        return jnp.concatenate([ref[:, cols] for _, cols in places(unit)], axis=0)

    def doubled(x):
        old = jnp.concatenate([old_ref[...].astype(jnp.bfloat16)] * UNIT, axis=0)
        return jnp.concatenate([x * old, x * (1 - old)], axis=1)

    def picked(x):
        old = jnp.concatenate([old_ref[...]] * UNIT, axis=0)
        return jnp.where(old > 0.5, x[:, :HEAD_SIZE], x[:, HEAD_SIZE:])

    def scores(unit, slot):
        q = stacked(q_ref, unit)
        s_refs[slot][:, two] = dot(doubled(q), key2_t_ref[...])
        s_refs[slot][:, rest] = dot(q, key_t_ref[...])

    def softmax(slot):
        for r in range(0, stack, ROWS):
            here = slice(r, r + ROWS)
            row = slice(r % rows, r % rows + ROWS)
            s = s_refs[slot][here] * EXP2_SCALE + bias_ref[row]
            e = jnp.exp2(s - jnp.max(s, axis=1, keepdims=True))
            inv = 1.0 / jnp.sum(e, axis=1, keepdims=True)
            inv_ref[here] = jnp.broadcast_to(inv, (ROWS, HEAD_SIZE))
            p_refs[slot][here] = e.astype(jnp.bfloat16)

    def mix(unit, slot):
        p_ref, g_ref_here = p_refs[slot], g_refs[slot]
        total = picked(dot(p_ref[:, two], value2_ref[...])) + dot(p_ref[:, rest], value_ref[...])
        for here, cols in places(unit):
            inv = inv_ref[here]
            out = (total[here] * inv).astype(jnp.bfloat16)
            out_ref[:, cols] = out
            g = g_ref[:, cols].astype(jnp.float32) * inv
            delta = jnp.sum(g * out.astype(jnp.float32), axis=1, keepdims=True)
            delta_refs[slot][here] = jnp.broadcast_to(delta, (rows, HEAD_SIZE))
            g_ref_here[here] = g.astype(jnp.bfloat16)
        g = g_ref_here[...]
        dp_refs[slot][:, two] = dot(doubled(g), value2_t_ref[...])
        dp_refs[slot][:, rest] = dot(g, value_t_ref[...])

    def score_grad(slot):
        for r in range(0, stack, ROWS):
            here = slice(r, r + ROWS)
            delta = jnp.concatenate([delta_refs[slot][here]] * (window // HEAD_SIZE), axis=1)
            d_refs[slot][here] = p_refs[slot][here] * (dp_refs[slot][here] - delta).astype(jnp.bfloat16)

    def spread(unit, slot):
        p_ref, d_ref = p_refs[slot], d_refs[slot]
        total = picked(dot(d_ref[:, two], key2_ref[...])) + dot(d_ref[:, rest], key_ref[...])
        for here, cols in places(unit):
            dq_ref[:, cols] = (total[here] * SCALE).astype(jnp.bfloat16)
        q = stacked(q_ref, unit)
        g = g_refs[slot][...]
        for total_ref, left, right in (
            (dk2_ref, doubled(q), d_ref[:, two]),
            (dk_ref, q, d_ref[:, rest]),
            (dv2_ref, doubled(g), p_ref[:, two]),
            (dv_ref, g, p_ref[:, rest]),
        ):
            term = dot(left.T, right)
            total_ref[...] = term if unit == 0 else total_ref[...] + term

    def send(unit, scratch_ref, full_ref, at):
        part = slice(unit * UNIT * HEAD_SIZE, (unit + 1) * UNIT * HEAD_SIZE)
        place = slice(head * wide + part.start, head * wide + part.stop)
        copy = pltpu.make_async_copy(scratch_ref.at[:, part], full_ref.at[:, place], sem.at[at])
        copy.start()
        return copy

    q_copy.wait()
    scores(0, 0)
    sent = []
    for unit in range(units):
        slot = unit % 2
        if unit + 1 < units:
            scores(unit + 1, 1 - slot)
        if unit > 0:
            score_grad(1 - slot)
        softmax(slot)
        if unit > 0:
            spread(unit - 1, 1 - slot)
            sent.append(send(unit - 1, dq_ref, dq_full_ref, 2 + 2 * (unit - 1)))
        if unit == 0:
            g_copy.wait()
        mix(unit, slot)
        sent.append(send(unit, out_ref, out_full_ref, 3 + 2 * unit))
    score_grad((units - 1) % 2)
    spread(units - 1, (units - 1) % 2)
    sent.append(send(units - 1, dq_ref, dq_full_ref, 2 * units))
    for span, grad, grad2, scale in ((key_out, dk_ref, dk2_ref, SCALE), (value_out, dv_ref, dv2_ref, 1.0)):
        either = grad2[:HEAD_SIZE].T * scale
        own = grad2[HEAD_SIZE:].T * scale
        dbehind_ref[0, :, span] = (grad[:, :rows].T * scale).astype(jnp.bfloat16)
        dbehind_ref[1, :, span] = jnp.where(from_far, either, 0.0).astype(jnp.bfloat16)
        dnear_ref[:, span] = grad[:, rows:].T * scale
        down_ref[:, span] = own + jnp.where(from_far, 0.0, either)
    for copy in sent:
        copy.wait()


def attention(head, first, lengths, queries, out_grad, blocks, place, grads, masks):
    rows = queries.shape[0]
    wide = GROUP * HEAD_SIZE
    pair = 2 * HEAD_SIZE
    window = (SPAN - 1) * rows
    leads = masks is None
    query_spec = pl.BlockSpec(memory_space=pl.ANY)

    def whole(shape):
        return pl.BlockSpec(shape, lambda i, *_: (0,) * len(shape))

    mask_shapes = ((rows, window), (rows, HEAD_SIZE), (8, HEAD_SIZE))
    mask_specs = [whole(shape) for shape in mask_shapes]
    fore = blocks[-1].shape[1] // pair
    where = [head, *(at * HEAD_SIZE for at in (place, fore + place, 0, 1))]
    operands = [first, lengths, queries, out_grad, *blocks]
    in_specs = [query_spec] * 2 + [whole(block.shape) for block in blocks]
    aliases = {}
    if not leads:
        operands += masks
        in_specs += mask_specs
    for at, array in enumerate(grads):
        if array is not None:
            aliases[len(operands)] = at
            operands.append(array)
            in_specs.append(pl.BlockSpec(memory_space=pl.ANY))
    bf16, f32 = jnp.bfloat16, jnp.float32
    results = pl.pallas_call(
        functools.partial(attention_kernel, where, leads),
        out_shape=[
            jax.ShapeDtypeStruct(queries.shape, bf16),
            jax.ShapeDtypeStruct(queries.shape, bf16),
            jax.ShapeDtypeStruct((2, rows, pair), bf16),
            jax.ShapeDtypeStruct((rows, pair), f32),
            jax.ShapeDtypeStruct((rows, pair), f32),
        ]
        + [jax.ShapeDtypeStruct(*mask) for mask in zip(mask_shapes, (f32, f32, jnp.int32)) if leads],
        grid_spec=pltpu.PrefetchScalarGridSpec(
            num_scalar_prefetch=2,
            grid=(1,),
            in_specs=in_specs,
            out_specs=[query_spec] * 2
            + [whole((2, rows, pair)), whole((rows, pair)), whole((rows, pair))]
            + (mask_specs if leads else []),
            scratch_shapes=[
                pltpu.VMEM(shape, kind)
                for shape, kind, count in (
                    ((2 * rows, HEAD_SIZE), bf16, 2),
                    ((HEAD_SIZE, 2 * rows), bf16, 2),
                    ((rows, pair), bf16, 2),
                    ((pair, rows), bf16, 2),
                    ((HEAD_SIZE, 2 * rows), f32, 2),
                    ((pair, rows), f32, 2),
                    ((UNIT * rows, window), f32, 2),
                    ((UNIT * rows, window), bf16, 2),
                    ((UNIT * rows, window), f32, 2),
                    ((UNIT * rows, window), bf16, 2),
                    ((UNIT * rows, HEAD_SIZE), bf16, 2),
                    ((UNIT * rows, HEAD_SIZE), f32, 2),
                    ((UNIT * rows, HEAD_SIZE), f32, 1),
                )
                for _ in range(count)
            ]
            + [pltpu.VMEM((rows, wide), bf16)] * 4
            + [pltpu.SemaphoreType.DMA((2 + 2 * GROUP // UNIT,))],
        ),
        input_output_aliases=aliases,
        compiler_params=pltpu.CompilerParams(vmem_limit_bytes=48 * 1024 * 1024),
        cost_estimate=pl.CostEstimate(
            flops=12 * rows * GROUP * window * HEAD_SIZE * 2,
            bytes_accessed=4 * rows * wide * 2 + 22 * rows * pair,
            transcendentals=0,
        ),
        name="attention",
    )(*operands)
    return results[:2], results[2:OUTS], results[OUTS:] if leads else masks


def pack_kernel(keys_ref, values_ref, *refs):
    for at, heads in enumerate(FORWARD):
        span = slice(heads[0] * HEAD_SIZE, (heads[-1] + 1) * HEAD_SIZE)
        width = span.stop - span.start
        own_ref, pair_ref = refs[2 * at : 2 * at + 2]
        for target_ref in (own_ref, pair_ref.at[0]):
            target_ref[:, :width] = keys_ref[:, span]
            target_ref[:, width:] = values_ref[:, span]


def pack(keys, values):
    rows = keys.shape[0]
    shapes, specs = [], []
    for heads in FORWARD:
        own = (rows, 2 * HEAD_SIZE * len(heads))
        shapes += [jax.ShapeDtypeStruct(own, keys.dtype), jax.ShapeDtypeStruct((2, *own), keys.dtype)]
        specs += [pl.BlockSpec(own, lambda i: (0, 0)), pl.BlockSpec((1, *own), lambda i: (0, 0, 0))]
    results = pl.pallas_call(
        pack_kernel,
        grid=(1,),
        out_shape=shapes,
        in_specs=[pl.BlockSpec(keys.shape, lambda i: (0, 0))] * 2,
        out_specs=specs,
        name="pack",
    )(keys, values)
    return results[0::2], results[1::2]


def local(queries, keys, values, out_grad, doc_lengths):
    rows = queries.shape[0]
    index = lax.axis_index(AXES)
    first = (index * rows).astype(jnp.int32).reshape(1)
    bf16, f32 = jnp.bfloat16, jnp.float32
    blocks, nears = {}, []
    owns, pairs = pack(keys, values)
    for own in owns:
        nears.append(passed_along(own, 1))
    pairs = [pair.at[1].set(near) for pair, near in zip(pairs, nears)]
    for heads, own, near, pair in zip(FORWARD, owns, nears, pairs):
        behind = passed_along(pair, 2)
        for place, head in enumerate(heads):
            blocks[head] = ((behind, near, own), place)
    grads, masks = (None, None), None
    parts = []

    def attend(head, after=()):
        nonlocal grads, masks
        (behind, near, own), place = blocks[head]
        own, *after = lax.optimization_barrier((own, *after))
        grads, part, masks = attention(
            head, first, doc_lengths, queries, out_grad, (behind, near, own), place, grads, masks
        )
        parts.append(list(part))
        return after

    def second_hop(near, own, got):
        got = got.astype(f32)
        return (near + got[1]).astype(bf16), own + got[0]

    attend(0, pairs)
    gots = [passed_along(parts[0][0], -2)]
    attend(1)
    gots.append(passed_along(parts[1][0], -2))
    gots[0], _ = lax.optimization_barrier((gots[0], parts[1][0]))
    nears, owns = zip(second_hop(*parts[0][1:], gots[0]))
    (nears,) = attend(2, nears)
    gots.append(passed_along(parts[2][0], -2))
    gots[1], _ = lax.optimization_barrier((gots[1], parts[2][0]))
    more = second_hop(*parts[1][1:], gots[1])
    (nears, *more) = attend(3, (nears, *more))
    gots[2], near = lax.optimization_barrier((gots[2], parts[3][1]))
    gots.append(passed_along(parts[3][0], -2))
    parts[3][1] = near
    rest = [second_hop(*part[1:], got) for part, got in zip(parts[2:], gots[2:])]
    nears, owns = zip((nears, *owns), more, *rest)
    last = [passed_along(jnp.concatenate(nears[at : at + 2], axis=1), -1) for at in (0, 2)]
    total = (jnp.concatenate(owns, axis=1) + jnp.concatenate(last, axis=1).astype(f32)).astype(bf16)
    columns = [total[:, at : at + HEAD_SIZE] for at in range(0, total.shape[1], HEAD_SIZE)]
    return (
        grads[0],
        grads[1],
        jnp.concatenate(columns[0::2], axis=1),
        jnp.concatenate(columns[1::2], axis=1),
    )


def solution(mesh):
    spec = P(AXES, None)
    return jax.shard_map(
        local,
        mesh=mesh,
        in_specs=(spec, spec, spec, spec, P()),
        out_specs=(spec, spec, spec, spec),
        check_vma=False,
    )
```

```python
import functools
import math

import jax
import jax.numpy as jnp
from jax import lax
from jax.experimental import pallas as pl
from jax.experimental.pallas import tpu as pltpu
from jax.sharding import PartitionSpec as P

HEAD_SIZE = 128
QUERY_HEADS = 32
KEY_VALUE_HEADS = 4
GROUP = QUERY_HEADS // KEY_VALUE_HEADS
SPAN = 4
AXES = ("blk", "inner")
ROWS = 32
UNIT = 4
FORWARD = ((0,), (1,), (2, 3))
OUTS = 5
SCRATCH = 31
MASKED = -1e30
SCALE = 1.0 / math.sqrt(HEAD_SIZE)
EXP2_SCALE = SCALE * math.log2(math.e)

NN = (((1,), (0,)), ((), ()))


def dot(a, b, dims=NN):
    return lax.dot_general(a, b, dims, preferred_element_type=jnp.float32)


def device_count():
    return lax.axis_size("blk") * lax.axis_size("inner")


def passed_along(value, steps):
    count = device_count()
    first, last = (max(0, -steps), min(count, count - steps))
    return lax.ppermute(value, AXES, [(source, source + steps) for source in range(first, last)])


def write_masks(bias_ref, old_ref, cut_ref, lengths_ref, first_ref, rows):
    docs = lengths_ref.shape[0]
    first = first_ref[0]
    row = lax.broadcasted_iota(jnp.int32, (rows, 128), 0)
    query_pos = first + row

    def step(doc, carry):
        end, start = carry
        end = end + lengths_ref[doc]
        return end, jnp.where(query_pos >= end, end, start)

    _, start = lax.fori_loop(0, docs, step, (jnp.int32(0), jnp.zeros((rows, 128), jnp.int32)))
    lane = lax.broadcasted_iota(jnp.int32, (rows, 128), 1)
    old = start < first - (SPAN - 2) * rows
    old_ref[...] = jnp.where(old, 1.0, 0.0)
    cut = jnp.min(jnp.where(old, start - (first - (SPAN - 1) * rows), rows), axis=0, keepdims=True)
    cut_ref[...] = jnp.broadcast_to(cut, cut_ref.shape)
    cut = jnp.broadcast_to(cut, (rows, 128))
    for part in range((SPAN - 1) * rows // 128):
        offset = part * 128 + lane
        if part < rows // 128:
            own = (offset <= row) & ((first + offset >= start) | (old & (offset < cut)))
            allowed = own | (old & (offset >= cut))
        else:
            allowed = first - (SPAN - 1) * rows + offset >= start
        bias_ref[:, part * 128 : (part + 1) * 128] = jnp.where(allowed, 0.0, MASKED)


def attention_kernel(where, q_ref, g_ref, behind_ref, near_ref, own_full_ref, bias_ref, old_ref, cut_ref, *refs):
    out_ref, dq_ref, dbehind_ref, dnear_ref, down_ref = refs[-(OUTS + SCRATCH) : -SCRATCH]
    (
        key_ref, value_ref, key_t_ref, value_t_ref, key2_ref, value2_ref, key2_t_ref, value2_t_ref,
        dk_ref, dv_ref, dk2_ref, dv2_ref, *slots,
    ) = refs[-SCRATCH:]
    slots, copies = slots[:13], slots[13:]
    s_refs, p_refs, dp_refs, d_refs, g_refs, delta_refs = (slots[i : i + 2] for i in range(0, 12, 2))
    (inv_ref,) = slots[12:]
    head, *offsets = where
    key_in, value_in, key_out, value_out = (slice(at, at + HEAD_SIZE) for at in offsets)
    q_full_ref, g_full_ref, out_full_ref, dq_full_ref = q_ref, g_ref, out_ref, dq_ref
    q_ref, g_ref, out_ref, dq_ref, own_ref, sem = copies
    rows, wide = q_ref.shape
    mine = slice(head * wide, (head + 1) * wide)
    q_copy = pltpu.make_async_copy(q_full_ref.at[:, mine], q_ref, sem.at[0])
    g_copy = pltpu.make_async_copy(g_full_ref.at[:, mine], g_ref, sem.at[1])
    own_copy = pltpu.make_async_copy(own_full_ref, own_ref, sem.at[2 + 2 * GROUP // UNIT])
    own_copy.start()
    q_copy.start()
    g_copy.start()
    window = (SPAN - 1) * rows
    units = GROUP // UNIT
    stack = UNIT * rows
    two = slice(0, rows)
    rest = slice(rows, window)

    own_copy.wait()
    from_far = lax.broadcasted_iota(jnp.int32, (rows, HEAD_SIZE), 0) >= cut_ref[0, 0]
    mid, far, near, own = behind_ref.at[0], behind_ref.at[1], near_ref, own_ref
    for j, block in enumerate((mid, near)):
        span = slice(j * rows, (j + 1) * rows)
        key_ref[span] = block[:, key_in]
        value_ref[span] = block[:, value_in]
        key_t_ref[:, span] = block[:, key_in].T
        value_t_ref[:, span] = block[:, value_in].T
    for which, plain_ref, turned_ref in ((key_in, key2_ref, key2_t_ref), (value_in, value2_ref, value2_t_ref)):
        mine = own[:, which]
        either = jnp.where(from_far, far[:, which].astype(jnp.float32), mine.astype(jnp.float32))
        for j, block in enumerate((either.astype(jnp.bfloat16), mine)):
            span = slice(j * HEAD_SIZE, (j + 1) * HEAD_SIZE)
            plain_ref[:, span] = block
            turned_ref[span] = block.T

    def places(unit):
        return [
            (
                slice(i * rows, (i + 1) * rows),
                slice((unit * UNIT + i) * HEAD_SIZE, (unit * UNIT + i + 1) * HEAD_SIZE),
            )
            for i in range(UNIT)
        ]

    def stacked(ref, unit):
        return jnp.concatenate([ref[:, cols] for _, cols in places(unit)], axis=0)

    def doubled(x):
        old = jnp.concatenate([old_ref[...].astype(jnp.bfloat16)] * UNIT, axis=0)
        return jnp.concatenate([x * old, x * (1 - old)], axis=1)

    def picked(x):
        old = jnp.concatenate([old_ref[...]] * UNIT, axis=0)
        return jnp.where(old > 0.5, x[:, :HEAD_SIZE], x[:, HEAD_SIZE:])

    def scores(unit, slot):
        q = stacked(q_ref, unit)
        s_refs[slot][:, two] = dot(doubled(q), key2_t_ref[...])
        s_refs[slot][:, rest] = dot(q, key_t_ref[...])

    def softmax(slot):
        for r in range(0, stack, ROWS):
            here = slice(r, r + ROWS)
            row = slice(r % rows, r % rows + ROWS)
            s = s_refs[slot][here] * EXP2_SCALE + bias_ref[row]
            e = jnp.exp2(s - jnp.max(s, axis=1, keepdims=True))
            inv = 1.0 / jnp.sum(e, axis=1, keepdims=True)
            inv_ref[here] = jnp.broadcast_to(inv, (ROWS, HEAD_SIZE))
            p_refs[slot][here] = e.astype(jnp.bfloat16)

    def mix(unit, slot):
        p_ref, g_ref_here = p_refs[slot], g_refs[slot]
        total = picked(dot(p_ref[:, two], value2_ref[...])) + dot(p_ref[:, rest], value_ref[...])
        for here, cols in places(unit):
            inv = inv_ref[here]
            out = (total[here] * inv).astype(jnp.bfloat16)
            out_ref[:, cols] = out
            g = g_ref[:, cols].astype(jnp.float32) * inv
            delta = jnp.sum(g * out.astype(jnp.float32), axis=1, keepdims=True)
            delta_refs[slot][here] = jnp.broadcast_to(delta, (rows, HEAD_SIZE))
            g_ref_here[here] = g.astype(jnp.bfloat16)
        g = g_ref_here[...]
        dp_refs[slot][:, two] = dot(doubled(g), value2_t_ref[...])
        dp_refs[slot][:, rest] = dot(g, value_t_ref[...])

    def score_grad(slot):
        for r in range(0, stack, ROWS):
            here = slice(r, r + ROWS)
            delta = jnp.concatenate([delta_refs[slot][here]] * (window // HEAD_SIZE), axis=1)
            d_refs[slot][here] = p_refs[slot][here] * (dp_refs[slot][here] - delta).astype(jnp.bfloat16)

    def spread(unit, slot):
        p_ref, d_ref = p_refs[slot], d_refs[slot]
        total = picked(dot(d_ref[:, two], key2_ref[...])) + dot(d_ref[:, rest], key_ref[...])
        for here, cols in places(unit):
            dq_ref[:, cols] = (total[here] * SCALE).astype(jnp.bfloat16)
        q = stacked(q_ref, unit)
        g = g_refs[slot][...]
        for total_ref, left, right in (
            (dk2_ref, doubled(q), d_ref[:, two]),
            (dk_ref, q, d_ref[:, rest]),
            (dv2_ref, doubled(g), p_ref[:, two]),
            (dv_ref, g, p_ref[:, rest]),
        ):
            term = dot(left.T, right)
            total_ref[...] = term if unit == 0 else total_ref[...] + term

    def send(unit, scratch_ref, full_ref, at):
        part = slice(unit * UNIT * HEAD_SIZE, (unit + 1) * UNIT * HEAD_SIZE)
        place = slice(head * wide + part.start, head * wide + part.stop)
        copy = pltpu.make_async_copy(scratch_ref.at[:, part], full_ref.at[:, place], sem.at[at])
        copy.start()
        return copy

    q_copy.wait()
    scores(0, 0)
    sent = []
    for unit in range(units):
        slot = unit % 2
        if unit + 1 < units:
            scores(unit + 1, 1 - slot)
        if unit > 0:
            score_grad(1 - slot)
        softmax(slot)
        if unit > 0:
            spread(unit - 1, 1 - slot)
            sent.append(send(unit - 1, dq_ref, dq_full_ref, 2 + 2 * (unit - 1)))
        if unit == 0:
            g_copy.wait()
        mix(unit, slot)
        sent.append(send(unit, out_ref, out_full_ref, 3 + 2 * unit))
    score_grad((units - 1) % 2)
    spread(units - 1, (units - 1) % 2)
    sent.append(send(units - 1, dq_ref, dq_full_ref, 2 * units))
    for span, grad, grad2, scale in ((key_out, dk_ref, dk2_ref, SCALE), (value_out, dv_ref, dv2_ref, 1.0)):
        either = grad2[:HEAD_SIZE].T * scale
        own = grad2[HEAD_SIZE:].T * scale
        dbehind_ref[0, :, span] = (grad[:, :rows].T * scale).astype(jnp.bfloat16)
        dbehind_ref[1, :, span] = jnp.where(from_far, either, 0.0).astype(jnp.bfloat16)
        dnear_ref[:, span] = grad[:, rows:].T * scale
        down_ref[:, span] = own + jnp.where(from_far, 0.0, either)
    for copy in sent:
        copy.wait()


def attention(head, queries, out_grad, blocks, place, grads, masks):
    rows = queries.shape[0]
    wide = GROUP * HEAD_SIZE
    pair = 2 * HEAD_SIZE
    window = (SPAN - 1) * rows
    query_spec = pl.BlockSpec(memory_space=pltpu.HBM)

    def whole(shape):
        return pl.BlockSpec(shape, lambda i, *_: (0,) * len(shape))

    fore = blocks[-1].shape[1] // pair
    where = [head, *(at * HEAD_SIZE for at in (place, fore + place, 0, 1))]
    operands = [queries, out_grad, *blocks, *masks]
    in_specs = [query_spec] * 2 + [whole(block.shape) for block in blocks[:-1]]
    in_specs += [pl.BlockSpec(memory_space=pl.ANY)] + [whole(mask.shape) for mask in masks]
    aliases = {}
    for at, array in enumerate(grads):
        if array is not None:
            aliases[len(operands)] = at
            operands.append(array)
            in_specs.append(query_spec)
    bf16, f32 = jnp.bfloat16, jnp.float32
    results = pl.pallas_call(
        functools.partial(attention_kernel, where),
        out_shape=[
            jax.ShapeDtypeStruct(queries.shape, bf16),
            jax.ShapeDtypeStruct(queries.shape, bf16),
            jax.ShapeDtypeStruct((2, rows, pair), bf16),
            jax.ShapeDtypeStruct((rows, pair), f32),
            jax.ShapeDtypeStruct((rows, pair), f32),
        ],
        grid_spec=pltpu.PrefetchScalarGridSpec(
            num_scalar_prefetch=0,
            grid=(1,),
            in_specs=in_specs,
            out_specs=[query_spec] * 2
            + [whole((2, rows, pair)), whole((rows, pair)), whole((rows, pair))],
            scratch_shapes=[
                pltpu.VMEM(shape, kind)
                for shape, kind, count in (
                    ((2 * rows, HEAD_SIZE), bf16, 2),
                    ((HEAD_SIZE, 2 * rows), bf16, 2),
                    ((rows, pair), bf16, 2),
                    ((pair, rows), bf16, 2),
                    ((HEAD_SIZE, 2 * rows), f32, 2),
                    ((pair, rows), f32, 2),
                    ((UNIT * rows, window), f32, 2),
                    ((UNIT * rows, window), bf16, 2),
                    ((UNIT * rows, window), f32, 2),
                    ((UNIT * rows, window), bf16, 2),
                    ((UNIT * rows, HEAD_SIZE), bf16, 2),
                    ((UNIT * rows, HEAD_SIZE), f32, 2),
                    ((UNIT * rows, HEAD_SIZE), f32, 1),
                )
                for _ in range(count)
            ]
            + [pltpu.VMEM((rows, wide), bf16)] * 4
            + [pltpu.VMEM(blocks[-1].shape, bf16), pltpu.SemaphoreType.DMA((3 + 2 * GROUP // UNIT,))],
        ),
        input_output_aliases=aliases,
        compiler_params=pltpu.CompilerParams(vmem_limit_bytes=51 * 1024 * 1024),
        cost_estimate=pl.CostEstimate(
            flops=12 * rows * GROUP * window * HEAD_SIZE * 2,
            bytes_accessed=4 * rows * wide * 2 + 22 * rows * pair,
            transcendentals=0,
        ),
        name="attention",
    )(*operands)
    return results[:2], results[2:]


def origin(rank, *_):
    return (0,) * rank


def pack_kernel(first_ref, lengths_ref, keys_ref, values_ref, *refs):
    write_masks(*refs[-3:], lengths_ref, first_ref, keys_ref.shape[0])
    for at, heads in enumerate(FORWARD):
        span = slice(heads[0] * HEAD_SIZE, (heads[-1] + 1) * HEAD_SIZE)
        width = span.stop - span.start
        own_ref, pair_ref = refs[2 * at : 2 * at + 2]
        for target_ref in (own_ref, pair_ref.at[0]):
            target_ref[:, :width] = keys_ref[:, span]
            target_ref[:, width:] = values_ref[:, span]


def pack(first, lengths, keys, values):
    rows = keys.shape[0]
    shapes = []
    for heads in FORWARD:
        own = (rows, 2 * HEAD_SIZE * len(heads))
        shapes += [jax.ShapeDtypeStruct(own, keys.dtype), jax.ShapeDtypeStruct((2, *own), keys.dtype)]
    specs = [
        pl.BlockSpec((1,) * (len(packed.shape) - 2) + packed.shape[-2:], functools.partial(origin, len(packed.shape)))
        for packed in shapes
    ]
    masks = [
        jax.ShapeDtypeStruct((rows, (SPAN - 1) * rows), jnp.float32),
        jax.ShapeDtypeStruct((rows, HEAD_SIZE), jnp.float32),
        jax.ShapeDtypeStruct((8, HEAD_SIZE), jnp.int32),
    ]
    two = functools.partial(origin, 2)
    results = pl.pallas_call(
        pack_kernel,
        out_shape=shapes + masks,
        grid_spec=pltpu.PrefetchScalarGridSpec(
            num_scalar_prefetch=2,
            grid=(1,),
            in_specs=[pl.BlockSpec(keys.shape, two)] * 2,
            out_specs=specs + [pl.BlockSpec(mask.shape, two) for mask in masks],
        ),
        name="pack",
    )(first, lengths, keys, values)
    packed = results[: len(shapes)]
    return packed[0::2], packed[1::2], results[len(shapes) :]


def local(queries, keys, values, out_grad, doc_lengths):
    rows = queries.shape[0]
    index = lax.axis_index(AXES)
    first = (index * rows).astype(jnp.int32).reshape(1)
    bf16, f32 = jnp.bfloat16, jnp.float32
    blocks, nears = {}, []
    owns, pairs, masks = pack(first, doc_lengths, keys, values)
    for own in owns:
        nears.append(passed_along(own, 1))
    pairs = [pair.at[1].set(near) for pair, near in zip(pairs, nears)]
    for heads, own, near, pair in zip(FORWARD, owns, nears, pairs):
        behind = passed_along(pair, 2)
        for place, head in enumerate(heads):
            blocks[head] = ((behind, near, own), place)
    grads = (None, None)
    parts = []

    def attend(head, after=()):
        nonlocal grads
        (behind, near, own), place = blocks[head]
        own, *after = lax.optimization_barrier((own, *after))
        grads, part = attention(head, queries, out_grad, (behind, near, own), place, grads, masks)
        parts.append(list(part))
        return after

    def second_hop(near, own, got):
        got = got.astype(f32)
        return (near + got[1]).astype(bf16), own + got[0]

    attend(0, pairs)
    gots = [passed_along(parts[0][0], -2)]
    attend(1)
    gots.append(passed_along(parts[1][0], -2))
    gots[0], _ = lax.optimization_barrier((gots[0], parts[1][0]))
    nears, owns = zip(second_hop(*parts[0][1:], gots[0]))
    (nears,) = attend(2, nears)
    gots.append(passed_along(parts[2][0], -2))
    gots[1], _ = lax.optimization_barrier((gots[1], parts[2][0]))
    more = second_hop(*parts[1][1:], gots[1])
    (nears, *more) = attend(3, (nears, *more))
    gots[2], near = lax.optimization_barrier((gots[2], parts[3][1]))
    gots.append(passed_along(parts[3][0], -2))
    parts[3][1] = near
    rest = [second_hop(*part[1:], got) for part, got in zip(parts[2:], gots[2:])]
    nears, owns = zip((nears, *owns), more, *rest)
    last = [passed_along(jnp.concatenate(nears[at : at + 2], axis=1), -1) for at in (0, 2)]
    total = (jnp.concatenate(owns, axis=1) + jnp.concatenate(last, axis=1).astype(f32)).astype(bf16)
    columns = [total[:, at : at + HEAD_SIZE] for at in range(0, total.shape[1], HEAD_SIZE)]
    return (
        grads[0],
        grads[1],
        jnp.concatenate(columns[0::2], axis=1),
        jnp.concatenate(columns[1::2], axis=1),
    )


def solution(mesh):
    spec = P(AXES, None)
    return jax.shard_map(
        local,
        mesh=mesh,
        in_specs=(spec, spec, spec, spec, P()),
        out_specs=(spec, spec, spec, spec),
        check_vma=False,
    )
```

```python
import functools
import math

import jax
import jax.numpy as jnp
from jax import lax
from jax.experimental import pallas as pl
from jax.experimental.pallas import tpu as pltpu
from jax.sharding import PartitionSpec as P

HEAD_SIZE = 128
QUERY_HEADS = 32
KEY_VALUE_HEADS = 4
GROUP = QUERY_HEADS // KEY_VALUE_HEADS
SPAN = 4
AXES = ("blk", "inner")
ROWS = 32
UNIT = 4
FORWARD = ((0,), (1,), (2, 3))
OUTS = 5
SCRATCH = 31
MASKED = -1e30
SCALE = 1.0 / math.sqrt(HEAD_SIZE)
EXP2_SCALE = SCALE * math.log2(math.e)

NN = (((1,), (0,)), ((), ()))


def dot(a, b, dims=NN):
    return lax.dot_general(a, b, dims, preferred_element_type=jnp.float32)


def device_count():
    return lax.axis_size("blk") * lax.axis_size("inner")


def passed_along(value, steps):
    count = device_count()
    first, last = (max(0, -steps), min(count, count - steps))
    return lax.ppermute(value, AXES, [(source, source + steps) for source in range(first, last)])


def write_masks(bias_ref, old_ref, cut_ref, lengths_ref, first_ref, rows):
    docs = lengths_ref.shape[0]
    first = first_ref[0]
    row = lax.broadcasted_iota(jnp.int32, (rows, 128), 0)
    query_pos = first + row

    def step(doc, carry):
        end, start = carry
        end = end + lengths_ref[doc]
        return end, jnp.where(query_pos >= end, end, start)

    _, start = lax.fori_loop(0, docs, step, (jnp.int32(0), jnp.zeros((rows, 128), jnp.int32)))
    lane = lax.broadcasted_iota(jnp.int32, (rows, 128), 1)
    old = start < first - (SPAN - 2) * rows
    old_ref[...] = jnp.where(old, 1.0, 0.0)
    cut = jnp.min(jnp.where(old, start - (first - (SPAN - 1) * rows), rows), axis=0, keepdims=True)
    cut_ref[...] = jnp.broadcast_to(cut, cut_ref.shape)
    cut = jnp.broadcast_to(cut, (rows, 128))
    for part in range((SPAN - 1) * rows // 128):
        offset = part * 128 + lane
        if part < rows // 128:
            own = (offset <= row) & ((first + offset >= start) | (old & (offset < cut)))
            allowed = own | (old & (offset >= cut))
        else:
            allowed = first - (SPAN - 1) * rows + offset >= start
        bias_ref[:, part * 128 : (part + 1) * 128] = jnp.where(allowed, 0.0, MASKED)


def attention_kernel(where, q_ref, g_ref, behind_ref, near_ref, own_full_ref, bias_ref, old_ref, cut_ref, *refs):
    out_ref, dq_ref, dbehind_ref, dnear_ref, down_ref = refs[-(OUTS + SCRATCH) : -SCRATCH]
    (
        key_ref, value_ref, key_t_ref, value_t_ref, key2_ref, value2_ref, key2_t_ref, value2_t_ref,
        dk_ref, dv_ref, dk2_ref, dv2_ref, *slots,
    ) = refs[-SCRATCH:]
    slots, copies = slots[:13], slots[13:]
    s_refs, p_refs, dp_refs, d_refs, g_refs, delta_refs = (slots[i : i + 2] for i in range(0, 12, 2))
    (inv_ref,) = slots[12:]
    head, *offsets = where
    key_in, value_in, key_out, value_out = (slice(at, at + HEAD_SIZE) for at in offsets)
    q_full_ref, g_full_ref, out_full_ref, dq_full_ref = q_ref, g_ref, out_ref, dq_ref
    q_ref, g_ref, out_ref, dq_ref, own_ref, sem = copies
    rows, wide = q_ref.shape
    mine = slice(head * wide, (head + 1) * wide)
    q_copy = pltpu.make_async_copy(q_full_ref.at[:, mine], q_ref, sem.at[0])
    g_copy = pltpu.make_async_copy(g_full_ref.at[:, mine], g_ref, sem.at[1])
    own_copy = pltpu.make_async_copy(own_full_ref, own_ref, sem.at[2 + 2 * GROUP // UNIT])
    own_copy.start()
    q_copy.start()
    g_copy.start()
    window = (SPAN - 1) * rows
    units = GROUP // UNIT
    stack = UNIT * rows
    two = slice(0, rows)
    rest = slice(rows, window)

    own_copy.wait()
    from_far = lax.broadcasted_iota(jnp.int32, (rows, HEAD_SIZE), 0) >= cut_ref[0, 0]
    mid, far, near, own = behind_ref.at[0], behind_ref.at[1], near_ref, own_ref
    for j, block in enumerate((mid, near)):
        span = slice(j * rows, (j + 1) * rows)
        key_ref[span] = block[:, key_in]
        value_ref[span] = block[:, value_in]
        key_t_ref[:, span] = block[:, key_in].T
        value_t_ref[:, span] = block[:, value_in].T
    for which, plain_ref, turned_ref in ((key_in, key2_ref, key2_t_ref), (value_in, value2_ref, value2_t_ref)):
        mine = own[:, which]
        either = jnp.where(from_far, far[:, which].astype(jnp.float32), mine.astype(jnp.float32))
        for j, block in enumerate((either.astype(jnp.bfloat16), mine)):
            span = slice(j * HEAD_SIZE, (j + 1) * HEAD_SIZE)
            plain_ref[:, span] = block
            turned_ref[span] = block.T

    def places(unit):
        return [
            (
                slice(i * rows, (i + 1) * rows),
                slice((unit * UNIT + i) * HEAD_SIZE, (unit * UNIT + i + 1) * HEAD_SIZE),
            )
            for i in range(UNIT)
        ]

    def stacked(ref, unit):
        return jnp.concatenate([ref[:, cols] for _, cols in places(unit)], axis=0)

    def doubled(x):
        old = jnp.concatenate([old_ref[...].astype(jnp.bfloat16)] * UNIT, axis=0)
        return jnp.concatenate([x * old, x * (1 - old)], axis=1)

    def picked(x):
        old = jnp.concatenate([old_ref[...]] * UNIT, axis=0)
        return jnp.where(old > 0.5, x[:, :HEAD_SIZE], x[:, HEAD_SIZE:])

    def scores(unit, slot):
        q = stacked(q_ref, unit)
        s_refs[slot][:, two] = dot(doubled(q), key2_t_ref[...])
        s_refs[slot][:, rest] = dot(q, key_t_ref[...])

    def softmax(slot):
        for r in range(0, stack, ROWS):
            here = slice(r, r + ROWS)
            row = slice(r % rows, r % rows + ROWS)
            s = s_refs[slot][here] * EXP2_SCALE + bias_ref[row]
            e = jnp.exp2(s - jnp.max(s, axis=1, keepdims=True))
            inv = 1.0 / jnp.sum(e, axis=1, keepdims=True)
            inv_ref[here] = jnp.broadcast_to(inv, (ROWS, HEAD_SIZE))
            p_refs[slot][here] = e.astype(jnp.bfloat16)

    def mix(unit, slot):
        p_ref, g_ref_here = p_refs[slot], g_refs[slot]
        total = picked(dot(p_ref[:, two], value2_ref[...])) + dot(p_ref[:, rest], value_ref[...])
        for here, cols in places(unit):
            inv = inv_ref[here]
            out = (total[here] * inv).astype(jnp.bfloat16)
            out_ref[:, cols] = out
            g = g_ref[:, cols].astype(jnp.float32) * inv
            delta = jnp.sum(g * out.astype(jnp.float32), axis=1, keepdims=True)
            delta_refs[slot][here] = jnp.broadcast_to(delta, (rows, HEAD_SIZE))
            g_ref_here[here] = g.astype(jnp.bfloat16)
        g = g_ref_here[...]
        dp_refs[slot][:, two] = dot(doubled(g), value2_t_ref[...])
        dp_refs[slot][:, rest] = dot(g, value_t_ref[...])

    def score_grad(slot):
        for r in range(0, stack, ROWS):
            here = slice(r, r + ROWS)
            delta = jnp.concatenate([delta_refs[slot][here]] * (window // HEAD_SIZE), axis=1)
            d_refs[slot][here] = p_refs[slot][here] * (dp_refs[slot][here] - delta).astype(jnp.bfloat16)

    def spread(unit, slot):
        p_ref, d_ref = p_refs[slot], d_refs[slot]
        total = picked(dot(d_ref[:, two], key2_ref[...])) + dot(d_ref[:, rest], key_ref[...])
        for here, cols in places(unit):
            dq_ref[:, cols] = (total[here] * SCALE).astype(jnp.bfloat16)
        q = stacked(q_ref, unit)
        g = g_refs[slot][...]
        for total_ref, left, right in (
            (dk2_ref, doubled(q), d_ref[:, two]),
            (dk_ref, q, d_ref[:, rest]),
            (dv2_ref, doubled(g), p_ref[:, two]),
            (dv_ref, g, p_ref[:, rest]),
        ):
            term = dot(left.T, right)
            total_ref[...] = term if unit == 0 else total_ref[...] + term

    def send(unit, scratch_ref, full_ref, at):
        part = slice(unit * UNIT * HEAD_SIZE, (unit + 1) * UNIT * HEAD_SIZE)
        place = slice(head * wide + part.start, head * wide + part.stop)
        copy = pltpu.make_async_copy(scratch_ref.at[:, part], full_ref.at[:, place], sem.at[at])
        copy.start()
        return copy

    q_copy.wait()
    scores(0, 0)
    sent = []
    for unit in range(units):
        slot = unit % 2
        if unit + 1 < units:
            scores(unit + 1, 1 - slot)
        if unit > 0:
            score_grad(1 - slot)
        softmax(slot)
        if unit > 0:
            spread(unit - 1, 1 - slot)
            sent.append(send(unit - 1, dq_ref, dq_full_ref, 2 + 2 * (unit - 1)))
        if unit == 0:
            g_copy.wait()
        mix(unit, slot)
        sent.append(send(unit, out_ref, out_full_ref, 3 + 2 * unit))
    score_grad((units - 1) % 2)
    spread(units - 1, (units - 1) % 2)
    sent.append(send(units - 1, dq_ref, dq_full_ref, 2 * units))
    for span, grad, grad2, scale in ((key_out, dk_ref, dk2_ref, SCALE), (value_out, dv_ref, dv2_ref, 1.0)):
        either = grad2[:HEAD_SIZE].T * scale
        own = grad2[HEAD_SIZE:].T * scale
        dbehind_ref[0, :, span] = (grad[:, :rows].T * scale).astype(jnp.bfloat16)
        dbehind_ref[1, :, span] = jnp.where(from_far, either, 0.0).astype(jnp.bfloat16)
        dnear_ref[:, span] = grad[:, rows:].T * scale
        down_ref[:, span] = own + jnp.where(from_far, 0.0, either)
    for copy in sent:
        copy.wait()


def attention(head, queries, out_grad, blocks, place, grads, masks):
    rows = queries.shape[0]
    wide = GROUP * HEAD_SIZE
    pair = 2 * HEAD_SIZE
    window = (SPAN - 1) * rows
    query_spec = pl.BlockSpec(memory_space=pltpu.HBM)

    def whole(shape):
        return pl.BlockSpec(shape, lambda i, *_: (0,) * len(shape))

    fore = blocks[-1].shape[1] // pair
    where = [head, *(at * HEAD_SIZE for at in (place, fore + place, 0, 1))]
    operands = [queries, out_grad, *blocks, *masks]
    in_specs = [query_spec] * 2 + [whole(block.shape) for block in blocks[:-1]]
    in_specs += [pl.BlockSpec(memory_space=pl.ANY)] + [whole(mask.shape) for mask in masks]
    aliases = {}
    for at, array in enumerate(grads):
        if array is not None:
            aliases[len(operands)] = at
            operands.append(array)
            in_specs.append(query_spec)
    bf16, f32 = jnp.bfloat16, jnp.float32
    results = pl.pallas_call(
        functools.partial(attention_kernel, where),
        out_shape=[
            jax.ShapeDtypeStruct(queries.shape, bf16),
            jax.ShapeDtypeStruct(queries.shape, bf16),
            jax.ShapeDtypeStruct((2, rows, pair), bf16),
            jax.ShapeDtypeStruct((rows, pair), f32),
            jax.ShapeDtypeStruct((rows, pair), f32),
        ],
        grid_spec=pltpu.PrefetchScalarGridSpec(
            num_scalar_prefetch=0,
            grid=(1,),
            in_specs=in_specs,
            out_specs=[query_spec] * 2
            + [whole((2, rows, pair)), whole((rows, pair)), whole((rows, pair))],
            scratch_shapes=[
                pltpu.VMEM(shape, kind)
                for shape, kind, count in (
                    ((2 * rows, HEAD_SIZE), bf16, 2),
                    ((HEAD_SIZE, 2 * rows), bf16, 2),
                    ((rows, pair), bf16, 2),
                    ((pair, rows), bf16, 2),
                    ((HEAD_SIZE, 2 * rows), f32, 2),
                    ((pair, rows), f32, 2),
                    ((UNIT * rows, window), f32, 2),
                    ((UNIT * rows, window), bf16, 2),
                    ((UNIT * rows, window), f32, 2),
                    ((UNIT * rows, window), bf16, 2),
                    ((UNIT * rows, HEAD_SIZE), bf16, 2),
                    ((UNIT * rows, HEAD_SIZE), f32, 2),
                    ((UNIT * rows, HEAD_SIZE), f32, 1),
                )
                for _ in range(count)
            ]
            + [pltpu.VMEM((rows, wide), bf16)] * 4
            + [pltpu.VMEM(blocks[-1].shape, bf16), pltpu.SemaphoreType.DMA((3 + 2 * GROUP // UNIT,))],
        ),
        input_output_aliases=aliases,
        compiler_params=pltpu.CompilerParams(vmem_limit_bytes=51 * 1024 * 1024),
        cost_estimate=pl.CostEstimate(
            flops=12 * rows * GROUP * window * HEAD_SIZE * 2,
            bytes_accessed=4 * rows * wide * 2 + 22 * rows * pair,
            transcendentals=0,
        ),
        name="attention",
    )(*operands)
    return results[:2], results[2:]


def origin(rank, *_):
    return (0,) * rank


def pack_kernel(first_ref, lengths_ref, keys_ref, values_ref, *refs):
    write_masks(*refs[-3:], lengths_ref, first_ref, keys_ref.shape[0])
    for at, heads in enumerate(FORWARD):
        span = slice(heads[0] * HEAD_SIZE, (heads[-1] + 1) * HEAD_SIZE)
        width = span.stop - span.start
        own_ref, pair_ref = refs[2 * at : 2 * at + 2]
        for target_ref in (own_ref, pair_ref.at[0]):
            target_ref[:, :width] = keys_ref[:, span]
            target_ref[:, width:] = values_ref[:, span]


def pack(first, lengths, keys, values):
    rows = keys.shape[0]
    shapes = []
    for heads in FORWARD:
        own = (rows, 2 * HEAD_SIZE * len(heads))
        shapes += [jax.ShapeDtypeStruct(own, keys.dtype), jax.ShapeDtypeStruct((2, *own), keys.dtype)]
    specs = [
        pl.BlockSpec((1,) * (len(packed.shape) - 2) + packed.shape[-2:], functools.partial(origin, len(packed.shape)))
        for packed in shapes
    ]
    masks = [
        jax.ShapeDtypeStruct((rows, (SPAN - 1) * rows), jnp.float32),
        jax.ShapeDtypeStruct((rows, HEAD_SIZE), jnp.float32),
        jax.ShapeDtypeStruct((8, HEAD_SIZE), jnp.int32),
    ]
    two = functools.partial(origin, 2)
    results = pl.pallas_call(
        pack_kernel,
        out_shape=shapes + masks,
        grid_spec=pltpu.PrefetchScalarGridSpec(
            num_scalar_prefetch=2,
            grid=(1,),
            in_specs=[pl.BlockSpec(keys.shape, two)] * 2,
            out_specs=specs + [pl.BlockSpec(mask.shape, two) for mask in masks],
        ),
        compiler_params=pltpu.CompilerParams(vmem_limit_bytes=12 * 1024 * 1024),
        name="pack",
    )(first, lengths, keys, values)
    packed = results[: len(shapes)]
    return packed[0::2], packed[1::2], results[len(shapes) :]


def local(queries, keys, values, out_grad, doc_lengths):
    rows = queries.shape[0]
    index = lax.axis_index(AXES)
    first = (index * rows).astype(jnp.int32).reshape(1)
    bf16, f32 = jnp.bfloat16, jnp.float32
    blocks, nears = {}, []
    owns, pairs, masks = pack(first, doc_lengths, keys, values)
    for own in owns:
        nears.append(passed_along(own, 1))
    pairs = [pair.at[1].set(near) for pair, near in zip(pairs, nears)]
    for heads, own, near, pair in zip(FORWARD, owns, nears, pairs):
        behind = passed_along(pair, 2)
        for place, head in enumerate(heads):
            blocks[head] = ((behind, near, own), place)
    grads = (None, None)
    parts = []

    def attend(head, after=()):
        nonlocal grads
        (behind, near, own), place = blocks[head]
        own, *after = lax.optimization_barrier((own, *after))
        grads, part = attention(head, queries, out_grad, (behind, near, own), place, grads, masks)
        parts.append(list(part))
        return after

    def second_hop(near, own, got):
        got = got.astype(f32)
        return (near + got[1]).astype(bf16), own + got[0]

    attend(0, pairs)
    attend(1)
    got_early = passed_along(jnp.concatenate([parts[0][0], parts[1][0]], axis=2), -2)
    attend(2)
    got = passed_along(parts[2][0], -2)
    attend(3)
    got_early, got, parts[3][1] = lax.optimization_barrier((got_early, got, parts[3][1]))
    pair = 2 * HEAD_SIZE
    early = [second_hop(*parts[at][1:], got_early[:, :, at * pair : (at + 1) * pair]) for at in range(2)]
    nears, owns = zip(*early)
    near = jnp.concatenate(nears, axis=1)
    near, parts[3][0] = lax.optimization_barrier((near, parts[3][0]))
    got_last = passed_along(parts[3][0], -2)
    last = [passed_along(near, -1)]
    late = [second_hop(*parts[2][1:], got), second_hop(*parts[3][1:], got_last)]
    nears, late = zip(*late)
    last.append(passed_along(jnp.concatenate(nears, axis=1), -1))
    owns += late
    total = (jnp.concatenate(owns, axis=1) + jnp.concatenate(last, axis=1).astype(f32)).astype(bf16)
    columns = [total[:, at : at + HEAD_SIZE] for at in range(0, total.shape[1], HEAD_SIZE)]
    return (
        grads[0],
        grads[1],
        jnp.concatenate(columns[0::2], axis=1),
        jnp.concatenate(columns[1::2], axis=1),
    )


def solution(mesh):
    spec = P(AXES, None)
    return jax.shard_map(
        local,
        mesh=mesh,
        in_specs=(spec, spec, spec, spec, P()),
        out_specs=(spec, spec, spec, spec),
        check_vma=False,
    )
```

```python
import functools
import math

import jax
import jax.numpy as jnp
from jax import lax
from jax.experimental import pallas as pl
from jax.experimental.pallas import tpu as pltpu
from jax.sharding import PartitionSpec as P

HEAD_SIZE = 128
QUERY_HEADS = 32
KEY_VALUE_HEADS = 4
GROUP = QUERY_HEADS // KEY_VALUE_HEADS
SPAN = 4
AXES = ("blk", "inner")
ROWS = 32
UNIT = 4
FORWARD = ((0,), (1,), (2, 3))
OUTS = 5
SCRATCH = 37
MASKED = -1e30
SCALE = 1.0 / math.sqrt(HEAD_SIZE)
EXP2_SCALE = SCALE * math.log2(math.e)

NN = (((1,), (0,)), ((), ()))


def dot(a, b, dims=NN):
    return lax.dot_general(a, b, dims, preferred_element_type=jnp.float32)


def device_count():
    return lax.axis_size("blk") * lax.axis_size("inner")


def passed_along(value, steps):
    count = device_count()
    first, last = (max(0, -steps), min(count, count - steps))
    return lax.ppermute(value, AXES, [(source, source + steps) for source in range(first, last)])


def write_masks(bias_ref, old_ref, cut_ref, lengths_ref, first_ref, rows):
    docs = lengths_ref.shape[0]
    first = first_ref[0]
    row = lax.broadcasted_iota(jnp.int32, (rows, 128), 0)
    query_pos = first + row

    def step(doc, carry):
        end, start = carry
        end = end + lengths_ref[doc]
        return end, jnp.where(query_pos >= end, end, start)

    _, start = lax.fori_loop(0, docs, step, (jnp.int32(0), jnp.zeros((rows, 128), jnp.int32)))
    lane = lax.broadcasted_iota(jnp.int32, (rows, 128), 1)
    old = start < first - (SPAN - 2) * rows
    old_ref[...] = jnp.where(old, 1.0, 0.0)
    cut = jnp.min(jnp.where(old, start - (first - (SPAN - 1) * rows), rows), axis=0, keepdims=True)
    cut_ref[...] = jnp.broadcast_to(cut, cut_ref.shape)
    cut = jnp.broadcast_to(cut, (rows, 128))
    for part in range((SPAN - 1) * rows // 128):
        offset = part * 128 + lane
        if part < rows // 128:
            own = (offset <= row) & ((first + offset >= start) | (old & (offset < cut)))
            allowed = own | (old & (offset >= cut))
        else:
            allowed = first - (SPAN - 1) * rows + offset >= start
        bias_ref[:, part * 128 : (part + 1) * 128] = jnp.where(allowed, 0.0, MASKED)


def attention_kernel(where, q_ref, g_ref, *refs):
    given_refs = refs[:6]
    out_ref, dq_ref, dbehind_ref, dnear_ref, down_ref = refs[-(OUTS + SCRATCH) : -SCRATCH]
    (
        key_ref, value_ref, key_t_ref, value_t_ref, key2_ref, value2_ref, key2_t_ref, value2_t_ref,
        dk_ref, dv_ref, dk2_ref, dv2_ref, *slots,
    ) = refs[-SCRATCH:]
    slots, copies = slots[:13], slots[13:]
    s_refs, p_refs, dp_refs, d_refs, g_refs, delta_refs = (slots[i : i + 2] for i in range(0, 12, 2))
    (inv_ref,) = slots[12:]
    head, *offsets = where
    key_in, value_in, key_out, value_out = (slice(at, at + HEAD_SIZE) for at in offsets)
    q_full_ref, g_full_ref, out_full_ref, dq_full_ref = q_ref, g_ref, out_ref, dq_ref
    q_ref, g_ref, out_ref, dq_ref, *held_refs, sem, held_sem = copies
    behind_ref, near_ref, own_ref, bias_ref, old_ref, cut_ref = held_refs
    rows, wide = q_ref.shape
    mine = slice(head * wide, (head + 1) * wide)
    q_copy = pltpu.make_async_copy(q_full_ref.at[:, mine], q_ref, sem.at[0])
    g_copy = pltpu.make_async_copy(g_full_ref.at[:, mine], g_ref, sem.at[1])
    held = [
        pltpu.make_async_copy(given, here, held_sem.at[at])
        for at, (given, here) in enumerate(zip(given_refs, held_refs))
    ]
    behind_copy, near_copy, own_copy, bias_copy, old_copy, cut_copy = held
    for copy in (own_copy, cut_copy, near_copy, behind_copy, q_copy, old_copy, bias_copy, g_copy):
        copy.start()
    window = (SPAN - 1) * rows
    units = GROUP // UNIT
    stack = UNIT * rows
    two = slice(0, rows)
    rest = slice(rows, window)

    for copy in (own_copy, cut_copy, near_copy, behind_copy):
        copy.wait()
    from_far = lax.broadcasted_iota(jnp.int32, (rows, HEAD_SIZE), 0) >= cut_ref[0, 0]
    mid, far, near, own = behind_ref.at[0], behind_ref.at[1], near_ref, own_ref
    for j, block in enumerate((mid, near)):
        span = slice(j * rows, (j + 1) * rows)
        key_ref[span] = block[:, key_in]
        value_ref[span] = block[:, value_in]
        key_t_ref[:, span] = block[:, key_in].T
        value_t_ref[:, span] = block[:, value_in].T
    for which, plain_ref, turned_ref in ((key_in, key2_ref, key2_t_ref), (value_in, value2_ref, value2_t_ref)):
        mine = own[:, which]
        either = jnp.where(from_far, far[:, which].astype(jnp.float32), mine.astype(jnp.float32))
        for j, block in enumerate((either.astype(jnp.bfloat16), mine)):
            span = slice(j * HEAD_SIZE, (j + 1) * HEAD_SIZE)
            plain_ref[:, span] = block
            turned_ref[span] = block.T

    def places(unit):
        return [
            (
                slice(i * rows, (i + 1) * rows),
                slice((unit * UNIT + i) * HEAD_SIZE, (unit * UNIT + i + 1) * HEAD_SIZE),
            )
            for i in range(UNIT)
        ]

    def stacked(ref, unit):
        return jnp.concatenate([ref[:, cols] for _, cols in places(unit)], axis=0)

    def doubled(x):
        old = jnp.concatenate([old_ref[...].astype(jnp.bfloat16)] * UNIT, axis=0)
        return jnp.concatenate([x * old, x * (1 - old)], axis=1)

    def picked(x):
        old = jnp.concatenate([old_ref[...]] * UNIT, axis=0)
        return jnp.where(old > 0.5, x[:, :HEAD_SIZE], x[:, HEAD_SIZE:])

    def scores(unit, slot):
        q = stacked(q_ref, unit)
        s_refs[slot][:, two] = dot(doubled(q), key2_t_ref[...])
        s_refs[slot][:, rest] = dot(q, key_t_ref[...])

    def softmax(slot):
        for r in range(0, stack, ROWS):
            here = slice(r, r + ROWS)
            row = slice(r % rows, r % rows + ROWS)
            s = s_refs[slot][here] * EXP2_SCALE + bias_ref[row]
            e = jnp.exp2(s - jnp.max(s, axis=1, keepdims=True))
            inv = 1.0 / jnp.sum(e, axis=1, keepdims=True)
            inv_ref[here] = jnp.broadcast_to(inv, (ROWS, HEAD_SIZE))
            p_refs[slot][here] = e.astype(jnp.bfloat16)

    def mix(unit, slot):
        p_ref, g_ref_here = p_refs[slot], g_refs[slot]
        total = picked(dot(p_ref[:, two], value2_ref[...])) + dot(p_ref[:, rest], value_ref[...])
        for here, cols in places(unit):
            inv = inv_ref[here]
            out = (total[here] * inv).astype(jnp.bfloat16)
            out_ref[:, cols] = out
            g = g_ref[:, cols].astype(jnp.float32) * inv
            delta = jnp.sum(g * out.astype(jnp.float32), axis=1, keepdims=True)
            delta_refs[slot][here] = jnp.broadcast_to(delta, (rows, HEAD_SIZE))
            g_ref_here[here] = g.astype(jnp.bfloat16)
        g = g_ref_here[...]
        dp_refs[slot][:, two] = dot(doubled(g), value2_t_ref[...])
        dp_refs[slot][:, rest] = dot(g, value_t_ref[...])

    def score_grad(slot):
        for r in range(0, stack, ROWS):
            here = slice(r, r + ROWS)
            delta = jnp.concatenate([delta_refs[slot][here]] * (window // HEAD_SIZE), axis=1)
            d_refs[slot][here] = p_refs[slot][here] * (dp_refs[slot][here] - delta).astype(jnp.bfloat16)

    def spread(unit, slot):
        p_ref, d_ref = p_refs[slot], d_refs[slot]
        total = picked(dot(d_ref[:, two], key2_ref[...])) + dot(d_ref[:, rest], key_ref[...])
        for here, cols in places(unit):
            dq_ref[:, cols] = (total[here] * SCALE).astype(jnp.bfloat16)
        q = stacked(q_ref, unit)
        g = g_refs[slot][...]
        for total_ref, left, right in (
            (dk2_ref, doubled(q), d_ref[:, two]),
            (dk_ref, q, d_ref[:, rest]),
            (dv2_ref, doubled(g), p_ref[:, two]),
            (dv_ref, g, p_ref[:, rest]),
        ):
            term = dot(left.T, right)
            total_ref[...] = term if unit == 0 else total_ref[...] + term

    def send(unit, scratch_ref, full_ref, at):
        part = slice(unit * UNIT * HEAD_SIZE, (unit + 1) * UNIT * HEAD_SIZE)
        place = slice(head * wide + part.start, head * wide + part.stop)
        copy = pltpu.make_async_copy(scratch_ref.at[:, part], full_ref.at[:, place], sem.at[at])
        copy.start()
        return copy

    q_copy.wait()
    old_copy.wait()
    scores(0, 0)
    bias_copy.wait()
    sent = []
    for unit in range(units):
        slot = unit % 2
        if unit + 1 < units:
            scores(unit + 1, 1 - slot)
        if unit > 0:
            score_grad(1 - slot)
        softmax(slot)
        if unit > 0:
            spread(unit - 1, 1 - slot)
            sent.append(send(unit - 1, dq_ref, dq_full_ref, 2 + 2 * (unit - 1)))
        if unit == 0:
            g_copy.wait()
        mix(unit, slot)
        sent.append(send(unit, out_ref, out_full_ref, 3 + 2 * unit))
    score_grad((units - 1) % 2)
    spread(units - 1, (units - 1) % 2)
    sent.append(send(units - 1, dq_ref, dq_full_ref, 2 * units))
    for span, grad, grad2, scale in ((key_out, dk_ref, dk2_ref, SCALE), (value_out, dv_ref, dv2_ref, 1.0)):
        either = grad2[:HEAD_SIZE].T * scale
        own = grad2[HEAD_SIZE:].T * scale
        dbehind_ref[0, :, span] = (grad[:, :rows].T * scale).astype(jnp.bfloat16)
        dbehind_ref[1, :, span] = jnp.where(from_far, either, 0.0).astype(jnp.bfloat16)
        dnear_ref[:, span] = grad[:, rows:].T * scale
        down_ref[:, span] = own + jnp.where(from_far, 0.0, either)
    for copy in sent:
        copy.wait()


def attention(head, queries, out_grad, blocks, place, grads, masks):
    rows = queries.shape[0]
    wide = GROUP * HEAD_SIZE
    pair = 2 * HEAD_SIZE
    window = (SPAN - 1) * rows
    query_spec = pl.BlockSpec(memory_space=pltpu.HBM)

    def whole(shape):
        return pl.BlockSpec(shape, lambda i, *_: (0,) * len(shape))

    fore = blocks[-1].shape[1] // pair
    where = [head, *(at * HEAD_SIZE for at in (place, fore + place, 0, 1))]
    operands = [queries, out_grad, *blocks, *masks]
    in_specs = [query_spec] * 2 + [pl.BlockSpec(memory_space=pl.ANY)] * 6
    aliases = {}
    for at, array in enumerate(grads):
        if array is not None:
            aliases[len(operands)] = at
            operands.append(array)
            in_specs.append(query_spec)
    bf16, f32 = jnp.bfloat16, jnp.float32
    results = pl.pallas_call(
        functools.partial(attention_kernel, where),
        out_shape=[
            jax.ShapeDtypeStruct(queries.shape, bf16),
            jax.ShapeDtypeStruct(queries.shape, bf16),
            jax.ShapeDtypeStruct((2, rows, pair), bf16),
            jax.ShapeDtypeStruct((rows, pair), f32),
            jax.ShapeDtypeStruct((rows, pair), f32),
        ],
        grid_spec=pltpu.PrefetchScalarGridSpec(
            num_scalar_prefetch=0,
            grid=(1,),
            in_specs=in_specs,
            out_specs=[query_spec] * 2
            + [whole((2, rows, pair)), whole((rows, pair)), whole((rows, pair))],
            scratch_shapes=[
                pltpu.VMEM(shape, kind)
                for shape, kind, count in (
                    ((2 * rows, HEAD_SIZE), bf16, 2),
                    ((HEAD_SIZE, 2 * rows), bf16, 2),
                    ((rows, pair), bf16, 2),
                    ((pair, rows), bf16, 2),
                    ((HEAD_SIZE, 2 * rows), f32, 2),
                    ((pair, rows), f32, 2),
                    ((UNIT * rows, window), f32, 2),
                    ((UNIT * rows, window), bf16, 2),
                    ((UNIT * rows, window), f32, 2),
                    ((UNIT * rows, window), bf16, 2),
                    ((UNIT * rows, HEAD_SIZE), bf16, 2),
                    ((UNIT * rows, HEAD_SIZE), f32, 2),
                    ((UNIT * rows, HEAD_SIZE), f32, 1),
                )
                for _ in range(count)
            ]
            + [pltpu.VMEM((rows, wide), bf16)] * 4
            + [pltpu.VMEM(array.shape, array.dtype) for array in (*blocks, *masks)]
            + [pltpu.SemaphoreType.DMA((2 + 2 * GROUP // UNIT,)), pltpu.SemaphoreType.DMA((6,))],
        ),
        input_output_aliases=aliases,
        compiler_params=pltpu.CompilerParams(vmem_limit_bytes=51 * 1024 * 1024),
        cost_estimate=pl.CostEstimate(
            flops=12 * rows * GROUP * window * HEAD_SIZE * 2,
            bytes_accessed=4 * rows * wide * 2 + 22 * rows * pair,
            transcendentals=0,
        ),
        name="attention",
    )(*operands)
    return results[:2], results[2:]


def origin(rank, *_):
    return (0,) * rank


def pack_kernel(first_ref, keys_full_ref, values_full_ref, lengths_full_ref, *refs):
    *refs, keys_ref, values_ref, lengths_ref, sem = refs
    copies = [
        pltpu.make_async_copy(full, here, sem.at[at])
        for at, (full, here) in enumerate(
            ((lengths_full_ref, lengths_ref), (keys_full_ref, keys_ref), (values_full_ref, values_ref))
        )
    ]
    for copy in copies:
        copy.start()
    copies[0].wait()
    write_masks(*refs[-3:], lengths_ref, first_ref, keys_ref.shape[0])
    copies[1].wait()
    copies[2].wait()
    for at, heads in enumerate(FORWARD):
        span = slice(heads[0] * HEAD_SIZE, (heads[-1] + 1) * HEAD_SIZE)
        width = span.stop - span.start
        own_ref, pair_ref = refs[2 * at : 2 * at + 2]
        for target_ref in (own_ref, pair_ref.at[0]):
            target_ref[:, :width] = keys_ref[:, span]
            target_ref[:, width:] = values_ref[:, span]


def pack(first, lengths, keys, values):
    rows = keys.shape[0]
    shapes = []
    for heads in FORWARD:
        own = (rows, 2 * HEAD_SIZE * len(heads))
        shapes += [jax.ShapeDtypeStruct(own, keys.dtype), jax.ShapeDtypeStruct((2, *own), keys.dtype)]
    specs = [
        pl.BlockSpec((1,) * (len(packed.shape) - 2) + packed.shape[-2:], functools.partial(origin, len(packed.shape)))
        for packed in shapes
    ]
    masks = [
        jax.ShapeDtypeStruct((rows, (SPAN - 1) * rows), jnp.float32),
        jax.ShapeDtypeStruct((rows, HEAD_SIZE), jnp.float32),
        jax.ShapeDtypeStruct((8, HEAD_SIZE), jnp.int32),
    ]
    two = functools.partial(origin, 2)
    results = pl.pallas_call(
        pack_kernel,
        out_shape=shapes + masks,
        grid_spec=pltpu.PrefetchScalarGridSpec(
            num_scalar_prefetch=1,
            grid=(1,),
            in_specs=[pl.BlockSpec(memory_space=pltpu.HBM)] * 3,
            out_specs=specs + [pl.BlockSpec(mask.shape, two) for mask in masks],
            scratch_shapes=[
                pltpu.VMEM(keys.shape, keys.dtype),
                pltpu.VMEM(values.shape, values.dtype),
                pltpu.SMEM(lengths.shape, lengths.dtype),
                pltpu.SemaphoreType.DMA((3,)),
            ],
        ),
        compiler_params=pltpu.CompilerParams(vmem_limit_bytes=12 * 1024 * 1024),
        name="pack",
    )(first, keys, values, lengths)
    packed = results[: len(shapes)]
    return packed[0::2], packed[1::2], results[len(shapes) :]


def local(queries, keys, values, out_grad, doc_lengths):
    rows = queries.shape[0]
    index = lax.axis_index(AXES)
    first = (index * rows).astype(jnp.int32).reshape(1)
    bf16, f32 = jnp.bfloat16, jnp.float32
    blocks, nears = {}, []
    owns, pairs, masks = pack(first, doc_lengths, keys, values)
    for own in owns:
        nears.append(passed_along(own, 1))
    pairs = [pair.at[1].set(near) for pair, near in zip(pairs, nears)]
    for heads, own, near, pair in zip(FORWARD, owns, nears, pairs):
        behind = passed_along(pair, 2)
        for place, head in enumerate(heads):
            blocks[head] = ((behind, near, own), place)
    grads = (None, None)
    parts = []

    def attend(head, after=()):
        nonlocal grads
        (behind, near, own), place = blocks[head]
        own, *after = lax.optimization_barrier((own, *after))
        grads, part = attention(head, queries, out_grad, (behind, near, own), place, grads, masks)
        parts.append(list(part))
        return after

    def second_hop(near, own, got):
        got = got.astype(f32)
        return (near + got[1]).astype(bf16), own + got[0]

    attend(0, pairs)
    gots = [passed_along(parts[0][0], -2)]
    attend(1)
    gots.append(passed_along(parts[1][0], -2))
    gots[0], _ = lax.optimization_barrier((gots[0], parts[1][0]))
    nears, owns = zip(second_hop(*parts[0][1:], gots[0]))
    (nears,) = attend(2, nears)
    gots.append(passed_along(parts[2][0], -2))
    gots[1], _ = lax.optimization_barrier((gots[1], parts[2][0]))
    more = second_hop(*parts[1][1:], gots[1])
    (nears, *more) = attend(3, (nears, *more))
    gots[2], near = lax.optimization_barrier((gots[2], parts[3][1]))
    gots.append(passed_along(parts[3][0], -2))
    parts[3][1] = near
    rest = [second_hop(*part[1:], got) for part, got in zip(parts[2:], gots[2:])]
    nears, owns = zip((nears, *owns), more, *rest)
    last = [passed_along(jnp.concatenate(nears[at : at + 2], axis=1), -1) for at in (0, 2)]
    total = (jnp.concatenate(owns, axis=1) + jnp.concatenate(last, axis=1).astype(f32)).astype(bf16)
    columns = [total[:, at : at + HEAD_SIZE] for at in range(0, total.shape[1], HEAD_SIZE)]
    return (
        grads[0],
        grads[1],
        jnp.concatenate(columns[0::2], axis=1),
        jnp.concatenate(columns[1::2], axis=1),
    )


def solution(mesh):
    spec = P(AXES, None)
    return jax.shard_map(
        local,
        mesh=mesh,
        in_specs=(spec, spec, spec, spec, P()),
        out_specs=(spec, spec, spec, spec),
        check_vma=False,
    )
```

```python
import functools
import math

import jax
import jax.numpy as jnp
from jax import lax
from jax.experimental import pallas as pl
from jax.experimental.pallas import tpu as pltpu
from jax.sharding import PartitionSpec as P

HEAD_SIZE = 128
QUERY_HEADS = 32
KEY_VALUE_HEADS = 4
GROUP = QUERY_HEADS // KEY_VALUE_HEADS
SPAN = 4
AXES = ("blk", "inner")
ROWS = 32
UNIT = 4
FORWARD = ((0,), (1,), (2, 3))
OUTS = 5
SCRATCH = 30
MASKED = -1e30
SCALE = 1.0 / math.sqrt(HEAD_SIZE)
EXP2_SCALE = SCALE * math.log2(math.e)

NN = (((1,), (0,)), ((), ()))


def dot(a, b, dims=NN):
    return lax.dot_general(a, b, dims, preferred_element_type=jnp.float32)


def device_count():
    return lax.axis_size("blk") * lax.axis_size("inner")


def passed_along(value, steps):
    count = device_count()
    first, last = (max(0, -steps), min(count, count - steps))
    return lax.ppermute(value, AXES, [(source, source + steps) for source in range(first, last)])


def write_masks(bias_ref, old_ref, cut_ref, lengths_ref, first_ref, rows):
    docs = lengths_ref.shape[0]
    first = first_ref[0]
    row = lax.broadcasted_iota(jnp.int32, (rows, 128), 0)
    query_pos = first + row

    def step(doc, carry):
        end, start = carry
        end = end + lengths_ref[doc]
        return end, jnp.where(query_pos >= end, end, start)

    _, start = lax.fori_loop(0, docs, step, (jnp.int32(0), jnp.zeros((rows, 128), jnp.int32)))
    lane = lax.broadcasted_iota(jnp.int32, (rows, 128), 1)
    old = start < first - (SPAN - 2) * rows
    old_ref[...] = jnp.where(old, 1.0, 0.0)
    cut = jnp.min(jnp.where(old, start - (first - (SPAN - 1) * rows), rows), axis=0, keepdims=True)
    cut_ref[...] = jnp.broadcast_to(cut, cut_ref.shape)
    cut = jnp.broadcast_to(cut, (rows, 128))
    for part in range((SPAN - 1) * rows // 128):
        offset = part * 128 + lane
        if part < rows // 128:
            own = (offset <= row) & ((first + offset >= start) | (old & (offset < cut)))
            allowed = own | (old & (offset >= cut))
        else:
            allowed = first - (SPAN - 1) * rows + offset >= start
        bias_ref[:, part * 128 : (part + 1) * 128] = jnp.where(allowed, 0.0, MASKED)


def attention_kernel(where, q_ref, g_ref, behind_ref, near_ref, own_ref, bias_ref, old_ref, cut_ref, *refs):
    out_ref, dq_ref, dbehind_ref, dnear_ref, down_ref = refs[-(OUTS + SCRATCH) : -SCRATCH]
    (
        key_ref, value_ref, key_t_ref, value_t_ref, key2_ref, value2_ref, key2_t_ref, value2_t_ref,
        dk_ref, dv_ref, dk2_ref, dv2_ref, *slots,
    ) = refs[-SCRATCH:]
    slots, copies = slots[:13], slots[13:]
    s_refs, p_refs, dp_refs, d_refs, g_refs, delta_refs = (slots[i : i + 2] for i in range(0, 12, 2))
    (inv_ref,) = slots[12:]
    head, *offsets = where
    key_in, value_in, key_out, value_out = (slice(at, at + HEAD_SIZE) for at in offsets)
    q_full_ref, g_full_ref, out_full_ref, dq_full_ref = q_ref, g_ref, out_ref, dq_ref
    q_ref, g_ref, out_ref, dq_ref, sem = copies
    rows, wide = q_ref.shape
    mine = slice(head * wide, (head + 1) * wide)
    q_copy = pltpu.make_async_copy(q_full_ref.at[:, mine], q_ref, sem.at[0])
    g_copy = pltpu.make_async_copy(g_full_ref.at[:, mine], g_ref, sem.at[1])
    q_copy.start()
    g_copy.start()
    window = (SPAN - 1) * rows
    units = GROUP // UNIT
    stack = UNIT * rows
    two = slice(0, rows)
    rest = slice(rows, window)

    from_far = lax.broadcasted_iota(jnp.int32, (rows, HEAD_SIZE), 0) >= cut_ref[0, 0]
    mid, far, near, own = behind_ref.at[0], behind_ref.at[1], near_ref, own_ref
    for j, block in enumerate((mid, near)):
        span = slice(j * rows, (j + 1) * rows)
        key_ref[span] = block[:, key_in]
        value_ref[span] = block[:, value_in]
        key_t_ref[:, span] = block[:, key_in].T
        value_t_ref[:, span] = block[:, value_in].T
    for which, plain_ref, turned_ref in ((key_in, key2_ref, key2_t_ref), (value_in, value2_ref, value2_t_ref)):
        mine = own[:, which]
        either = jnp.where(from_far, far[:, which].astype(jnp.float32), mine.astype(jnp.float32))
        for j, block in enumerate((either.astype(jnp.bfloat16), mine)):
            span = slice(j * HEAD_SIZE, (j + 1) * HEAD_SIZE)
            plain_ref[:, span] = block
            turned_ref[span] = block.T

    def places(unit):
        return [
            (
                slice(i * rows, (i + 1) * rows),
                slice((unit * UNIT + i) * HEAD_SIZE, (unit * UNIT + i + 1) * HEAD_SIZE),
            )
            for i in range(UNIT)
        ]

    def stacked(ref, unit):
        return jnp.concatenate([ref[:, cols] for _, cols in places(unit)], axis=0)

    def doubled(x):
        old = jnp.concatenate([old_ref[...].astype(jnp.bfloat16)] * UNIT, axis=0)
        return jnp.concatenate([x * old, x * (1 - old)], axis=1)

    def picked(x):
        old = jnp.concatenate([old_ref[...]] * UNIT, axis=0)
        return jnp.where(old > 0.5, x[:, :HEAD_SIZE], x[:, HEAD_SIZE:])

    def scores(unit, slot):
        q = stacked(q_ref, unit)
        s_refs[slot][:, two] = dot(doubled(q), key2_t_ref[...])
        s_refs[slot][:, rest] = dot(q, key_t_ref[...])

    def softmax(slot):
        for r in range(0, stack, ROWS):
            here = slice(r, r + ROWS)
            row = slice(r % rows, r % rows + ROWS)
            s = s_refs[slot][here] * EXP2_SCALE + bias_ref[row]
            e = jnp.exp2(s - jnp.max(s, axis=1, keepdims=True))
            inv = 1.0 / jnp.sum(e, axis=1, keepdims=True)
            inv_ref[here] = jnp.broadcast_to(inv, (ROWS, HEAD_SIZE))
            p_refs[slot][here] = e.astype(jnp.bfloat16)

    def mix(unit, slot):
        p_ref, g_ref_here = p_refs[slot], g_refs[slot]
        total = picked(dot(p_ref[:, two], value2_ref[...])) + dot(p_ref[:, rest], value_ref[...])
        for here, cols in places(unit):
            inv = inv_ref[here]
            out = (total[here] * inv).astype(jnp.bfloat16)
            out_ref[:, cols] = out
            g = g_ref[:, cols].astype(jnp.float32) * inv
            delta = jnp.sum(g * out.astype(jnp.float32), axis=1, keepdims=True)
            delta_refs[slot][here] = jnp.broadcast_to(delta, (rows, HEAD_SIZE))
            g_ref_here[here] = g.astype(jnp.bfloat16)
        g = g_ref_here[...]
        dp_refs[slot][:, two] = dot(doubled(g), value2_t_ref[...])
        dp_refs[slot][:, rest] = dot(g, value_t_ref[...])

    def score_grad(slot):
        for r in range(0, stack, ROWS):
            here = slice(r, r + ROWS)
            delta = jnp.concatenate([delta_refs[slot][here]] * (window // HEAD_SIZE), axis=1)
            d_refs[slot][here] = p_refs[slot][here] * (dp_refs[slot][here] - delta).astype(jnp.bfloat16)

    def spread(unit, slot):
        p_ref, d_ref = p_refs[slot], d_refs[slot]
        total = picked(dot(d_ref[:, two], key2_ref[...])) + dot(d_ref[:, rest], key_ref[...])
        for here, cols in places(unit):
            dq_ref[:, cols] = (total[here] * SCALE).astype(jnp.bfloat16)
        q = stacked(q_ref, unit)
        g = g_refs[slot][...]
        for total_ref, left, right in (
            (dk2_ref, doubled(q), d_ref[:, two]),
            (dk_ref, q, d_ref[:, rest]),
            (dv2_ref, doubled(g), p_ref[:, two]),
            (dv_ref, g, p_ref[:, rest]),
        ):
            term = dot(left.T, right)
            total_ref[...] = term if unit == 0 else total_ref[...] + term

    def send(unit, scratch_ref, full_ref, at):
        part = slice(unit * UNIT * HEAD_SIZE, (unit + 1) * UNIT * HEAD_SIZE)
        place = slice(head * wide + part.start, head * wide + part.stop)
        copy = pltpu.make_async_copy(scratch_ref.at[:, part], full_ref.at[:, place], sem.at[at])
        copy.start()
        return copy

    q_copy.wait()
    scores(0, 0)
    sent = []
    for unit in range(units):
        slot = unit % 2
        if unit + 1 < units:
            scores(unit + 1, 1 - slot)
        if unit > 0:
            score_grad(1 - slot)
        softmax(slot)
        if unit > 0:
            spread(unit - 1, 1 - slot)
            sent.append(send(unit - 1, dq_ref, dq_full_ref, 2 + 2 * (unit - 1)))
        if unit == 0:
            g_copy.wait()
        mix(unit, slot)
        sent.append(send(unit, out_ref, out_full_ref, 3 + 2 * unit))
    score_grad((units - 1) % 2)
    spread(units - 1, (units - 1) % 2)
    sent.append(send(units - 1, dq_ref, dq_full_ref, 2 * units))
    for span, grad, grad2, scale in ((key_out, dk_ref, dk2_ref, SCALE), (value_out, dv_ref, dv2_ref, 1.0)):
        either = grad2[:HEAD_SIZE].T * scale
        own = grad2[HEAD_SIZE:].T * scale
        dbehind_ref[0, :, span] = (grad[:, :rows].T * scale).astype(jnp.bfloat16)
        dbehind_ref[1, :, span] = jnp.where(from_far, either, 0.0).astype(jnp.bfloat16)
        dnear_ref[:, span] = grad[:, rows:].T * scale
        down_ref[:, span] = own + jnp.where(from_far, 0.0, either)
    for copy in sent:
        copy.wait()


def attention(head, queries, out_grad, blocks, place, grads, masks):
    rows = queries.shape[0]
    wide = GROUP * HEAD_SIZE
    pair = 2 * HEAD_SIZE
    window = (SPAN - 1) * rows
    query_spec = pl.BlockSpec(memory_space=pltpu.HBM)

    def whole(shape):
        return pl.BlockSpec(shape, lambda i, *_: (0,) * len(shape))

    fore = blocks[-1].shape[1] // pair
    where = [head, *(at * HEAD_SIZE for at in (place, fore + place, 0, 1))]
    operands = [queries, out_grad, *blocks, *masks]
    in_specs = [query_spec] * 2 + [whole(array.shape) for array in (*blocks, *masks)]
    aliases = {}
    for at, array in enumerate(grads):
        if array is not None:
            aliases[len(operands)] = at
            operands.append(array)
            in_specs.append(query_spec)
    bf16, f32 = jnp.bfloat16, jnp.float32
    results = pl.pallas_call(
        functools.partial(attention_kernel, where),
        out_shape=[
            jax.ShapeDtypeStruct(queries.shape, bf16),
            jax.ShapeDtypeStruct(queries.shape, bf16),
            jax.ShapeDtypeStruct((2, rows, pair), bf16),
            jax.ShapeDtypeStruct((rows, pair), f32),
            jax.ShapeDtypeStruct((rows, pair), f32),
        ],
        grid_spec=pltpu.PrefetchScalarGridSpec(
            num_scalar_prefetch=0,
            grid=(1,),
            in_specs=in_specs,
            out_specs=[query_spec] * 2
            + [whole((2, rows, pair)), whole((rows, pair)), whole((rows, pair))],
            scratch_shapes=[
                pltpu.VMEM(shape, kind)
                for shape, kind, count in (
                    ((2 * rows, HEAD_SIZE), bf16, 2),
                    ((HEAD_SIZE, 2 * rows), bf16, 2),
                    ((rows, pair), bf16, 2),
                    ((pair, rows), bf16, 2),
                    ((HEAD_SIZE, 2 * rows), f32, 2),
                    ((pair, rows), f32, 2),
                    ((UNIT * rows, window), f32, 2),
                    ((UNIT * rows, window), bf16, 2),
                    ((UNIT * rows, window), f32, 2),
                    ((UNIT * rows, window), bf16, 2),
                    ((UNIT * rows, HEAD_SIZE), bf16, 2),
                    ((UNIT * rows, HEAD_SIZE), f32, 2),
                    ((UNIT * rows, HEAD_SIZE), f32, 1),
                )
                for _ in range(count)
            ]
            + [pltpu.VMEM((rows, wide), bf16)] * 4
            + [pltpu.SemaphoreType.DMA((2 + 2 * GROUP // UNIT,))],
        ),
        input_output_aliases=aliases,
        compiler_params=pltpu.CompilerParams(vmem_limit_bytes=48 * 1024 * 1024),
        cost_estimate=pl.CostEstimate(
            flops=12 * rows * GROUP * window * HEAD_SIZE * 2,
            bytes_accessed=4 * rows * wide * 2 + 22 * rows * pair,
            transcendentals=0,
        ),
        name="attention",
    )(*operands)
    return results[:2], results[2:]


def origin(rank, *_):
    return (0,) * rank


def pack_kernel(first_ref, lengths_ref, keys_ref, values_ref, *refs):
    write_masks(*refs[-3:], lengths_ref, first_ref, keys_ref.shape[0])
    for at, heads in enumerate(FORWARD):
        span = slice(heads[0] * HEAD_SIZE, (heads[-1] + 1) * HEAD_SIZE)
        width = span.stop - span.start
        own_ref, pair_ref = refs[2 * at : 2 * at + 2]
        for target_ref in (own_ref, pair_ref.at[0]):
            target_ref[:, :width] = keys_ref[:, span]
            target_ref[:, width:] = values_ref[:, span]


def pack(first, lengths, keys, values):
    rows = keys.shape[0]
    shapes = []
    for heads in FORWARD:
        own = (rows, 2 * HEAD_SIZE * len(heads))
        shapes += [jax.ShapeDtypeStruct(own, keys.dtype), jax.ShapeDtypeStruct((2, *own), keys.dtype)]
    specs = [
        pl.BlockSpec((1,) * (len(packed.shape) - 2) + packed.shape[-2:], functools.partial(origin, len(packed.shape)))
        for packed in shapes
    ]
    masks = [
        jax.ShapeDtypeStruct((rows, (SPAN - 1) * rows), jnp.float32),
        jax.ShapeDtypeStruct((rows, HEAD_SIZE), jnp.float32),
        jax.ShapeDtypeStruct((8, HEAD_SIZE), jnp.int32),
    ]
    two = functools.partial(origin, 2)
    results = pl.pallas_call(
        pack_kernel,
        out_shape=shapes + masks,
        grid_spec=pltpu.PrefetchScalarGridSpec(
            num_scalar_prefetch=2,
            grid=(1,),
            in_specs=[pl.BlockSpec(keys.shape, two)] * 2,
            out_specs=specs + [pl.BlockSpec(mask.shape, two) for mask in masks],
        ),
        compiler_params=pltpu.CompilerParams(vmem_limit_bytes=12 * 1024 * 1024),
        name="pack",
    )(first, lengths, keys, values)
    packed = results[: len(shapes)]
    return packed[0::2], packed[1::2], results[len(shapes) :]


def local(queries, keys, values, out_grad, doc_lengths):
    rows = queries.shape[0]
    index = lax.axis_index(AXES)
    first = (index * rows).astype(jnp.int32).reshape(1)
    bf16, f32 = jnp.bfloat16, jnp.float32
    blocks, nears = {}, []
    owns, pairs, masks = pack(first, doc_lengths, keys, values)
    for own in owns:
        nears.append(passed_along(own, 1))
    pairs = [pair.at[1].set(near) for pair, near in zip(pairs, nears)]
    for heads, own, near, pair in zip(FORWARD, owns, nears, pairs):
        behind = passed_along(pair, 2)
        for place, head in enumerate(heads):
            blocks[head] = ((behind, near, own), place)
    grads = (None, None)
    parts = []

    def attend(head, after=()):
        nonlocal grads
        (behind, near, own), place = blocks[head]
        own, *after = lax.optimization_barrier((own, *after))
        grads, part = attention(head, queries, out_grad, (behind, near, own), place, grads, masks)
        parts.append(list(part))
        return after

    def second_hop(near, own, got):
        got = got.astype(f32)
        return (near + got[1]).astype(bf16), own + got[0]

    attend(0, pairs)
    gots = [passed_along(parts[0][0], -2)]
    attend(1)
    gots.append(passed_along(parts[1][0], -2))
    gots[0], _ = lax.optimization_barrier((gots[0], parts[1][0]))
    nears, owns = zip(second_hop(*parts[0][1:], gots[0]))
    (nears,) = attend(2, nears)
    gots.append(passed_along(parts[2][0], -2))
    gots[1], _ = lax.optimization_barrier((gots[1], parts[2][0]))
    more = second_hop(*parts[1][1:], gots[1])
    (nears, *more) = attend(3, (nears, *more))
    gots[2], near = lax.optimization_barrier((gots[2], parts[3][1]))
    gots.append(passed_along(parts[3][0], -2))
    parts[3][1] = near
    rest = [second_hop(*part[1:], got) for part, got in zip(parts[2:], gots[2:])]
    nears, owns = zip((nears, *owns), more, *rest)
    last = [passed_along(jnp.concatenate(nears[at : at + 2], axis=1), -1) for at in (0, 2)]
    total = (jnp.concatenate(owns, axis=1) + jnp.concatenate(last, axis=1).astype(f32)).astype(bf16)
    columns = [total[:, at : at + HEAD_SIZE] for at in range(0, total.shape[1], HEAD_SIZE)]
    return (
        grads[0],
        grads[1],
        jnp.concatenate(columns[0::2], axis=1),
        jnp.concatenate(columns[1::2], axis=1),
    )


def solution(mesh):
    spec = P(AXES, None)
    return jax.shard_map(
        local,
        mesh=mesh,
        in_specs=(spec, spec, spec, spec, P()),
        out_specs=(spec, spec, spec, spec),
        check_vma=False,
    )
```

```python
import functools
import math

import jax
import jax.numpy as jnp
from jax import lax
from jax.experimental import pallas as pl
from jax.experimental.pallas import tpu as pltpu
from jax.sharding import PartitionSpec as P

HEAD_SIZE = 128
QUERY_HEADS = 32
KEY_VALUE_HEADS = 4
GROUP = QUERY_HEADS // KEY_VALUE_HEADS
SPAN = 4
AXES = ("blk", "inner")
ROWS = 32
UNIT = 4
FORWARD = ((0,), (1,), (2, 3))
OUTS = 5
SCRATCH = 30
MASKED = -1e30
SCALE = 1.0 / math.sqrt(HEAD_SIZE)
EXP2_SCALE = SCALE * math.log2(math.e)

NN = (((1,), (0,)), ((), ()))


def dot(a, b, dims=NN):
    return lax.dot_general(a, b, dims, preferred_element_type=jnp.float32)


def device_count():
    return lax.axis_size("blk") * lax.axis_size("inner")


def passed_along(value, steps):
    count = device_count()
    first, last = (max(0, -steps), min(count, count - steps))
    return lax.ppermute(value, AXES, [(source, source + steps) for source in range(first, last)])


def write_masks(bias_ref, old_ref, cut_ref, lengths_ref, first_ref, rows):
    docs = lengths_ref.shape[0]
    first = first_ref[0]
    row = lax.broadcasted_iota(jnp.int32, (rows, 128), 0)
    query_pos = first + row

    def step(doc, carry):
        end, start = carry
        end = end + lengths_ref[doc]
        return end, jnp.where(query_pos >= end, end, start)

    _, start = lax.fori_loop(0, docs, step, (jnp.int32(0), jnp.zeros((rows, 128), jnp.int32)))
    lane = lax.broadcasted_iota(jnp.int32, (rows, 128), 1)
    old = start < first - (SPAN - 2) * rows
    old_ref[...] = jnp.where(old, 1.0, 0.0)
    cut = jnp.min(jnp.where(old, start - (first - (SPAN - 1) * rows), rows), axis=0, keepdims=True)
    cut_ref[...] = jnp.broadcast_to(cut, cut_ref.shape)
    cut = jnp.broadcast_to(cut, (rows, 128))
    for part in range((SPAN - 1) * rows // 128):
        offset = part * 128 + lane
        if part < rows // 128:
            own = (offset <= row) & ((first + offset >= start) | (old & (offset < cut)))
            allowed = own | (old & (offset >= cut))
        else:
            allowed = first - (SPAN - 1) * rows + offset >= start
        bias_ref[:, part * 128 : (part + 1) * 128] = jnp.where(allowed, 0.0, MASKED)


def attention_kernel(where, q_ref, g_ref, behind_ref, near_ref, own_ref, bias_ref, old_ref, cut_ref, *refs):
    out_ref, dq_ref, dbehind_ref, dnear_ref, down_ref = refs[-(OUTS + SCRATCH) : -SCRATCH]
    (
        key_ref, value_ref, key_t_ref, value_t_ref, key2_ref, value2_ref, key2_t_ref, value2_t_ref,
        dk_ref, dv_ref, dk2_ref, dv2_ref, *slots,
    ) = refs[-SCRATCH:]
    slots, copies = slots[:13], slots[13:]
    s_refs, p_refs, dp_refs, d_refs, g_refs, delta_refs = (slots[i : i + 2] for i in range(0, 12, 2))
    (inv_ref,) = slots[12:]
    head, *offsets = where
    key_in, value_in, key_out, value_out = (slice(at, at + HEAD_SIZE) for at in offsets)
    q_full_ref, g_full_ref, out_full_ref, dq_full_ref = q_ref, g_ref, out_ref, dq_ref
    q_ref, g_ref, out_ref, dq_ref, sem = copies
    rows, wide = q_ref.shape
    mine = slice(head * wide, (head + 1) * wide)
    q_copy = pltpu.make_async_copy(q_full_ref.at[:, mine], q_ref, sem.at[0])
    g_copy = pltpu.make_async_copy(g_full_ref.at[:, mine], g_ref, sem.at[1])
    q_copy.start()
    g_copy.start()
    window = (SPAN - 1) * rows
    units = GROUP // UNIT
    stack = UNIT * rows
    two = slice(0, rows)
    rest = slice(rows, window)

    from_far = lax.broadcasted_iota(jnp.int32, (rows, HEAD_SIZE), 0) >= cut_ref[0, 0]
    mid, far, near, own = behind_ref.at[0], behind_ref.at[1], near_ref, own_ref
    for j, block in enumerate((mid, near)):
        span = slice(j * rows, (j + 1) * rows)
        key_ref[span] = block[:, key_in]
        value_ref[span] = block[:, value_in]
        key_t_ref[:, span] = block[:, key_in].T
        value_t_ref[:, span] = block[:, value_in].T
    for which, plain_ref, turned_ref in ((key_in, key2_ref, key2_t_ref), (value_in, value2_ref, value2_t_ref)):
        mine = own[:, which]
        either = jnp.where(from_far, far[:, which].astype(jnp.float32), mine.astype(jnp.float32))
        for j, block in enumerate((either.astype(jnp.bfloat16), mine)):
            span = slice(j * HEAD_SIZE, (j + 1) * HEAD_SIZE)
            plain_ref[:, span] = block
            turned_ref[span] = block.T

    def places(unit):
        return [
            (
                slice(i * rows, (i + 1) * rows),
                slice((unit * UNIT + i) * HEAD_SIZE, (unit * UNIT + i + 1) * HEAD_SIZE),
            )
            for i in range(UNIT)
        ]

    def stacked(ref, unit):
        return jnp.concatenate([ref[:, cols] for _, cols in places(unit)], axis=0)

    def doubled(x):
        old = jnp.concatenate([old_ref[...].astype(jnp.bfloat16)] * UNIT, axis=0)
        return jnp.concatenate([x * old, x * (1 - old)], axis=1)

    def picked(x):
        old = jnp.concatenate([old_ref[...]] * UNIT, axis=0)
        return jnp.where(old > 0.5, x[:, :HEAD_SIZE], x[:, HEAD_SIZE:])

    def scores(unit, slot):
        q = stacked(q_ref, unit)
        s_refs[slot][:, two] = dot(doubled(q), key2_t_ref[...])
        s_refs[slot][:, rest] = dot(q, key_t_ref[...])

    def softmax(slot):
        for r in range(0, stack, ROWS):
            here = slice(r, r + ROWS)
            row = slice(r % rows, r % rows + ROWS)
            s = s_refs[slot][here] * EXP2_SCALE + bias_ref[row]
            e = jnp.exp2(s - jnp.max(s, axis=1, keepdims=True))
            inv = 1.0 / jnp.sum(e, axis=1, keepdims=True)
            inv_ref[here] = jnp.broadcast_to(inv, (ROWS, HEAD_SIZE))
            p_refs[slot][here] = e.astype(jnp.bfloat16)

    def mix(unit, slot):
        p_ref, g_ref_here = p_refs[slot], g_refs[slot]
        total = picked(dot(p_ref[:, two], value2_ref[...])) + dot(p_ref[:, rest], value_ref[...])
        for here, cols in places(unit):
            inv = inv_ref[here]
            out = (total[here] * inv).astype(jnp.bfloat16)
            out_ref[:, cols] = out
            g = g_ref[:, cols].astype(jnp.float32) * inv
            delta = jnp.sum(g * out.astype(jnp.float32), axis=1, keepdims=True)
            delta_refs[slot][here] = jnp.broadcast_to(delta, (rows, HEAD_SIZE))
            g_ref_here[here] = g.astype(jnp.bfloat16)
        g = g_ref_here[...]
        dp_refs[slot][:, two] = dot(doubled(g), value2_t_ref[...])
        dp_refs[slot][:, rest] = dot(g, value_t_ref[...])

    def score_grad(slot):
        for r in range(0, stack, ROWS):
            here = slice(r, r + ROWS)
            delta = jnp.concatenate([delta_refs[slot][here]] * (window // HEAD_SIZE), axis=1)
            d_refs[slot][here] = p_refs[slot][here] * (dp_refs[slot][here] - delta).astype(jnp.bfloat16)

    def spread(unit, slot):
        p_ref, d_ref = p_refs[slot], d_refs[slot]
        total = picked(dot(d_ref[:, two], key2_ref[...])) + dot(d_ref[:, rest], key_ref[...])
        for here, cols in places(unit):
            dq_ref[:, cols] = (total[here] * SCALE).astype(jnp.bfloat16)
        q = stacked(q_ref, unit)
        g = g_refs[slot][...]
        for total_ref, left, right in (
            (dk2_ref, doubled(q), d_ref[:, two]),
            (dk_ref, q, d_ref[:, rest]),
            (dv2_ref, doubled(g), p_ref[:, two]),
            (dv_ref, g, p_ref[:, rest]),
        ):
            term = dot(left.T, right)
            total_ref[...] = term if unit == 0 else total_ref[...] + term

    def send(unit, scratch_ref, full_ref, at):
        part = slice(unit * UNIT * HEAD_SIZE, (unit + 1) * UNIT * HEAD_SIZE)
        place = slice(head * wide + part.start, head * wide + part.stop)
        copy = pltpu.make_async_copy(scratch_ref.at[:, part], full_ref.at[:, place], sem.at[at])
        copy.start()
        return copy

    q_copy.wait()
    scores(0, 0)
    sent = []
    for unit in range(units):
        slot = unit % 2
        if unit + 1 < units:
            scores(unit + 1, 1 - slot)
        if unit > 0:
            score_grad(1 - slot)
        softmax(slot)
        if unit > 0:
            spread(unit - 1, 1 - slot)
            sent.append(send(unit - 1, dq_ref, dq_full_ref, 2 + 2 * (unit - 1)))
        if unit == 0:
            g_copy.wait()
        mix(unit, slot)
        sent.append(send(unit, out_ref, out_full_ref, 3 + 2 * unit))
    score_grad((units - 1) % 2)
    spread(units - 1, (units - 1) % 2)
    sent.append(send(units - 1, dq_ref, dq_full_ref, 2 * units))
    for span, grad, grad2, scale in ((key_out, dk_ref, dk2_ref, SCALE), (value_out, dv_ref, dv2_ref, 1.0)):
        either = grad2[:HEAD_SIZE].T * scale
        own = grad2[HEAD_SIZE:].T * scale
        dbehind_ref[0, :, span] = (grad[:, :rows].T * scale).astype(jnp.bfloat16)
        dbehind_ref[1, :, span] = jnp.where(from_far, either, 0.0).astype(jnp.bfloat16)
        dnear_ref[:, span] = grad[:, rows:].T * scale
        down_ref[:, span] = own + jnp.where(from_far, 0.0, either)
    for copy in sent:
        copy.wait()


def attention(head, queries, out_grad, blocks, place, grads, masks):
    rows = queries.shape[0]
    wide = GROUP * HEAD_SIZE
    pair = 2 * HEAD_SIZE
    window = (SPAN - 1) * rows
    query_spec = pl.BlockSpec(memory_space=pltpu.HBM)

    def whole(shape):
        return pl.BlockSpec(shape, lambda i, *_: (0,) * len(shape))

    fore = blocks[-1].shape[1] // pair
    where = [head, *(at * HEAD_SIZE for at in (place, fore + place, 0, 1))]
    operands = [queries, out_grad, *blocks, *masks]
    in_specs = [query_spec] * 2 + [whole(array.shape) for array in (*blocks, *masks)]
    aliases = {}
    for at, array in enumerate(grads):
        if array is not None:
            aliases[len(operands)] = at
            operands.append(array)
            in_specs.append(query_spec)
    bf16, f32 = jnp.bfloat16, jnp.float32
    results = pl.pallas_call(
        functools.partial(attention_kernel, where),
        out_shape=[
            jax.ShapeDtypeStruct(queries.shape, bf16),
            jax.ShapeDtypeStruct(queries.shape, bf16),
            jax.ShapeDtypeStruct((2, rows, pair), bf16),
            jax.ShapeDtypeStruct((rows, pair), f32),
            jax.ShapeDtypeStruct((rows, pair), f32),
        ],
        grid_spec=pltpu.PrefetchScalarGridSpec(
            num_scalar_prefetch=0,
            grid=(1,),
            in_specs=in_specs,
            out_specs=[query_spec] * 2
            + [whole((2, rows, pair)), whole((rows, pair)), whole((rows, pair))],
            scratch_shapes=[
                pltpu.VMEM(shape, kind)
                for shape, kind, count in (
                    ((2 * rows, HEAD_SIZE), bf16, 2),
                    ((HEAD_SIZE, 2 * rows), bf16, 2),
                    ((rows, pair), bf16, 2),
                    ((pair, rows), bf16, 2),
                    ((HEAD_SIZE, 2 * rows), f32, 2),
                    ((pair, rows), f32, 2),
                    ((UNIT * rows, window), f32, 2),
                    ((UNIT * rows, window), bf16, 2),
                    ((UNIT * rows, window), f32, 2),
                    ((UNIT * rows, window), bf16, 2),
                    ((UNIT * rows, HEAD_SIZE), bf16, 2),
                    ((UNIT * rows, HEAD_SIZE), f32, 2),
                    ((UNIT * rows, HEAD_SIZE), f32, 1),
                )
                for _ in range(count)
            ]
            + [pltpu.VMEM((rows, wide), bf16)] * 4
            + [pltpu.SemaphoreType.DMA((2 + 2 * GROUP // UNIT,))],
        ),
        input_output_aliases=aliases,
        compiler_params=pltpu.CompilerParams(vmem_limit_bytes=48 * 1024 * 1024),
        cost_estimate=pl.CostEstimate(
            flops=12 * rows * GROUP * window * HEAD_SIZE * 2,
            bytes_accessed=4 * rows * wide * 2 + 22 * rows * pair,
            transcendentals=0,
        ),
        name="attention",
    )(*operands)
    return results[:2], results[2:]


def origin(rank, *_):
    return (0,) * rank


def pack_kernel(first_ref, lengths_ref, keys_ref, values_ref, *refs):
    write_masks(*refs[-3:], lengths_ref, first_ref, keys_ref.shape[0])
    for at, heads in enumerate(FORWARD):
        span = slice(heads[0] * HEAD_SIZE, (heads[-1] + 1) * HEAD_SIZE)
        width = span.stop - span.start
        own_ref, pair_ref = refs[2 * at : 2 * at + 2]
        for target_ref in (own_ref, pair_ref.at[0]):
            target_ref[:, :width] = keys_ref[:, span]
            target_ref[:, width:] = values_ref[:, span]


def pack(first, lengths, keys, values):
    rows = keys.shape[0]
    shapes = []
    for heads in FORWARD:
        own = (rows, 2 * HEAD_SIZE * len(heads))
        shapes += [jax.ShapeDtypeStruct(own, keys.dtype), jax.ShapeDtypeStruct((2, *own), keys.dtype)]
    specs = [
        pl.BlockSpec((1,) * (len(packed.shape) - 2) + packed.shape[-2:], functools.partial(origin, len(packed.shape)))
        for packed in shapes
    ]
    masks = [
        jax.ShapeDtypeStruct((rows, (SPAN - 1) * rows), jnp.float32),
        jax.ShapeDtypeStruct((rows, HEAD_SIZE), jnp.float32),
        jax.ShapeDtypeStruct((8, HEAD_SIZE), jnp.int32),
    ]
    two = functools.partial(origin, 2)
    results = pl.pallas_call(
        pack_kernel,
        out_shape=shapes + masks,
        grid_spec=pltpu.PrefetchScalarGridSpec(
            num_scalar_prefetch=2,
            grid=(1,),
            in_specs=[pl.BlockSpec(keys.shape, two)] * 2,
            out_specs=specs + [pl.BlockSpec(mask.shape, two) for mask in masks],
        ),
        compiler_params=pltpu.CompilerParams(vmem_limit_bytes=12 * 1024 * 1024),
        name="pack",
    )(first, lengths, keys, values)
    packed = results[: len(shapes)]
    return packed[0::2], packed[1::2], results[len(shapes) :]


def local(queries, keys, values, out_grad, doc_lengths):
    rows = queries.shape[0]
    index = lax.axis_index(AXES)
    first = (index * rows).astype(jnp.int32).reshape(1)
    bf16, f32 = jnp.bfloat16, jnp.float32
    blocks, nears = {}, []
    owns, pairs, masks = pack(first, doc_lengths, keys, values)
    for own in owns:
        nears.append(passed_along(own, 1))
    pairs = [pair.at[1].set(near) for pair, near in zip(pairs, nears)]
    for heads, own, near, pair in zip(FORWARD, owns, nears, pairs):
        behind = passed_along(pair, 2)
        for place, head in enumerate(heads):
            blocks[head] = ((behind, near, own), place)
    grads = (None, None)
    parts = []

    def attend(head, after=()):
        nonlocal grads
        (behind, near, own), place = blocks[head]
        own, *after = lax.optimization_barrier((own, *after))
        grads, part = attention(head, queries, out_grad, (behind, near, own), place, grads, masks)
        parts.append(list(part))
        return after

    def second_hop(near, own, got):
        got = got.astype(f32)
        return (near + got[1]).astype(bf16), own + got[0]

    attend(0, pairs)
    gots = [passed_along(parts[0][0], -2)]
    attend(1)
    gots.append(passed_along(parts[1][0], -2))
    attend(2)
    gots.append(passed_along(parts[2][0], -2))
    gots[0], gots[1], _ = lax.optimization_barrier((gots[0], gots[1], parts[2][0]))
    nears, owns = zip(second_hop(*parts[0][1:], gots[0]))
    more = second_hop(*parts[1][1:], gots[1])
    (nears, *more) = attend(3, (*nears, *more))
    gots[2], near = lax.optimization_barrier((gots[2], parts[3][1]))
    gots.append(passed_along(parts[3][0], -2))
    parts[3][1] = near
    rest = [second_hop(*part[1:], got) for part, got in zip(parts[2:], gots[2:])]
    nears, owns = zip((nears, *owns), more, *rest)
    last = [passed_along(jnp.concatenate(nears[at : at + 2], axis=1), -1) for at in (0, 2)]
    total = (jnp.concatenate(owns, axis=1) + jnp.concatenate(last, axis=1).astype(f32)).astype(bf16)
    columns = [total[:, at : at + HEAD_SIZE] for at in range(0, total.shape[1], HEAD_SIZE)]
    return (
        grads[0],
        grads[1],
        jnp.concatenate(columns[0::2], axis=1),
        jnp.concatenate(columns[1::2], axis=1),
    )


def solution(mesh):
    spec = P(AXES, None)
    return jax.shard_map(
        local,
        mesh=mesh,
        in_specs=(spec, spec, spec, spec, P()),
        out_specs=(spec, spec, spec, spec),
        check_vma=False,
    )
```

```python
import functools
import math

import jax
import jax.numpy as jnp
from jax import lax
from jax.experimental import pallas as pl
from jax.experimental.pallas import tpu as pltpu
from jax.sharding import PartitionSpec as P

HEAD_SIZE = 128
QUERY_HEADS = 32
KEY_VALUE_HEADS = 4
GROUP = QUERY_HEADS // KEY_VALUE_HEADS
SPAN = 4
AXES = ("blk", "inner")
ROWS = 32
UNIT = 4
FORWARD = ((0,), (1,), (2, 3))
OUTS = 5
SCRATCH = 30
MASKED = -1e30
SCALE = 1.0 / math.sqrt(HEAD_SIZE)
EXP2_SCALE = SCALE * math.log2(math.e)

NN = (((1,), (0,)), ((), ()))


def dot(a, b, dims=NN):
    return lax.dot_general(a, b, dims, preferred_element_type=jnp.float32)


def device_count():
    return lax.axis_size("blk") * lax.axis_size("inner")


def passed_along(value, steps):
    count = device_count()
    first, last = (max(0, -steps), min(count, count - steps))
    return lax.ppermute(value, AXES, [(source, source + steps) for source in range(first, last)])


def write_masks(bias_ref, old_ref, cut_ref, lengths_ref, first_ref, rows):
    docs = lengths_ref.shape[0]
    first = first_ref[0]
    row = lax.broadcasted_iota(jnp.int32, (rows, 128), 0)
    query_pos = first + row

    def step(doc, carry):
        end, start = carry
        end = end + lengths_ref[doc]
        return end, jnp.where(query_pos >= end, end, start)

    _, start = lax.fori_loop(0, docs, step, (jnp.int32(0), jnp.zeros((rows, 128), jnp.int32)))
    lane = lax.broadcasted_iota(jnp.int32, (rows, 128), 1)
    old = start < first - (SPAN - 2) * rows
    old_ref[...] = jnp.where(old, 1.0, 0.0)
    cut = jnp.min(jnp.where(old, start - (first - (SPAN - 1) * rows), rows), axis=0, keepdims=True)
    cut_ref[...] = jnp.broadcast_to(cut, cut_ref.shape)
    cut = jnp.broadcast_to(cut, (rows, 128))
    for part in range((SPAN - 1) * rows // 128):
        offset = part * 128 + lane
        if part < rows // 128:
            own = (offset <= row) & ((first + offset >= start) | (old & (offset < cut)))
            allowed = own | (old & (offset >= cut))
        else:
            allowed = first - (SPAN - 1) * rows + offset >= start
        bias_ref[:, part * 128 : (part + 1) * 128] = jnp.where(allowed, 0.0, MASKED)


def attention_kernel(where, q_ref, g_ref, behind_ref, near_ref, own_ref, bias_ref, old_ref, cut_ref, *refs):
    out_ref, dq_ref, dbehind_ref, dnear_ref, down_ref = refs[-(OUTS + SCRATCH) : -SCRATCH]
    (
        key_ref, value_ref, key_t_ref, value_t_ref, key2_ref, value2_ref, key2_t_ref, value2_t_ref,
        dk_ref, dv_ref, dk2_ref, dv2_ref, *slots,
    ) = refs[-SCRATCH:]
    slots, copies = slots[:13], slots[13:]
    s_refs, p_refs, dp_refs, d_refs, g_refs, delta_refs = (slots[i : i + 2] for i in range(0, 12, 2))
    (inv_ref,) = slots[12:]
    head, *offsets = where
    key_in, value_in, key_out, value_out = (slice(at, at + HEAD_SIZE) for at in offsets)
    q_full_ref, g_full_ref, out_full_ref, dq_full_ref = q_ref, g_ref, out_ref, dq_ref
    q_ref, g_ref, out_ref, dq_ref, sem = copies
    rows, wide = q_ref.shape
    mine = slice(head * wide, (head + 1) * wide)
    q_copy = pltpu.make_async_copy(q_full_ref.at[:, mine], q_ref, sem.at[0])
    g_copy = pltpu.make_async_copy(g_full_ref.at[:, mine], g_ref, sem.at[1])
    q_copy.start()
    g_copy.start()
    window = (SPAN - 1) * rows
    units = GROUP // UNIT
    stack = UNIT * rows
    two = slice(0, rows)
    rest = slice(rows, window)

    from_far = lax.broadcasted_iota(jnp.int32, (rows, HEAD_SIZE), 0) >= cut_ref[0, 0]
    mid, far, near, own = behind_ref.at[0], behind_ref.at[1], near_ref, own_ref
    for j, block in enumerate((mid, near)):
        span = slice(j * rows, (j + 1) * rows)
        key_ref[span] = block[:, key_in]
        value_ref[span] = block[:, value_in]
        key_t_ref[:, span] = block[:, key_in].T
        value_t_ref[:, span] = block[:, value_in].T
    for which, plain_ref, turned_ref in ((key_in, key2_ref, key2_t_ref), (value_in, value2_ref, value2_t_ref)):
        mine = own[:, which]
        either = jnp.where(from_far, far[:, which].astype(jnp.float32), mine.astype(jnp.float32))
        for j, block in enumerate((either.astype(jnp.bfloat16), mine)):
            span = slice(j * HEAD_SIZE, (j + 1) * HEAD_SIZE)
            plain_ref[:, span] = block
            turned_ref[span] = block.T

    def places(unit):
        return [
            (
                slice(i * rows, (i + 1) * rows),
                slice((unit * UNIT + i) * HEAD_SIZE, (unit * UNIT + i + 1) * HEAD_SIZE),
            )
            for i in range(UNIT)
        ]

    def stacked(ref, unit):
        return jnp.concatenate([ref[:, cols] for _, cols in places(unit)], axis=0)

    def doubled(x):
        old = jnp.concatenate([old_ref[...].astype(jnp.bfloat16)] * UNIT, axis=0)
        return jnp.concatenate([x * old, x * (1 - old)], axis=1)

    def picked(x):
        old = jnp.concatenate([old_ref[...]] * UNIT, axis=0)
        return jnp.where(old > 0.5, x[:, :HEAD_SIZE], x[:, HEAD_SIZE:])

    def scores(unit, slot):
        q = stacked(q_ref, unit)
        s_refs[slot][:, two] = dot(doubled(q), key2_t_ref[...])
        s_refs[slot][:, rest] = dot(q, key_t_ref[...])

    def softmax(slot):
        for r in range(0, stack, ROWS):
            here = slice(r, r + ROWS)
            row = slice(r % rows, r % rows + ROWS)
            s = s_refs[slot][here] * EXP2_SCALE + bias_ref[row]
            e = jnp.exp2(s - jnp.max(s, axis=1, keepdims=True))
            inv = 1.0 / jnp.sum(e, axis=1, keepdims=True)
            inv_ref[here] = jnp.broadcast_to(inv, (ROWS, HEAD_SIZE))
            p_refs[slot][here] = e.astype(jnp.bfloat16)

    def mix(unit, slot):
        p_ref, g_ref_here = p_refs[slot], g_refs[slot]
        total = picked(dot(p_ref[:, two], value2_ref[...])) + dot(p_ref[:, rest], value_ref[...])
        for here, cols in places(unit):
            inv = inv_ref[here]
            out = (total[here] * inv).astype(jnp.bfloat16)
            out_ref[:, cols] = out
            g = g_ref[:, cols].astype(jnp.float32) * inv
            delta = jnp.sum(g * out.astype(jnp.float32), axis=1, keepdims=True)
            delta_refs[slot][here] = jnp.broadcast_to(delta, (rows, HEAD_SIZE))
            g_ref_here[here] = g.astype(jnp.bfloat16)
        g = g_ref_here[...]
        dp_refs[slot][:, two] = dot(doubled(g), value2_t_ref[...])
        dp_refs[slot][:, rest] = dot(g, value_t_ref[...])

    def score_grad(slot):
        for r in range(0, stack, ROWS):
            here = slice(r, r + ROWS)
            delta = jnp.concatenate([delta_refs[slot][here]] * (window // HEAD_SIZE), axis=1)
            d_refs[slot][here] = p_refs[slot][here] * (dp_refs[slot][here] - delta).astype(jnp.bfloat16)

    def spread(unit, slot):
        p_ref, d_ref = p_refs[slot], d_refs[slot]
        total = picked(dot(d_ref[:, two], key2_ref[...])) + dot(d_ref[:, rest], key_ref[...])
        for here, cols in places(unit):
            dq_ref[:, cols] = (total[here] * SCALE).astype(jnp.bfloat16)
        q = stacked(q_ref, unit)
        g = g_refs[slot][...]
        for total_ref, left, right in (
            (dk2_ref, doubled(q), d_ref[:, two]),
            (dk_ref, q, d_ref[:, rest]),
            (dv2_ref, doubled(g), p_ref[:, two]),
            (dv_ref, g, p_ref[:, rest]),
        ):
            term = dot(left.T, right)
            total_ref[...] = term if unit == 0 else total_ref[...] + term

    def send(unit, scratch_ref, full_ref, at):
        part = slice(unit * UNIT * HEAD_SIZE, (unit + 1) * UNIT * HEAD_SIZE)
        place = slice(head * wide + part.start, head * wide + part.stop)
        copy = pltpu.make_async_copy(scratch_ref.at[:, part], full_ref.at[:, place], sem.at[at])
        copy.start()
        return copy

    q_copy.wait()
    scores(0, 0)
    sent = []
    for unit in range(units):
        slot = unit % 2
        if unit + 1 < units:
            scores(unit + 1, 1 - slot)
        if unit > 0:
            score_grad(1 - slot)
        softmax(slot)
        if unit > 0:
            spread(unit - 1, 1 - slot)
            sent.append(send(unit - 1, dq_ref, dq_full_ref, 2 + 2 * (unit - 1)))
        if unit == 0:
            g_copy.wait()
        mix(unit, slot)
        sent.append(send(unit, out_ref, out_full_ref, 3 + 2 * unit))
    score_grad((units - 1) % 2)
    spread(units - 1, (units - 1) % 2)
    sent.append(send(units - 1, dq_ref, dq_full_ref, 2 * units))
    for span, grad, grad2, scale in ((key_out, dk_ref, dk2_ref, SCALE), (value_out, dv_ref, dv2_ref, 1.0)):
        either = grad2[:HEAD_SIZE].T * scale
        own = grad2[HEAD_SIZE:].T * scale
        dbehind_ref[0, :, span] = (grad[:, :rows].T * scale).astype(jnp.bfloat16)
        dbehind_ref[1, :, span] = jnp.where(from_far, either, 0.0).astype(jnp.bfloat16)
        dnear_ref[:, span] = grad[:, rows:].T * scale
        down_ref[:, span] = own + jnp.where(from_far, 0.0, either)
    for copy in sent:
        copy.wait()


def attention(head, queries, out_grad, blocks, place, grads, masks):
    rows = queries.shape[0]
    wide = GROUP * HEAD_SIZE
    pair = 2 * HEAD_SIZE
    window = (SPAN - 1) * rows
    query_spec = pl.BlockSpec(memory_space=pltpu.HBM)

    def whole(shape):
        return pl.BlockSpec(shape, lambda i, *_: (0,) * len(shape))

    fore = blocks[-1].shape[1] // pair
    where = [head, *(at * HEAD_SIZE for at in (place, fore + place, 0, 1))]
    operands = [queries, out_grad, *blocks, *masks]
    in_specs = [query_spec] * 2 + [whole(array.shape) for array in (*blocks, *masks)]
    aliases = {}
    for at, array in enumerate(grads):
        if array is not None:
            aliases[len(operands)] = at
            operands.append(array)
            in_specs.append(query_spec)
    bf16, f32 = jnp.bfloat16, jnp.float32
    results = pl.pallas_call(
        functools.partial(attention_kernel, where),
        out_shape=[
            jax.ShapeDtypeStruct(queries.shape, bf16),
            jax.ShapeDtypeStruct(queries.shape, bf16),
            jax.ShapeDtypeStruct((2, rows, pair), bf16),
            jax.ShapeDtypeStruct((rows, pair), f32),
            jax.ShapeDtypeStruct((rows, pair), f32),
        ],
        grid_spec=pltpu.PrefetchScalarGridSpec(
            num_scalar_prefetch=0,
            grid=(1,),
            in_specs=in_specs,
            out_specs=[query_spec] * 2
            + [whole((2, rows, pair)), whole((rows, pair)), whole((rows, pair))],
            scratch_shapes=[
                pltpu.VMEM(shape, kind)
                for shape, kind, count in (
                    ((2 * rows, HEAD_SIZE), bf16, 2),
                    ((HEAD_SIZE, 2 * rows), bf16, 2),
                    ((rows, pair), bf16, 2),
                    ((pair, rows), bf16, 2),
                    ((HEAD_SIZE, 2 * rows), f32, 2),
                    ((pair, rows), f32, 2),
                    ((UNIT * rows, window), f32, 2),
                    ((UNIT * rows, window), bf16, 2),
                    ((UNIT * rows, window), f32, 2),
                    ((UNIT * rows, window), bf16, 2),
                    ((UNIT * rows, HEAD_SIZE), bf16, 2),
                    ((UNIT * rows, HEAD_SIZE), f32, 2),
                    ((UNIT * rows, HEAD_SIZE), f32, 1),
                )
                for _ in range(count)
            ]
            + [pltpu.VMEM((rows, wide), bf16)] * 4
            + [pltpu.SemaphoreType.DMA((2 + 2 * GROUP // UNIT,))],
        ),
        input_output_aliases=aliases,
        compiler_params=pltpu.CompilerParams(vmem_limit_bytes=51 * 1024 * 1024),
        cost_estimate=pl.CostEstimate(
            flops=12 * rows * GROUP * window * HEAD_SIZE * 2,
            bytes_accessed=4 * rows * wide * 2 + 22 * rows * pair,
            transcendentals=0,
        ),
        name="attention",
    )(*operands)
    return results[:2], results[2:]


def origin(rank, *_):
    return (0,) * rank


def pack_kernel(first_ref, lengths_ref, keys_ref, values_ref, *refs):
    write_masks(*refs[-3:], lengths_ref, first_ref, keys_ref.shape[0])
    for at, heads in enumerate(FORWARD):
        span = slice(heads[0] * HEAD_SIZE, (heads[-1] + 1) * HEAD_SIZE)
        width = span.stop - span.start
        own_ref, pair_ref = refs[2 * at : 2 * at + 2]
        for target_ref in (own_ref, pair_ref.at[0]):
            target_ref[:, :width] = keys_ref[:, span]
            target_ref[:, width:] = values_ref[:, span]


def pack(first, lengths, keys, values):
    rows = keys.shape[0]
    shapes = []
    for heads in FORWARD:
        own = (rows, 2 * HEAD_SIZE * len(heads))
        shapes += [jax.ShapeDtypeStruct(own, keys.dtype), jax.ShapeDtypeStruct((2, *own), keys.dtype)]
    specs = [
        pl.BlockSpec((1,) * (len(packed.shape) - 2) + packed.shape[-2:], functools.partial(origin, len(packed.shape)))
        for packed in shapes
    ]
    masks = [
        jax.ShapeDtypeStruct((rows, (SPAN - 1) * rows), jnp.float32),
        jax.ShapeDtypeStruct((rows, HEAD_SIZE), jnp.float32),
        jax.ShapeDtypeStruct((8, HEAD_SIZE), jnp.int32),
    ]
    two = functools.partial(origin, 2)
    results = pl.pallas_call(
        pack_kernel,
        out_shape=shapes + masks,
        grid_spec=pltpu.PrefetchScalarGridSpec(
            num_scalar_prefetch=2,
            grid=(1,),
            in_specs=[pl.BlockSpec(keys.shape, two)] * 2,
            out_specs=specs + [pl.BlockSpec(mask.shape, two) for mask in masks],
        ),
        compiler_params=pltpu.CompilerParams(vmem_limit_bytes=12 * 1024 * 1024),
        name="pack",
    )(first, lengths, keys, values)
    packed = results[: len(shapes)]
    return packed[0::2], packed[1::2], results[len(shapes) :]


def local(queries, keys, values, out_grad, doc_lengths):
    rows = queries.shape[0]
    index = lax.axis_index(AXES)
    first = (index * rows).astype(jnp.int32).reshape(1)
    bf16, f32 = jnp.bfloat16, jnp.float32
    blocks, nears = {}, []
    owns, pairs, masks = pack(first, doc_lengths, keys, values)
    for own in owns:
        nears.append(passed_along(own, 1))
    pairs = [pair.at[1].set(near) for pair, near in zip(pairs, nears)]
    for heads, own, near, pair in zip(FORWARD, owns, nears, pairs):
        behind = passed_along(pair, 2)
        for place, head in enumerate(heads):
            blocks[head] = ((behind, near, own), place)
    grads = (None, None)
    parts = []

    def attend(head, after=()):
        nonlocal grads
        (behind, near, own), place = blocks[head]
        own, *after = lax.optimization_barrier((own, *after))
        grads, part = attention(head, queries, out_grad, (behind, near, own), place, grads, masks)
        parts.append(list(part))
        return after

    def second_hop(near, own, got):
        got = got.astype(f32)
        return (near + got[1]).astype(bf16), own + got[0]

    attend(0, pairs)
    gots = [passed_along(parts[0][0], -2)]
    attend(1)
    gots.append(passed_along(parts[1][0], -2))
    attend(2)
    gots.append(passed_along(parts[2][0], -2))
    gots[0], gots[1], _ = lax.optimization_barrier((gots[0], gots[1], parts[2][0]))
    nears, owns = zip(second_hop(*parts[0][1:], gots[0]))
    more = second_hop(*parts[1][1:], gots[1])
    (nears, *more) = attend(3, (*nears, *more))
    gots[2], near = lax.optimization_barrier((gots[2], parts[3][1]))
    gots.append(passed_along(parts[3][0], -2))
    parts[3][1] = near
    rest = [second_hop(*part[1:], got) for part, got in zip(parts[2:], gots[2:])]
    nears, owns = zip((nears, *owns), more, *rest)
    last = [passed_along(jnp.concatenate(nears[at : at + 2], axis=1), -1) for at in (0, 2)]
    total = (jnp.concatenate(owns, axis=1) + jnp.concatenate(last, axis=1).astype(f32)).astype(bf16)
    columns = [total[:, at : at + HEAD_SIZE] for at in range(0, total.shape[1], HEAD_SIZE)]
    return (
        grads[0],
        grads[1],
        jnp.concatenate(columns[0::2], axis=1),
        jnp.concatenate(columns[1::2], axis=1),
    )


def solution(mesh):
    spec = P(AXES, None)
    return jax.shard_map(
        local,
        mesh=mesh,
        in_specs=(spec, spec, spec, spec, P()),
        out_specs=(spec, spec, spec, spec),
        check_vma=False,
    )
```
